128 devices in a mesh: dp: 32 (over z, y, core), group: 4 (over x).
Axes of the slice: x: 4, y: 4, z: 4, core: 2. Of those that a mesh axis runs over, the one named last changes fastest.
Arguments:
- tokens: bfloat16 [32768, 1024], P(('dp', 'group')), may hold values from -16 to 16
- cotangent: bfloat16 [32768, 1024], P(('dp', 'group')), may hold values from -6 to 6
- doc_lengths: int32 [32, 4], P('dp'), may hold values from 1 to 896, 1024 in all within a row
- attn_in: float32 [1024, 3072], P(('dp', 'group')), may hold values from -0.1875 to 0.1875
- attn_out: float32 [1024, 1024], P(('dp', 'group')), may hold values from -2 to 2
- ff_in: float32 [1024, 4096], P(('dp', 'group')), may hold values from -0.1875 to 0.1875
- ff_out: float32 [4096, 1024], P(('dp', 'group')), may hold values from -0.09375 to 0.09375
- norm_gains: float32 [1024, 2], P(('dp', 'group')), may hold values from 0.5 to 1.5
- bias_table: float32 [1024, 6], P(('dp', 'group')), may hold values from -3 to 3
- ff_bias: float32 [4096], P(('dp', 'group')), may hold values from -3 to 5
- first_attn_in: float32 [1024, 3072], P(('dp', 'group')), may hold values from -0.0006 to 0.0006
- first_attn_out: float32 [1024, 1024], P(('dp', 'group')), may hold values from -0.0006 to 0.0006
- first_ff_in: float32 [1024, 4096], P(('dp', 'group')), may hold values from -0.0006 to 0.0006
- first_ff_out: float32 [4096, 1024], P(('dp', 'group')), may hold values from -0.0006 to 0.0006
- first_norm_gains: float32 [1024, 2], P(('dp', 'group')), may hold values from -0.0006 to 0.0006
- first_bias_table: float32 [1024, 6], P(('dp', 'group')), may hold values from -0.0006 to 0.0006
- first_ff_bias: float32 [4096], P(('dp', 'group')), may hold values from -0.0006 to 0.0006
- second_attn_in: float32 [1024, 3072], P(('dp', 'group')), may hold values from 1e-10 to 1e-08
- second_attn_out: float32 [1024, 1024], P(('dp', 'group')), may hold values from 1e-10 to 1e-08
- second_ff_in: float32 [1024, 4096], P(('dp', 'group')), may hold values from 1e-10 to 1e-08
- second_ff_out: float32 [4096, 1024], P(('dp', 'group')), may hold values from 1e-10 to 1e-08
- second_norm_gains: float32 [1024, 2], P(('dp', 'group')), may hold values from 1e-10 to 1e-08
- second_bias_table: float32 [1024, 6], P(('dp', 'group')), may hold values from 1e-10 to 1e-08
- second_ff_bias: float32 [4096], P(('dp', 'group')), may hold values from 1e-10 to 1e-08
Outputs:
- block_out: bfloat16 [32768, 1024], P(('dp', 'group'))
- input_grad: float32 [32768, 1024], P(('dp', 'group'))
- grad_attn_in: float32 [1024, 3072], P(('dp', 'group'))
- grad_attn_out: float32 [1024, 1024], P(('dp', 'group'))
- grad_ff_in: float32 [1024, 4096], P(('dp', 'group'))
- grad_ff_out: float32 [4096, 1024], P(('dp', 'group'))
- grad_norm_gains: float32 [1024, 2], P(('dp', 'group'))
- grad_bias_table: float32 [1024, 6], P(('dp', 'group'))
- grad_ff_bias: float32 [4096], P(('dp', 'group'))
- step_attn_in: float32 [1024, 3072], P(('dp', 'group'))
- step_attn_out: float32 [1024, 1024], P(('dp', 'group'))
- step_ff_in: float32 [1024, 4096], P(('dp', 'group'))
- step_ff_out: float32 [4096, 1024], P(('dp', 'group'))
- step_norm_gains: float32 [1024, 2], P(('dp', 'group'))
- step_bias_table: float32 [1024, 6], P(('dp', 'group'))
- step_ff_bias: float32 [4096], P(('dp', 'group'))
The draws below stay inside these ranges and needn't reach their ends.
Inputs may be any that keep to these rules, and one draw needn't show every extreme that they name: `doc_lengths`: each row lists the lengths of the 4 documents packed in order into one sequence; a row sums to 1024 and its longest document has exactly 896 tokens.
All inputs are finite; a program needn't handle non-finite values.
Results may differ from the reference program's by a relative error of at most 0.015.
The reference program's roundings to bfloat16 on the way count: a program that leaves them out, or rounds other values in their place, can miss the bound.
Values may be sent and summed in bfloat16 or wider, within the bound.
No kernel may reach another device: no remote copies, remote signals or barrier semaphores. Data moves between devices by JAX's collectives and lax.ppermute only.
A program may use at most 192 MiB of HBM per device.

```python
import math
import jax
import jax.numpy as jnp
import numpy as np
from jax import lax

D = 1024
HEADS = 16
HEAD_DIM = 64
FF = 4096
WINDOW = 1024
DOCS = 4
TOK_DEV = 256
SEQS = 32
LENGTH = 1024
TOKENS = 32768
DEVICES = 128


def rising_scale(count, low_end, high_end):
    ramp = jnp.arange(count, dtype=jnp.float32) / (count - 1)
    return jnp.exp(jnp.log(low_end) + ramp * (jnp.log(high_end) - jnp.log(low_end)))


def draw_tokens(key, part):
    key = jax.random.fold_in(key, 11)
    base = jnp.clip(jax.random.normal(key, (TOKENS, D), jnp.float32), -6.0, 6.0)
    column = rising_scale(D, 0.7, 2.5)
    return jnp.clip(base * column[None, :], -16.0, 16.0).astype(jnp.bfloat16)


def draw_ff_bias(key, part):
    key = jax.random.fold_in(key, 23)
    ramp = jnp.arange(FF, dtype=jnp.float32) / (FF - 1)
    rough = jnp.clip(jax.random.normal(key, (FF,), jnp.float32), -3.0, 3.0) * 0.3
    trend = -0.5 + 3.0 * ramp
    return jnp.clip(trend + rough, -3.0, 5.0)


def level_of(own_key, extent, split, least, high):
    def one(position, blocks):
        draws = jax.random.uniform(jax.random.fold_in(jax.random.fold_in(own_key, 6), position), (blocks,), jnp.float32, least / len(split), high / len(split))
        return jnp.repeat(jnp.exp(draws), extent[position] // blocks).reshape((-1,) + (1,) * (len(extent) - position - 1))

    loudness = one(*split[0])
    for cut in split[1:]:
        loudness = loudness * one(*cut)
    return loudness


def profile(count, total, bound, slope):
    portions = [(1 << 20) // math.isqrt(rank ** slope) + 1 for rank in range(2, count + 1)]
    spare, holding = total - bound - (count - 1), [1] * (count - 1)
    while spare > 0:
        candidates = [i for i in range(count - 1) if holding[i] < bound]
        mass, left = sum([portions[i] for i in candidates]), spare
        for i in candidates:
            extra = min(bound - holding[i], max(1, left * portions[i] // mass), spare)
            holding[i] = holding[i] + extra
            spare = spare - extra
    return np.array([bound] + holding)


def uneven(rng, amount, total, reach, skew):
    if amount == 2:
        one = jax.random.randint(rng, (), max(1, total - reach), min(reach, total - 1) + 1)
        return jnp.stack([one, total - one])
    tallies = jnp.asarray(profile(amount, total, reach, skew), jnp.int32)
    pairs = (amount - 1) // 2
    donor, taker = tallies[1:1 + 2 * pairs:2], tallies[2:2 + 2 * pairs:2]
    room = jnp.minimum(donor - 1, reach - taker)
    moved = jax.random.randint(jax.random.fold_in(rng, 1), (pairs,), 0, 1 << 20) % (room + 1)
    tallies = tallies.at[1:1 + 2 * pairs:2].set(donor - moved).at[2:2 + 2 * pairs:2].set(taker + moved)
    return tallies[jax.random.permutation(jax.random.fold_in(rng, 2), amount)]


def noise(rng, shape, width, reach, shards=(), kind=jnp.bfloat16):
    values = width * jax.random.normal(rng, shape, jnp.float32)
    if shards:
        values = values * level_of(rng, shape, shards, -0.22, 0.18)
    return jnp.clip(values, -reach, reach).astype(kind)


def setup_inputs(seed: int = 0) -> dict:
    key_list = jax.random.split(jax.random.key(seed), 25)
    tokens = draw_tokens(jax.random.fold_in(key_list[24], 71), 0)
    cotangent = noise(key_list[1], (TOKENS, D), 1.0, 6.0, ((0, 128),))
    doc_lengths = jax.vmap(lambda own: uneven(own, DOCS, LENGTH, LENGTH - TOK_DEV // 2, 0))(jax.random.split(key_list[2], SEQS)).reshape((SEQS, DOCS)).astype(jnp.int32)
    attn_in = noise(key_list[3], (D, 3 * D), D ** -0.5, 0.1875, ((0, 128),), jnp.float32)
    attn_out = noise(key_list[4], (D, D), (D // 128) ** -0.5, 2.0, ((0, 128),), jnp.float32)
    ff_in = noise(key_list[5], (D, FF), D ** -0.5, 0.1875, ((0, 128),), jnp.float32)
    ff_out = noise(key_list[6], (FF, D), FF ** -0.5, 0.09375, ((0, 128),), jnp.float32)
    norm_gains = jnp.clip(1.0 + 0.1 * jax.random.normal(key_list[7], (D, 2), jnp.float32), 0.5, 1.5)
    bias_table = noise(key_list[8], (D, 6), 0.5, 3.0, ((0, 128),), jnp.float32)
    ff_bias = draw_ff_bias(jax.random.fold_in(key_list[24], 71), 0)
    first_attn_in = noise(key_list[10], (D, 3 * D), 0.0001, 0.0006, ((0, 128),), jnp.float32)
    first_attn_out = noise(key_list[11], (D, D), 0.0001, 0.0006, ((0, 128),), jnp.float32)
    first_ff_in = noise(key_list[12], (D, FF), 0.0001, 0.0006, ((0, 128),), jnp.float32)
    first_ff_out = noise(key_list[13], (FF, D), 0.0001, 0.0006, ((0, 128),), jnp.float32)
    first_norm_gains = noise(key_list[14], (D, 2), 0.0001, 0.0006, ((0, 128),), jnp.float32)
    first_bias_table = noise(key_list[15], (D, 6), 0.0001, 0.0006, ((0, 128),), jnp.float32)
    first_ff_bias = noise(key_list[16], (FF,), 0.0001, 0.0006, ((0, 128),), jnp.float32)
    second_attn_in = jnp.clip(jnp.exp(math.log(9.99999993922529e-09) - 4.6051702 * jax.random.uniform(key_list[17], (D, 3 * D), jnp.float32) ** level_of(key_list[17], (D, 3 * D), ((0, 128),), -0.2, 0.2)), 1.000000013351432e-10, 9.99999993922529e-09)
    second_attn_out = jnp.clip(jnp.exp(math.log(9.99999993922529e-09) - 4.6051702 * jax.random.uniform(key_list[18], (D, D), jnp.float32) ** level_of(key_list[18], (D, D), ((0, 128),), -0.2, 0.2)), 1.000000013351432e-10, 9.99999993922529e-09)
    second_ff_in = jnp.clip(jnp.exp(math.log(9.99999993922529e-09) - 4.6051702 * jax.random.uniform(key_list[19], (D, FF), jnp.float32) ** level_of(key_list[19], (D, FF), ((0, 128),), -0.2, 0.2)), 1.000000013351432e-10, 9.99999993922529e-09)
    second_ff_out = jnp.clip(jnp.exp(math.log(9.99999993922529e-09) - 4.6051702 * jax.random.uniform(key_list[20], (FF, D), jnp.float32) ** level_of(key_list[20], (FF, D), ((0, 128),), -0.2, 0.2)), 1.000000013351432e-10, 9.99999993922529e-09)
    second_norm_gains = jnp.clip(jnp.exp(math.log(9.99999993922529e-09) - 4.6051702 * jax.random.uniform(key_list[21], (D, 2), jnp.float32) ** level_of(key_list[21], (D, 2), ((0, 128),), -0.2, 0.2)), 1.000000013351432e-10, 9.99999993922529e-09)
    second_bias_table = jnp.clip(jnp.exp(math.log(9.99999993922529e-09) - 4.6051702 * jax.random.uniform(key_list[22], (D, 6), jnp.float32) ** level_of(key_list[22], (D, 6), ((0, 128),), -0.2, 0.2)), 1.000000013351432e-10, 9.99999993922529e-09)
    second_ff_bias = jnp.clip(jnp.exp(math.log(9.99999993922529e-09) - 4.6051702 * jax.random.uniform(key_list[23], (FF,), jnp.float32) ** level_of(key_list[23], (FF,), ((0, 128),), -0.2, 0.2)), 1.000000013351432e-10, 9.99999993922529e-09)
    return dict(tokens=tokens, cotangent=cotangent, doc_lengths=doc_lengths, attn_in=attn_in, attn_out=attn_out, ff_in=ff_in, ff_out=ff_out, norm_gains=norm_gains, bias_table=bias_table, ff_bias=ff_bias, first_attn_in=first_attn_in, first_attn_out=first_attn_out, first_ff_in=first_ff_in, first_ff_out=first_ff_out, first_norm_gains=first_norm_gains, first_bias_table=first_bias_table, first_ff_bias=first_ff_bias, second_attn_in=second_attn_in, second_attn_out=second_attn_out, second_ff_in=second_ff_in, second_ff_out=second_ff_out, second_norm_gains=second_norm_gains, second_bias_table=second_bias_table, second_ff_bias=second_ff_bias)


@jax.custom_vjp
def low(v):
    return lax.optimization_barrier(v.astype(jnp.bfloat16)).astype(jnp.float32)

@jax.custom_vjp
def low_back(v):
    return v

def low_keep(v):
    return (low(v), None)

def low_pass(kept, grad):
    return (grad,)

def back_keep(v):
    return (v, None)

def back_low(kept, grad):
    return (low(grad),)
low.defvjp(low_keep, low_pass)
low_back.defvjp(back_keep, back_low)
NORM_EPS = 1e-06
CLIP_NORM = 1.0
BETA_ONE = 0.9
BETA_TWO = 0.999
STEP_COUNT = 10
ADAM_EPS = 1e-06
WEIGHT_DECAY = 0.01
MASKED_SCORE = -1e+30
HIGHEST_PREC = lax.Precision.HIGHEST

def matmul(left, right):
    return jnp.dot(left, right, precision=HIGHEST_PREC, preferred_element_type=jnp.float32)

def layer_norm(values_in, gain_vec, shift_vec):
    center = values_in - lax.optimization_barrier(jnp.mean(values_in, axis=-1, keepdims=True))
    spread = lax.optimization_barrier(jnp.mean(center * center, axis=-1, keepdims=True))
    return center * lax.rsqrt(spread + NORM_EPS) * gain_vec + shift_vec

def doc_ids(lengths, positions):
    doc_ends = jnp.cumsum(lengths).astype(jnp.int32)
    return lax.optimization_barrier(jnp.sum((positions[:, None] >= doc_ends[None, :-1]).astype(jnp.int32), axis=1)).astype(jnp.int32)

def forward(inputs, attn_in, attn_out, ff_in, ff_out, norm_gains, bias_table, ff_bias, visible):
    w_in = low(attn_in)
    w_out = low(attn_out)
    w_up = low(ff_in)
    w_down = low(ff_out)
    gain_low = low(norm_gains)
    bias_low = low(bias_table)
    ffb_low = low(ff_bias)
    seq_len = inputs.shape[0]
    model_width = inputs.shape[1]
    zero_col = jnp.zeros((model_width,), jnp.float32)
    in_bias = jnp.concatenate([bias_low[:, 0], zero_col, bias_low[:, 1]])
    qkv = low_back(low(matmul(inputs, w_in) + in_bias))
    query = qkv[:, :model_width].reshape(seq_len, HEADS, HEAD_DIM)
    keys = qkv[:, model_width:2 * model_width].reshape(seq_len, HEADS, HEAD_DIM)
    values = qkv[:, 2 * model_width:].reshape(seq_len, HEADS, HEAD_DIM)
    scores = jnp.einsum('thd,shd->hts', query, keys, precision=HIGHEST_PREC) * HEAD_DIM ** (-0.5)
    scores = low_back(scores)
    scores = jnp.where(visible[None], scores, MASKED_SCORE)
    row_top = lax.optimization_barrier(jnp.max(scores, axis=-1, keepdims=True))
    row_total = jnp.log(lax.optimization_barrier(jnp.sum(jnp.exp(scores - row_top), axis=-1, keepdims=True))) + row_top
    attn_probs = low(jnp.exp(scores - row_total))
    context = jnp.einsum('hts,shd->thd', attn_probs, values, precision=HIGHEST_PREC).reshape(seq_len, model_width)
    context = low_back(low(context))
    attended = low_back(matmul(context, w_out) + bias_low[:, 2])
    first = layer_norm(inputs + attended, gain_low[:, 0], bias_low[:, 3])
    hidden = low_back(matmul(low(first), w_up) + ffb_low)
    active = low(jax.nn.gelu(hidden, approximate=True))
    branch = low_back(matmul(active, w_down) + bias_low[:, 4])
    return layer_norm(first + branch, gain_low[:, 1], bias_low[:, 5])

def lamb_step(weight, grad, first_mom, second_mom):
    new_first = BETA_ONE * first_mom + (1.0 - BETA_ONE) * grad
    new_second = BETA_TWO * second_mom + (1.0 - BETA_TWO) * grad * grad
    direction = new_first / (1.0 - BETA_ONE ** STEP_COUNT) / (jnp.sqrt(new_second / (1.0 - BETA_TWO ** STEP_COUNT)) + ADAM_EPS) + WEIGHT_DECAY * weight
    flat_weight = weight.reshape(DEVICES, -1)
    flat_dir = direction.reshape(DEVICES, -1)
    weight_norm = jnp.sqrt(lax.optimization_barrier(jnp.sum(flat_weight * flat_weight, axis=1, keepdims=True)))
    dir_norm = jnp.sqrt(lax.optimization_barrier(jnp.sum(flat_dir * flat_dir, axis=1, keepdims=True)))
    return (flat_dir * (weight_norm / jnp.maximum(dir_norm, 1.0))).reshape(weight.shape)

def reference(tokens, cotangent, doc_lengths, attn_in, attn_out, ff_in, ff_out, norm_gains, bias_table, ff_bias, first_attn_in, first_attn_out, first_ff_in, first_ff_out, first_norm_gains, first_bias_table, first_ff_bias, second_attn_in, second_attn_out, second_ff_in, second_ff_out, second_norm_gains, second_bias_table, second_ff_bias):
    params = (attn_in, attn_out, ff_in, ff_out, norm_gains, bias_table, ff_bias)
    firsts = (first_attn_in, first_attn_out, first_ff_in, first_ff_out, first_norm_gains, first_bias_table, first_ff_bias)
    seconds = (second_attn_in, second_attn_out, second_ff_in, second_ff_out, second_norm_gains, second_bias_table, second_ff_bias)
    inputs = tokens.astype(jnp.float32).reshape(SEQS, LENGTH, D)
    cotan = cotangent.astype(jnp.float32).reshape(SEQS, LENGTH, D)
    positions = jnp.arange(LENGTH, dtype=jnp.int32)
    nearby = jnp.abs(positions[:, None] - positions[None, :]) < WINDOW // 2

    def one_sequence(totals, item):
        seq_in, seq_cot, lengths = item
        seq_ids = doc_ids(lengths, positions)
        visible = (seq_ids[:, None] == seq_ids[None, :]) & nearby

        def run(seq_values, *weights):
            return forward(seq_values, *weights, visible)
        result, pullback = jax.vjp(run, seq_in, *params)
        grads_back = pullback(seq_cot)
        totals = tuple((acc + part for acc, part in zip(totals, grads_back[1:])))
        return (totals, (result.astype(jnp.bfloat16), grads_back[0]))
    zeros = tuple((jnp.zeros(weight.shape, jnp.float32) for weight in params))
    grads, (outputs, input_grads) = lax.scan(one_sequence, zeros, (inputs, cotan, doc_lengths))
    squares = sum((jnp.sum(grad * grad) for grad in grads))
    factor = CLIP_NORM / jnp.maximum(jnp.sqrt(squares), CLIP_NORM)
    steps = tuple((lamb_step(weight, grad * factor, first_mom, second_mom) for weight, grad, first_mom, second_mom in zip(params, grads, firsts, seconds)))
    return (outputs.reshape(TOKENS, D), input_grads.reshape(TOKENS, D), grads[0], grads[1], grads[2], grads[3], grads[4], grads[5], grads[6], steps[0], steps[1], steps[2], steps[3], steps[4], steps[5], steps[6])
```

```python
import jax
import jax.numpy as jnp
from jax import lax
from jax.experimental import pallas as pl
from jax.experimental.pallas import tpu as pltpu
from jax.sharding import PartitionSpec as P

HEADS = 16
WINDOW = 1024
AXES = ("dp", "group")
RADIX = {"z": 4, "y": 4, "core": 2, "x": 4}

NORM_EPS = 1e-06
CLIP_NORM = 1.0
BETA_ONE = 0.9
BETA_TWO = 0.999
STEP_COUNT = 10
ADAM_EPS = 1e-06
WEIGHT_DECAY = 0.01
MASKED_SCORE = -1e30
F32 = jnp.float32
BF16 = jnp.bfloat16


def pair_list(axis, shift):
    out = []
    for flat in range(128):
        at = {"z": flat // 32, "y": flat // 8 % 4, "core": flat // 4 % 2, "x": flat % 4}
        at[axis] = (at[axis] + shift) % RADIX[axis]
        out.append((flat, ((at["z"] * 4 + at["y"]) * 2 + at["core"]) * 4 + at["x"]))
    return out


def push(value, axis, shift):
    return lax.ppermute(value, AXES, pair_list(axis, shift))


def pick(value, index, dim):
    return lax.dynamic_index_in_dim(value, index, dim, keepdims=False)


def rolled(parts, me, dim):
    joined = jnp.concatenate(parts + parts[:3], axis=dim)
    width = parts[0].shape[dim]
    return lax.dynamic_slice_in_dim(joined, (4 - me) % 4 * width, 4 * width, dim)


def gather_small(value, axis, me, dim):
    value = jnp.expand_dims(value, dim)
    return rolled([value] + [push(value, axis, -j) for j in (1, 2, 3)], me, dim)


def gather_last(value, axis, me, core, buffer, dim, half):
    def put(buf, piece, place, start=0):
        other = push(piece, "core", 1)
        for data, side in ((piece, core), (other, 1 - core)):
            data = jnp.expand_dims(jnp.expand_dims(data, 1), dim if dim != 1 else 1)
            at = [0] * 6
            at[2] = side
            at[dim] = place
            at[half] = start
            buf = lax.dynamic_update_slice(buf, data, tuple(at))
        return buf

    near_up = push(value, axis, -1)
    near_down = push(value, axis, 1)
    buffer = put(buffer, value, me)
    cut = value.shape[0] // 2
    far_one = push(near_up[:cut], axis, -1)
    far_two = push(near_down[cut:], axis, 1)
    buffer = put(buffer, near_up, (me + 1) % 4)
    buffer = put(buffer, near_down, (me + 3) % 4)
    buffer = put(buffer, far_one, (me + 2) % 4)
    return put(buffer, far_two, (me + 2) % 4, cut)


def core_sum(partial, core):
    other = push(pick(partial, 1 - core, 2), "core", 1)
    return (pick(partial, core, 2).astype(F32) + other.astype(F32)).astype(BF16)


def scatter_direct(value, axis, me, dim, dtype):
    total = pick(value, me, dim).astype(F32)
    for k in (1, 3, 2):
        total = total + push(pick(value, (me + k) % 4, dim), axis, k).astype(F32)
    return total.astype(dtype)


def scatter_two(value, axis, me, dim, dtype):
    far = pick(value, (me + 2) % 4, dim)
    cut = far.shape[0] // 2
    from_down = push(far[:cut], axis, 1)
    from_up = push(far[cut:], axis, -1)
    up = pick(value, (me + 1) % 4, dim)
    down = pick(value, (me + 3) % 4, dim)
    up = jnp.concatenate([(up[:cut].astype(F32) + from_down.astype(F32)).astype(BF16), up[cut:]], axis=0)
    down = jnp.concatenate([down[:cut], (down[cut:].astype(F32) + from_up.astype(F32)).astype(BF16)], axis=0)
    got_one = push(up, axis, 1)
    got_two = push(down, axis, -1)
    return (pick(value, me, dim).astype(F32) + got_one.astype(F32) + got_two.astype(F32)).astype(dtype)


def sum_all(value, axes):
    for axis in axes:
        total = value
        for k in range(1, RADIX[axis]):
            total = total + push(value, axis, k)
        value = total
    return value


def scores_of(query, key, code_col, code_row):
    raw = lax.dot_general(query, key, (((1,), (1,)), ((), ())), preferred_element_type=F32)
    return jnp.where(jnp.abs(code_col - code_row) < WINDOW // 2, raw, MASKED_SCORE)


def attend_kernel(q_ref, k_ref, v_ref, col_ref, row_ref, out_ref, lse_ref):
    code_row = row_ref[...]
    for head in range(2):
        lanes = slice(head * 64, head * 64 + 64)
        key = k_ref[:, lanes]
        value = v_ref[:, lanes]
        for block in range(4):
            rows = slice(block * 256, block * 256 + 256)
            query = q_ref[rows, lanes] * BF16(0.125)
            scores = scores_of(query, key, col_ref[rows, :], code_row)
            top = jnp.max(scores, axis=1, keepdims=True)
            raised = jnp.exp(scores - top)
            total = jnp.sum(raised, axis=1, keepdims=True)
            probs = (raised * (1.0 / total)).astype(BF16)
            out_ref[rows, lanes] = jnp.dot(probs, value, preferred_element_type=F32).astype(BF16)
            lse_ref[rows, lanes] = jnp.broadcast_to(jnp.log(total) + top, (256, 64))


def attend_back_kernel(q_ref, k_ref, v_ref, d_ref, col_ref, row_ref, lse_ref, dq_ref, dk_ref, dv_ref, sk_ref, sv_ref):
    code_row = row_ref[...]
    turn = (((0,), (0,)), ((), ()))
    for head in range(2):
        lanes = slice(head * 64, head * 64 + 64)
        key = k_ref[:, lanes]
        value = v_ref[:, lanes]
        sk_ref[...] = jnp.zeros_like(sk_ref)
        sv_ref[...] = jnp.zeros_like(sv_ref)
        for block in range(4):
            rows = slice(block * 256, block * 256 + 256)
            query = q_ref[rows, lanes] * BF16(0.125)
            d_out = d_ref[rows, lanes]
            scores = scores_of(query, key, col_ref[rows, :], code_row)
            probs = jnp.exp(scores - lse_ref[rows, head * 64 : head * 64 + 1])
            d_probs = lax.dot_general(d_out, value, (((1,), (1,)), ((), ())), preferred_element_type=F32)
            delta = jnp.sum(probs * d_probs, axis=1, keepdims=True)
            d_scores = (probs * (d_probs - delta)).astype(BF16)
            dq_ref[rows, lanes] = (jnp.dot(d_scores, key, preferred_element_type=F32) * 0.125).astype(BF16)
            sk_ref[...] += lax.dot_general(d_scores, query, turn, preferred_element_type=F32)
            sv_ref[...] += lax.dot_general(probs.astype(BF16), d_out, turn, preferred_element_type=F32)
        dk_ref[:, lanes] = sk_ref[...].astype(BF16)
        dv_ref[:, lanes] = sv_ref[...].astype(BF16)


def two_heads(first):
    return pl.BlockSpec((1024, 128), lambda i: (0, first + i))


def whole(shape):
    return pl.BlockSpec(shape, lambda i: (0, 0))


def attend(qkv, code_col, code_row):
    return pl.pallas_call(
        attend_kernel,
        grid=(2,),
        in_specs=[two_heads(0), two_heads(2), two_heads(4), whole((1024, 1)), whole((1, 1024))],
        out_specs=[two_heads(0), two_heads(0)],
        out_shape=[jax.ShapeDtypeStruct((1024, 256), BF16), jax.ShapeDtypeStruct((1024, 256), F32)],
        compiler_params=pltpu.CompilerParams(vmem_limit_bytes=40 * 2**20),
        cost_estimate=pl.CostEstimate(flops=2 * 2 * 4 * 1024 * 1024 * 64 * 4, bytes_accessed=4 * 2**20, transcendentals=4 * 2**20),
        name="attend",
    )(qkv, qkv, qkv, code_col, code_row)


def attend_back(qkv, d_out, code_col, code_row, lse):
    return pl.pallas_call(
        attend_back_kernel,
        grid=(2,),
        in_specs=[two_heads(0), two_heads(2), two_heads(4), two_heads(0), whole((1024, 1)), whole((1, 1024)), two_heads(0)],
        out_specs=[two_heads(0)] * 3,
        out_shape=[jax.ShapeDtypeStruct((1024, 256), BF16)] * 3,
        scratch_shapes=[pltpu.VMEM((1024, 64), F32), pltpu.VMEM((1024, 64), F32)],
        compiler_params=pltpu.CompilerParams(vmem_limit_bytes=40 * 2**20),
        cost_estimate=pl.CostEstimate(flops=5 * 2 * 4 * 1024 * 1024 * 64 * 4, bytes_accessed=6 * 2**20, transcendentals=4 * 2**20),
        name="attend_back",
    )(qkv, qkv, qkv, d_out, code_col, code_row, lse)


def layer_norm(values_in, gain_vec, shift_vec):
    center = values_in - jnp.mean(values_in, axis=-1, keepdims=True)
    spread = jnp.mean(center * center, axis=-1, keepdims=True)
    return center * lax.rsqrt(spread + NORM_EPS) * gain_vec + shift_vec


def gelu_tanh(values_in):
    return jax.nn.gelu(values_in, approximate=True)


def lamb_step(weight, grad, first_mom, second_mom):
    new_first = BETA_ONE * first_mom + (1.0 - BETA_ONE) * grad
    new_second = BETA_TWO * second_mom + (1.0 - BETA_TWO) * grad * grad
    direction = (
        new_first
        / (1.0 - BETA_ONE**STEP_COUNT)
        / (jnp.sqrt(new_second / (1.0 - BETA_TWO**STEP_COUNT)) + ADAM_EPS)
        + WEIGHT_DECAY * weight
    )
    weight_norm = jnp.sqrt(jnp.sum(weight * weight))
    dir_norm = jnp.sqrt(jnp.sum(direction * direction))
    return direction * (weight_norm / jnp.maximum(dir_norm, 1.0))


def body(tokens, cotangent, doc_lengths, *params):
    shards, firsts, seconds = params[:7], params[7:14], params[14:]
    lowered = tuple(weight.astype(BF16) for weight in shards)
    dp_index = lax.axis_index("dp")
    z_at, y_at, core, x_at = dp_index // 8, dp_index // 2 % 4, dp_index % 2, lax.axis_index("group")

    with jax.named_scope("gather_tokens"):
        tok_all = jnp.concatenate([tokens] + [push(tokens, "x", -j) for j in (1, 2, 3)], axis=0)

    with jax.named_scope("gather_attn_in"):
        small = jnp.concatenate(
            [lowered[4], lowered[5], lowered[6].reshape(4, 8).T, jnp.zeros((8, 116), BF16)], axis=1
        )
        cols = lowered[0].reshape(8, 3, 4, 256)

        def slice_for(group):
            return jnp.concatenate([pick(cols, group, 2).reshape(8, 768), small], axis=1)

        parts = [slice_for(x_at)[None]] + [
            push(slice_for((x_at + 4 - j) % 4)[None], "x", -j) for j in (1, 2, 3)
        ]
        part = rolled(parts, x_at, 0)
        part = gather_small(part, "y", y_at, 0)
        part = gather_small(part, "z", z_at, 0)
        other = push(part, "core", 1)
        pair = jnp.stack([jnp.where(core == 0, part, other), jnp.where(core == 0, other, part)], axis=2)
        packed = pair.reshape(1024, 896)
        w_in = packed[:, :768]
        vectors = packed[:, 768:780].astype(F32).T
        gains, biases = vectors[:2], vectors[2:8]
        ffb = vectors[8:12].reshape(4, 128, 8).transpose(1, 0, 2).reshape(4096)

    with jax.named_scope("gather_ff_in"):
        part = gather_small(gather_small(lowered[2], "x", x_at, 0), "z", z_at, 0)
        w_up = gather_last(part, "y", y_at, core, jnp.zeros((4, 4, 2, 4, 8, 4096), BF16), 1, 0).reshape(1024, 4096)
    with jax.named_scope("gather_ff_out"):
        part = gather_small(gather_small(lowered[3], "x", x_at, 0), "y", y_at, 0)
        w_down = gather_last(part, "z", z_at, core, jnp.zeros((4, 4, 2, 4, 32, 1024), BF16), 0, 1).reshape(4096, 1024)
    with jax.named_scope("gather_attn_out"):
        part = gather_small(gather_small(lowered[1], "x", x_at, 0), "z", z_at, 0)
        w_out = gather_last(part, "y", y_at, core, jnp.zeros((4, 4, 2, 4, 8, 1024), BF16), 1, 0).reshape(1024, 1024)

    with jax.named_scope("attention"):
        order = (x_at + jnp.arange(4, dtype=jnp.int32)) % 4
        positions = (order[:, None] * 256 + jnp.arange(256, dtype=jnp.int32)[None]).reshape(1024)
        doc_ends = jnp.cumsum(doc_lengths[0])
        ids = jnp.sum((positions[:, None] >= doc_ends[None, :-1]).astype(jnp.int32), axis=1)
        code = (positions + 4096 * ids).astype(F32)
        code_col, code_row = code[:, None], code[None]
        own_cols = x_at * 256
        in_bias = jnp.concatenate(
            [
                lax.dynamic_slice_in_dim(biases[0], own_cols, 256),
                jnp.zeros((256,), F32),
                lax.dynamic_slice_in_dim(biases[1], own_cols, 256),
            ]
        )
        qkv = (jnp.dot(tok_all, w_in, preferred_element_type=F32) + in_bias).astype(BF16)
        out_all, lse = attend(qkv, code_col, code_row)
        blocks = out_all.reshape(4, 256, 256)
        context = rolled([blocks[0]] + [push(blocks[4 - j], "x", -j) for j in (1, 2, 3)], x_at, 1)

    with jax.named_scope("feed_forward"):
        attended = jnp.dot(context, w_out, preferred_element_type=F32) + biases[2]
        first, norm_one_pull = jax.vjp(layer_norm, tokens.astype(F32) + attended, gains[0], biases[3])
        first_low = first.astype(BF16)
        hidden = jnp.dot(first_low, w_up, preferred_element_type=F32) + ffb
        active, gelu_pull = jax.vjp(gelu_tanh, hidden)
        active_low = active.astype(BF16)
        branch = jnp.dot(active_low, w_down, preferred_element_type=F32) + biases[4]
        output, norm_two_pull = jax.vjp(layer_norm, first + branch, gains[1], biases[5])
        block_out = output.astype(BF16)

    with jax.named_scope("feed_forward_back"):
        d_two, d_gain_two, d_shift_two = norm_two_pull(cotangent.astype(F32))
        d_branch = d_two.astype(BF16)
        grad_down = jnp.einsum("tf,td->fd", active_low, d_branch, preferred_element_type=F32).astype(BF16)
        d_active = jnp.einsum("td,fd->tf", d_branch, w_down, preferred_element_type=F32)
        (d_hidden,) = gelu_pull(d_active)
        d_hidden_low = d_hidden.astype(BF16)
        grad_up = jnp.einsum("td,tf->df", first_low, d_hidden_low, preferred_element_type=F32).astype(BF16)
        d_first = d_two + jnp.einsum("tf,df->td", d_hidden_low, w_up, preferred_element_type=F32)
        d_one, d_gain_one, d_shift_one = norm_one_pull(d_first)
        d_attended = d_one.astype(BF16)
        grad_out = jnp.einsum("td,te->de", context, d_attended, preferred_element_type=F32).astype(BF16)
        d_context = jnp.einsum("te,de->td", d_attended, w_out, preferred_element_type=F32).astype(BF16)

    with jax.named_scope("scatter_ff_out"):
        value = core_sum(grad_down.reshape(4, 4, 2, 4, 32, 1024), core)
        value = scatter_two(value, "z", z_at, 0, BF16)
        value = scatter_direct(value, "y", y_at, 0, BF16)
        g_down = scatter_direct(value, "x", x_at, 0, F32)
    with jax.named_scope("scatter_ff_in"):
        value = core_sum(grad_up.reshape(4, 4, 2, 4, 8, 4096), core)
        value = scatter_two(value, "y", y_at, 1, BF16)
        value = scatter_direct(value, "z", z_at, 0, BF16)
        g_up = scatter_direct(value, "x", x_at, 0, F32)
    with jax.named_scope("scatter_attn_out"):
        value = core_sum(grad_out.reshape(4, 4, 2, 4, 8, 1024), core)
        value = scatter_direct(value, "x", x_at, 2, BF16)
        value = scatter_direct(value, "y", y_at, 1, BF16)
        g_out = scatter_direct(value, "z", z_at, 0, F32)

    with jax.named_scope("attention_back"):
        d_blocks = d_context.reshape(256, 4, 256)
        d_all = jnp.concatenate(
            [pick(d_blocks, x_at, 1)] + [push(pick(d_blocks, (x_at + 4 - j) % 4, 1), "x", -j) for j in (1, 2, 3)], axis=0
        )
        d_q, d_k, d_v = attend_back(qkv, d_all, code_col, code_row, lse)
        d_qkv = jnp.concatenate([d_q, d_k, d_v], axis=1)
        grad_in = jnp.einsum("td,te->de", tok_all, d_qkv, preferred_element_type=F32).astype(BF16)
        back = jnp.einsum("te,de->td", d_qkv, w_in, preferred_element_type=F32)

    with jax.named_scope("scatter_attn_in"):
        value = core_sum(grad_in.reshape(4, 4, 2, 4, 8, 768), core)
        value = scatter_direct(value, "y", y_at, 1, BF16)
        value = scatter_direct(value, "z", z_at, 0, F32)
        parts = [pick(value, x_at, 0)] + [push(pick(value, (x_at + 4 - j) % 4, 0), "x", -j) for j in (1, 2, 3)]
        g_in = rolled([p.reshape(8, 3, 1, 256) for p in parts], x_at, 2).reshape(8, 3072)

    with jax.named_scope("input_grad"):
        back_low = back.astype(BF16).reshape(4, 256, 1024)
        input_grad = d_one + back[:256]
        for j in (1, 3, 2):
            input_grad = input_grad + push(back_low[j], "x", j).astype(F32)

    with jax.named_scope("small_grads"):

        def at_heads(vec):
            return lax.dynamic_update_slice(jnp.zeros((1024,), F32), vec, (own_cols,))

        rows = jnp.stack(
            [
                d_gain_one,
                d_gain_two,
                at_heads(jnp.sum(d_q.astype(F32), axis=0)),
                at_heads(jnp.sum(d_v.astype(F32), axis=0)),
                jnp.sum(d_attended.astype(F32), axis=0),
                d_shift_one,
                jnp.sum(d_branch.astype(F32), axis=0),
                d_shift_two,
            ]
        )
        rows = jnp.concatenate([rows, jnp.sum(d_hidden_low.astype(F32), axis=0).reshape(4, 1024)], axis=0)
        rows = sum_all(rows, ("core", "y", "z", "x"))
        own = dp_index * 4 + x_at
        mine = lax.dynamic_slice(rows[:8], (0, own * 8), (8, 8)).T
        g_gains, g_biases = mine[:, :2], mine[:, 2:]
        g_ffb = lax.dynamic_slice(rows[8:], (own // 32, own % 32 * 32), (1, 32)).reshape(32)

    grads = (g_in, g_out, g_up.reshape(8, 4096), g_down.reshape(32, 1024), g_gains, g_biases, g_ffb)
    with jax.named_scope("norm"):
        squares = sum(jnp.sum(grad * grad) for grad in grads)
        squares = sum_all(squares.reshape(1, 1), ("core", "y", "z", "x"))[0, 0]
        factor = CLIP_NORM / jnp.maximum(jnp.sqrt(squares), CLIP_NORM)
    with jax.named_scope("lamb"):
        steps = tuple(
            lamb_step(weight, grad * factor, first_mom, second_mom)
            for weight, grad, first_mom, second_mom in zip(shards, grads, firsts, seconds)
        )
    return (block_out, input_grad, *grads, *steps)


def solution(mesh):
    rows, vector, docs = P(AXES, None), P(AXES), P("dp", None)
    leaves = (rows,) * 6 + (vector,)
    return jax.shard_map(
        body,
        mesh=mesh,
        in_specs=(rows, rows, docs) + leaves * 3,
        out_specs=(rows, rows) + leaves * 2,
        check_vma=False,
    )
```

```python
import jax
import jax.numpy as jnp
from jax import lax
from jax.experimental import pallas as pl
from jax.experimental.pallas import tpu as pltpu
from jax.sharding import PartitionSpec as P

HEADS = 16
WINDOW = 1024
AXES = ("dp", "group")
RADIX = {"z": 4, "y": 4, "core": 2, "x": 4}

NORM_EPS = 1e-06
CLIP_NORM = 1.0
BETA_ONE = 0.9
BETA_TWO = 0.999
STEP_COUNT = 10
ADAM_EPS = 1e-06
WEIGHT_DECAY = 0.01
MASKED_SCORE = -1e30
F32 = jnp.float32
BF16 = jnp.bfloat16


def flat_of(at):
    return ((at["z"] * 4 + at["y"]) * 2 + at["core"]) * 4 + at["x"]


def device_pairs(move):
    out = []
    for flat in range(128):
        at = {"z": flat // 32, "y": flat // 8 % 4, "core": flat // 4 % 2, "x": flat % 4}
        move(at)
        out.append((flat, flat_of(at)))
    return out


def push(value, axis, shift):
    def move(at):
        at[axis] = (at[axis] + shift) % RADIX[axis]

    return lax.ppermute(value, AXES, device_pairs(move))


def swap(value, axis, step):
    def move(at):
        at[axis] ^= (1, 3)[(at["core"] + step) % 2]

    return lax.ppermute(value, AXES, device_pairs(move))


def spread(value):
    groups = [
        [flat_of({"z": z, "y": y, "core": core, "x": x}) for z in range(4) for y in range(4) for x in range(4)]
        for core in range(2)
    ]
    return lax.all_to_all(value, AXES, 0, 0, axis_index_groups=groups, tiled=True)


def pick(value, index, dim):
    return lax.dynamic_index_in_dim(value, index, dim, keepdims=False)


def rolled(parts, me, dim):
    joined = jnp.concatenate(parts + parts[:3], axis=dim)
    width = parts[0].shape[dim]
    return lax.dynamic_slice_in_dim(joined, (4 - me) % 4 * width, 4 * width, dim)


def doubled(value, axis, step):
    return jnp.concatenate([value, swap(value, axis, step)], axis=0)


def pieces_of(value, received, last):
    near = jnp.concatenate([value, received], axis=0)
    near_other = push(near, "core", 1)
    far = swap(near, last, 1)
    return near, far, near_other


def outgoing(terms):
    half = terms[0].shape[0] // 2
    return sum(term[half:].astype(F32) for term in terms).astype(BF16)


def step_down(terms, sent, axis, step):
    half = terms[0].shape[0] // 2
    return [term[:half] for term in terms] + [swap(sent, axis, step)]


def masks(core, owner_is_other):
    one = core * 2 + 1
    two = 3 - core * 2
    return (two, one) if owner_is_other else (one, two)


def dot_nn(a, b):
    return jnp.dot(a, b, preferred_element_type=F32)


def dot_nt(a, b):
    return lax.dot_general(a, b, (((1,), (1,)), ((), ())), preferred_element_type=F32)


def dot_tn(a, b):
    return lax.dot_general(a, b, (((0,), (0,)), ((), ())), preferred_element_type=F32)


def xor2(me, bit_one, bit_two, pair):
    value = me
    if bit_one:
        value = value ^ pair[0]
    if bit_two:
        value = value ^ pair[1]
    return value


def set_mask(mask_ref, col_ref, row_ref):
    @pl.loop(0, 8)
    def _(chunk):
        rows = pl.ds(pl.multiple_of(chunk * 128, 128), 128)
        near = jnp.abs(col_ref[rows, :] - row_ref[...]) < WINDOW // 2
        mask_ref[rows, :] = jnp.where(near, 0.0, MASKED_SCORE)


def attend_kernel(
    at_ref, own_ref, other_ref, t0, t1, t2, t3, col_ref, row_ref,
    qkv_ref, vec_ref, out_ref, lse_ref, joined_ref, w_ref, mask_ref, turn_ref,
):
    core, x_at = at_ref[2], at_ref[3]
    joined_ref[:, core] = own_ref[...]
    joined_ref[:, 1 - core] = other_ref[...]
    w_ref[...] = joined_ref[...].reshape(1024, 896)
    vec_ref[...] = w_ref[:, 768:896].astype(F32).T[:16]
    lanes = pl.ds(pl.multiple_of(x_at * 256, 256), 256)
    bias = jnp.concatenate([vec_ref[2:3, lanes], jnp.zeros((1, 256), F32), vec_ref[3:4, lanes]], axis=1)
    for j, tok in enumerate((t0, t1, t2, t3)):
        qkv_ref[j * 256 : j * 256 + 256, :] = (dot_nn(tok[...], w_ref[:, :768]) + bias).astype(BF16)
    set_mask(mask_ref, col_ref, row_ref)
    turn_ref[...] = qkv_ref[:, 512:768].T
    for block in range(4):
        rows = slice(block * 256, block * 256 + 256)
        outs = []
        for head in range(4):
            lanes = slice(head * 64, head * 64 + 64)
            key = qkv_ref[:, 256 + head * 64 : 320 + head * 64]
            query = qkv_ref[rows, lanes] * BF16(0.125)
            scores = dot_nt(key, query) + mask_ref[:, rows]
            top = jnp.max(scores, axis=0, keepdims=True)
            raised = jnp.exp(scores - top)
            total = jnp.sum(raised, axis=0, keepdims=True)
            probs = (raised * (1.0 / total)).astype(BF16)
            outs.append(dot_nn(turn_ref[lanes, :], probs))
            lse_ref[head : head + 1, rows] = jnp.log(total) + top
        out_ref[(x_at + block) % 4] = jnp.concatenate(outs, axis=0).T.astype(BF16)


def attend_back_kernel(
    at_ref, t0, t1, t2, t3, w_ref, qkv_ref, d_ref, col_ref, row_ref, lse_ref, small_ref,
    keep_ref, give_ref, own_ref, b1, b2, b3, dqkv_ref, sk_ref, sv_ref, rows_ref, mask_ref, turn_ref, joined_ref,
):
    core, x_at = at_ref[2], at_ref[3]
    set_mask(mask_ref, col_ref, row_ref)
    turn_ref[...] = qkv_ref[:, 256:512].T
    sk_ref[...] = jnp.zeros_like(sk_ref)
    sv_ref[...] = jnp.zeros_like(sv_ref)
    for block in range(4):
        rows = slice(block * 256, block * 256 + 256)
        d_block = d_ref[(x_at + block) % 4]
        outs = []
        for head in range(4):
            lanes = slice(head * 64, head * 64 + 64)
            key = qkv_ref[:, 256 + head * 64 : 320 + head * 64]
            value = qkv_ref[:, 512 + head * 64 : 576 + head * 64]
            query = qkv_ref[rows, lanes] * BF16(0.125)
            d_out = d_block[:, lanes]
            probs = jnp.exp(dot_nt(key, query) + mask_ref[:, rows] - lse_ref[head : head + 1, rows])
            d_probs = dot_nt(value, d_out)
            delta = jnp.sum(probs * d_probs, axis=0, keepdims=True)
            d_scores = (probs * (d_probs - delta)).astype(BF16)
            outs.append(dot_nn(turn_ref[lanes, :], d_scores) * 0.125)
            sk_ref[head] += dot_nn(d_scores, query)
            sv_ref[head] += dot_nn(probs.astype(BF16), d_out)
        dqkv_ref[rows, :256] = jnp.concatenate(outs, axis=0).T.astype(BF16)
    for head in range(4):
        dqkv_ref[:, 256 + head * 64 : 320 + head * 64] = sk_ref[head].astype(BF16)
        dqkv_ref[:, 512 + head * 64 : 576 + head * 64] = sv_ref[head].astype(BF16)
    rows_ref[...] = jnp.zeros_like(rows_ref)
    rows_ref[:16, :] = small_ref[...]
    lanes = pl.ds(pl.multiple_of(x_at * 256, 256), 256)
    sums = jnp.sum(dqkv_ref[...].astype(F32), axis=0, keepdims=True)
    rows_ref[2:3, lanes] = sums[:, :256]
    rows_ref[3:4, lanes] = sums[:, 512:]
    joined_ref[:, :, :, 768:896] = rows_ref[...].T.astype(BF16).reshape(16, 2, 32, 128)
    total = dot_tn(t0[...], dqkv_ref[:256, :])
    for block, tok in ((1, t1), (2, t2), (3, t3)):
        total = total + dot_tn(tok[...], dqkv_ref[block * 256 : block * 256 + 256, :])
    joined_ref[:, :, :, :768] = total.astype(BF16).reshape(16, 2, 32, 768)
    keep_ref[...] = joined_ref[:, core]
    give_ref[...] = joined_ref[:, 1 - core]
    for block, dst in enumerate((own_ref, b1, b2, b3)):
        back = dot_nt(dqkv_ref[block * 256 : block * 256 + 256, :], w_ref[...].reshape(1024, 896)[:, :768])
        dst[...] = back.astype(dst.dtype)


GELU_IN = 0.7978845608028654
GELU_CUBE = 0.044715


def norm_forward(value):
    center = value - jnp.mean(value, axis=-1, keepdims=True)
    spread = lax.rsqrt(jnp.mean(center * center, axis=-1, keepdims=True) + NORM_EPS)
    return center * spread, spread


def norm_back(d_normal, normal, spread):
    return spread * (
        d_normal
        - jnp.mean(d_normal, axis=-1, keepdims=True)
        - normal * jnp.mean(d_normal * normal, axis=-1, keepdims=True)
    )


def column_sum(value):
    return jnp.sum(value, axis=0, keepdims=True)


def token_kernel(
    at_ref, a0, a1, a2, a3, e0, e1, e2, e3, ctx_ref, tok_ref, cot_ref, vec_ref, ffb_ref,
    out_ref, keep_a, give_a, keep_b, give_b, done_ref, dctx_ref, small_ref, dffb_ref,
    w5, wd, hid, act, first_t, ctx_t, hf, n_one, r_one, d_two, d_first, d_hid, low, stage_a, stage_b, sem,
):
    z_at, y_at, core = at_ref[0], at_ref[1], at_ref[2]
    pairs = [masks(core, False), masks(core, True)]
    for parts, slot in ((pl.ds(4, 1), 0), (pl.ds(0, 4), 5)):
        for late, side, src in ((0, 0, a0), (1, 0, a1), (0, 1, a2), (1, 1, a3)):
            for block in range(8):
                y = xor2(y_at, block >> 2 & 1, late, pairs[side])
                z = xor2(z_at, block & 1, block >> 1 & 1, pairs[side])
                row = pl.multiple_of(((z * 4 + y) * 2 + (core ^ side)) * 32, 32)
                pltpu.make_async_copy(src.at[block, parts], w5.at[parts, pl.ds(row, 32), :], sem.at[slot]).start()
    for late, side, src in ((0, 0, e0), (1, 0, e1), (0, 1, e2), (1, 1, e3)):
        for block in range(8):
            z = xor2(z_at, block >> 2 & 1, late, pairs[side])
            y = xor2(y_at, block & 1, block >> 1 & 1, pairs[side])
            row = pl.multiple_of(((z * 4 + y) * 2 + (core ^ side)) * 128, 128)
            pltpu.make_async_copy(src.at[block], wd.at[pl.ds(row, 128), :], sem.at[1]).start()

    def ordered(scratch):
        for side in range(2):
            for block in range(16):
                y = xor2(y_at, block >> 3 & 1, block >> 2 & 1, pairs[side])
                z = xor2(z_at, block >> 1 & 1, block & 1, pairs[side])
                row = pl.multiple_of(((z * 4 + y) * 2 + (core ^ side)) * 32, 32)
                to = (side * 16 + block) * 32
                scratch[to : to + 32, :] = stage_b[pl.ds(row, 32), :256]

    for part in range(4):
        stage_b[part * 256 : part * 256 + 256, :256] = ctx_ref[part].T
    ordered(ctx_t)
    pltpu.make_async_copy(w5.at[pl.ds(4, 1)], w5.at[pl.ds(4, 1)], sem.at[0]).wait()
    attended = vec_ref[4:5, :]
    for part in range(4):
        attended = attended + dot_nn(ctx_ref[part], w5[4, part * 256 : part * 256 + 256, :])
    normal, spread = norm_forward(tok_ref[...].astype(F32) + attended)
    n_one[...] = normal
    r_one[...] = spread
    hf[...] = normal * vec_ref[0:1, :] + vec_ref[5:6, :]
    low[...] = hf[...].astype(BF16)
    stage_b[:, :256] = low[...].T
    ordered(first_t)
    pltpu.make_async_copy(w5.at[pl.ds(0, 4)], w5.at[pl.ds(0, 4)], sem.at[5]).wait()

    @pl.loop(0, 4)
    def _(cb):
        cols = pl.ds(pl.multiple_of(cb * 1024, 1024), 1024)
        hid[cb] = dot_nn(low[...], w5[cb]) + ffb_ref[:, cols]

        @pl.loop(0, 8)
        def _(chunk):
            rows = pl.ds(pl.multiple_of(chunk * 32, 32), 32)
            u = hid[cb, rows, :]
            t = jnp.tanh(GELU_IN * (u + GELU_CUBE * (u * u * u)))
            act[cb, rows, :] = (u * (0.5 * (1.0 + t))).astype(BF16)

    pltpu.make_async_copy(wd, wd, sem.at[1]).wait()
    d_first[...] = hf[...] + vec_ref[6:7, :]

    @pl.loop(0, 4)
    def _(cb):
        d_first[...] += dot_nn(act[cb], wd[pl.ds(pl.multiple_of(cb * 1024, 1024), 1024), :])

    normal, spread = norm_forward(d_first[...])
    out_ref[...] = (normal * vec_ref[1:2, :] + vec_ref[7:8, :]).astype(BF16)
    cot = cot_ref[...].astype(F32)
    small_ref[...] = jnp.zeros_like(small_ref)
    small_ref[1:2, :] = column_sum(cot * normal)
    small_ref[7:8, :] = column_sum(cot)
    d_two[...] = norm_back(cot * vec_ref[1:2, :], normal, spread)
    low[...] = d_two[...].astype(BF16)
    small_ref[6:7, :] = column_sum(low[...].astype(F32))
    d_first[...] = d_two[...]

    def send_a(part):
        return [
            pltpu.make_async_copy(stage_a.at[side], dst.at[:, part], sem.at[3 + side])
            for side, dst in ((0, keep_a), (1, give_a))
        ]

    @pl.loop(0, 4)
    def _(cb):
        @pl.when(cb > 0)
        def _():
            pltpu.make_async_copy(stage_b, stage_b, sem.at[2]).wait()

        stage_b[...] = dot_tn(act[cb], low[...]).astype(BF16)
        for side, dst in ((0, keep_b), (1, give_b)):
            one, two = pairs[side]
            gap = cb ^ z_at
            both = (gap == 2).astype(jnp.int32)
            place = ((gap == one).astype(jnp.int32) + both) * 8 + ((gap == two).astype(jnp.int32) + both) * 4
            for block in range(4):
                y = xor2(y_at, block >> 1, block & 1, pairs[side])
                row = pl.multiple_of((y * 2 + (core ^ side)) * 128, 128)
                pltpu.make_async_copy(stage_b.at[pl.ds(row, 128), :], dst.at[place + block], sem.at[2]).start()

        cols = pl.ds(pl.multiple_of(cb * 1024, 1024), 1024)
        d_hid[...] = dot_nt(low[...], wd[cols, :])
        dffb_ref[:, cols] = jnp.zeros((1, 1024), F32)

        @pl.loop(0, 8)
        def _(chunk):
            rows = pl.ds(pl.multiple_of(chunk * 32, 32), 32)
            u = hid[cb, rows, :]
            square = u * u
            t = jnp.tanh(GELU_IN * (u + GELU_CUBE * (square * u)))
            slope = 0.5 * (1.0 + t) + (0.5 * GELU_IN) * u * (1.0 - t * t) * (1.0 + (3.0 * GELU_CUBE) * square)
            d_low = (d_hid[rows, :] * slope).astype(BF16)
            act[cb, rows, :] = d_low
            dffb_ref[:, cols] += column_sum(d_low.astype(F32))

        @pl.when(cb > 0)
        def _():
            for copy in send_a(cb):
                copy.wait()

        stage_a[...] = dot_nn(first_t[...], act[cb]).astype(BF16).reshape(2, 16, 32, 1024)
        for copy in send_a(cb):
            copy.start()
        d_first[...] += dot_nt(act[cb], w5[cb])

    d_h = d_first[...]
    normal = n_one[...]
    small_ref[0:1, :] = column_sum(d_h * normal)
    small_ref[5:6, :] = column_sum(d_h)
    d_one = norm_back(d_h * vec_ref[0:1, :], normal, r_one[...])
    done_ref[...] = d_one
    low[...] = d_one.astype(BF16)
    small_ref[4:5, :] = column_sum(low[...].astype(F32))
    for part in range(4):
        dctx_ref[part] = dot_nt(low[...], w5[4, part * 256 : part * 256 + 256, :]).astype(BF16)
    for copy in send_a(4):
        copy.wait()
    stage_a[...] = dot_nn(ctx_t[...], low[...]).astype(BF16).reshape(2, 16, 32, 1024)
    for copy in send_a(4):
        copy.start()
    for copy in send_a(4):
        copy.wait()
    pltpu.make_async_copy(stage_b, stage_b, sem.at[2]).wait()


SMEM = pl.BlockSpec(memory_space=pltpu.SMEM)
VMEM = pl.BlockSpec(memory_space=pltpu.VMEM)
ANY = pl.BlockSpec(memory_space=pl.ANY)
MIB = 2**20


def attend(at, w_own, w_other, toks, code_col, code_row):
    return pl.pallas_call(
        attend_kernel,
        in_specs=[SMEM] + [VMEM] * 8,
        out_specs=[VMEM] * 5,
        out_shape=[
            jax.ShapeDtypeStruct((1024, 768), BF16),
            jax.ShapeDtypeStruct((16, 1024), F32),
            jax.ShapeDtypeStruct((4, 256, 256), BF16),
            jax.ShapeDtypeStruct((4, 1024), F32),
            jax.ShapeDtypeStruct((16, 2, 32, 896), BF16),
        ],
        scratch_shapes=[
            pltpu.VMEM((1024, 896), BF16),
            pltpu.VMEM((1024, 1024), F32),
            pltpu.VMEM((256, 1024), BF16),
        ],
        compiler_params=pltpu.CompilerParams(vmem_limit_bytes=48 * MIB),
        cost_estimate=pl.CostEstimate(flops=13 * 10**9, bytes_accessed=9 * MIB, transcendentals=4 * MIB),
        name="attend",
    )(at, w_own, w_other, *toks, code_col, code_row)


def attend_back(at, toks, w_in, qkv, d_all, code_col, code_row, lse, small):
    return pl.pallas_call(
        attend_back_kernel,
        in_specs=[SMEM] + [VMEM] * 11,
        out_specs=[VMEM] * 6,
        out_shape=[jax.ShapeDtypeStruct((16, 32, 896), BF16)] * 2
        + [jax.ShapeDtypeStruct((256, 1024), F32)]
        + [jax.ShapeDtypeStruct((256, 1024), BF16)] * 3,
        scratch_shapes=[
            pltpu.VMEM((1024, 768), BF16),
            pltpu.VMEM((4, 1024, 64), F32),
            pltpu.VMEM((4, 1024, 64), F32),
            pltpu.VMEM((128, 1024), F32),
            pltpu.VMEM((1024, 1024), F32),
            pltpu.VMEM((256, 1024), BF16),
            pltpu.VMEM((16, 2, 32, 896), BF16),
        ],
        compiler_params=pltpu.CompilerParams(vmem_limit_bytes=48 * MIB),
        cost_estimate=pl.CostEstimate(flops=22 * 10**9, bytes_accessed=14 * MIB, transcendentals=4 * MIB),
        name="attend_back",
    )(at, *toks, w_in, qkv, d_all, code_col, code_row, lse, small)


def token_layer(at, pieces_a, pieces_b, context, tokens, cotangent, vectors, ffb):
    return pl.pallas_call(
        token_kernel,
        in_specs=[SMEM] + [ANY] * 8 + [VMEM] * 5,
        out_specs=[VMEM] + [ANY] * 4 + [VMEM] * 4,
        out_shape=[jax.ShapeDtypeStruct((256, 1024), BF16)]
        + [jax.ShapeDtypeStruct((16, 5, 32, 1024), BF16)] * 2
        + [jax.ShapeDtypeStruct((16, 128, 1024), BF16)] * 2
        + [
            jax.ShapeDtypeStruct((256, 1024), F32),
            jax.ShapeDtypeStruct((4, 256, 256), BF16),
            jax.ShapeDtypeStruct((8, 1024), F32),
            jax.ShapeDtypeStruct((1, 4096), F32),
        ],
        scratch_shapes=[
            pltpu.VMEM((5, 1024, 1024), BF16),
            pltpu.VMEM((4096, 1024), BF16),
            pltpu.VMEM((4, 256, 1024), F32),
            pltpu.VMEM((4, 256, 1024), BF16),
            pltpu.VMEM((1024, 256), BF16),
            pltpu.VMEM((1024, 256), BF16),
            pltpu.VMEM((256, 1024), F32),
            pltpu.VMEM((256, 1024), F32),
            pltpu.VMEM((256, 1), F32),
            pltpu.VMEM((256, 1024), F32),
            pltpu.VMEM((256, 1024), F32),
            pltpu.VMEM((256, 1024), F32),
            pltpu.VMEM((256, 1024), BF16),
            pltpu.VMEM((2, 16, 32, 1024), BF16),
            pltpu.VMEM((1024, 1024), BF16),
            pltpu.SemaphoreType.DMA((6,)),
        ],
        compiler_params=pltpu.CompilerParams(vmem_limit_bytes=60 * MIB),
        cost_estimate=pl.CostEstimate(flops=15 * 10**9, bytes_accessed=45 * MIB, transcendentals=2 * MIB),
        name="token_layer",
    )(at, *pieces_a, *pieces_b, context, tokens, cotangent, vectors, ffb)


def squares_kernel(*refs):
    total = sum(jnp.sum(ref[...] * ref[...], keepdims=True) for ref in refs[:-1])
    refs[-1][...] = jnp.broadcast_to(total[None], refs[-1].shape)


def all_squares(grads):
    return pl.pallas_call(
        squares_kernel,
        in_specs=[VMEM] * 7,
        out_specs=VMEM,
        out_shape=jax.ShapeDtypeStruct((64, 8, 128), F32),
        name="squares",
    )(*grads)


def lamb_kernel(squares_ref, *refs):
    factor = CLIP_NORM / jnp.maximum(jnp.sqrt(squares_ref[...]), CLIP_NORM)
    for i in range(7):
        weight, grad = refs[i][...], refs[7 + i][...] * factor
        new_first = BETA_ONE * refs[14 + i][...] + (1.0 - BETA_ONE) * grad
        new_second = BETA_TWO * refs[21 + i][...] + (1.0 - BETA_TWO) * grad * grad
        direction = (
            new_first
            / (1.0 - BETA_ONE**STEP_COUNT)
            / (jnp.sqrt(new_second / (1.0 - BETA_TWO**STEP_COUNT)) + ADAM_EPS)
            + WEIGHT_DECAY * weight
        )
        weight_norm = jnp.sqrt(jnp.sum(weight * weight, keepdims=True))
        dir_norm = jnp.sqrt(jnp.sum(direction * direction, keepdims=True))
        refs[28 + i][...] = direction * (weight_norm / jnp.maximum(dir_norm, 1.0))


def lamb_steps(squares, weights, grads, firsts, seconds):
    return pl.pallas_call(
        lamb_kernel,
        in_specs=[VMEM] * 29,
        out_specs=[VMEM] * 7,
        out_shape=[jax.ShapeDtypeStruct(weight.shape, F32) for weight in weights],
        name="lamb",
    )(squares, *weights, *grads, *firsts, *seconds)


def body(tokens, cotangent, doc_lengths, *params):
    shards, firsts, seconds = params[:7], params[7:14], params[14:]
    lowered = tuple(weight.astype(BF16) for weight in shards)
    dp_index = lax.axis_index("dp")
    z_at, y_at, core, x_at = dp_index // 8, dp_index // 2 % 4, dp_index % 2, lax.axis_index("group")
    at = jnp.stack([z_at, y_at, core, x_at]).astype(jnp.int32)

    with jax.named_scope("gather_attn_in"):
        small = jnp.concatenate(
            [lowered[4], lowered[5], lowered[6].reshape(4, 8).T, jnp.zeros((8, 116), BF16)], axis=1
        )
        cols = lowered[0].reshape(8, 3, 4, 256)

        cols = cols.transpose(2, 0, 1, 3).reshape(4, 8, 768)
        packed = jnp.concatenate([cols, jnp.broadcast_to(small[None], (4, 8, 128))], axis=2)
        packed = jnp.broadcast_to(packed[None], (16, 4, 8, 896)).reshape(64, 8, 896)
        w_own = spread(packed).reshape(16, 32, 896)

    with jax.named_scope("gather_ff"):
        pack = jnp.concatenate(
            [lowered[2][:, cb * 1024 : cb * 1024 + 1024] for cb in range(4)] + [lowered[1], lowered[3]], axis=0
        )
        pack = rolled([pack[None]] + [push(pack, "x", -j)[None] for j in (1, 2, 3)], x_at, 0)
        part_a = pack[:, :40].reshape(4, 5, 8, 1024).transpose(1, 0, 2, 3).reshape(1, 5, 32, 1024)
        part_b = pack[:, 40:].reshape(1, 128, 1024)

    with jax.named_scope("gather_tokens"):
        toks = [tokens] + [push(tokens, "x", -j) for j in (1, 2, 3)]

    with jax.named_scope("gather_ff"):
        part_a, part_b = doubled(part_a, "z", 0), doubled(part_b, "y", 0)
        part_a, part_b, w_own, *toks = lax.optimization_barrier((part_a, part_b, w_own, *toks))
        w_other = push(w_own, "core", 1)
        part_a, part_b = doubled(part_a, "z", 1), doubled(part_b, "y", 1)
        part_a, part_b, w_other = lax.optimization_barrier((part_a, part_b, w_other))
        next_a, next_b = swap(part_a, "y", 0), swap(part_b, "z", 0)

    with jax.named_scope("attention"):
        order = (x_at + jnp.arange(4, dtype=jnp.int32)) % 4
        positions = (order[:, None] * 256 + jnp.arange(256, dtype=jnp.int32)[None]).reshape(1024)
        ends = [doc_lengths[0, 0], doc_lengths[0, 0] + doc_lengths[0, 1]]
        ends.append(ends[1] + doc_lengths[0, 2])
        ids = sum((positions >= end).astype(jnp.int32) for end in ends)
        code = (positions + 4096 * ids).astype(F32)
        code_col, code_row = code[:, None], code[None]
        qkv, vectors, out_all, lse, w_in = attend(at, w_own, w_other, toks, code_col, code_row)
        out_all, next_a, next_b = lax.optimization_barrier((out_all, next_a, next_b))
        context = lax.all_to_all(out_all, "group", 0, 0, tiled=True)
        ffb = vectors[8:12].reshape(4, 128, 8).transpose(1, 0, 2).reshape(1, 4096)

    with jax.named_scope("gather_ff"):
        pieces_a, pieces_b = pieces_of(part_a, next_a, "y"), pieces_of(part_b, next_b, "z")
        pieces_a, pieces_b, context = lax.optimization_barrier((pieces_a, pieces_b, context))
        pieces_a, pieces_b = (*pieces_a, push(pieces_a[1], "core", 1)), (*pieces_b, push(pieces_b[1], "core", 1))

    with jax.named_scope("tokens"):
        block_out, keep_a, give_a, keep_b, give_b, d_one, d_context, small, d_ffb = token_layer(
            at, pieces_a, pieces_b, context, tokens, cotangent, vectors, ffb
        )

    with jax.named_scope("scatter_ff"):
        terms_b = [keep_b, push(give_b, "core", 1)]
        terms_a = [keep_a, push(give_a, "core", 1)]
        sent_b, sent_a = outgoing(terms_b), outgoing(terms_a)

    with jax.named_scope("attention_back"):
        d_all = lax.all_to_all(d_context, "group", 0, 0, tiled=True)
        d_all, sent_b, sent_a = lax.optimization_barrier((d_all, sent_b, sent_a))

    with jax.named_scope("scatter_ff"):
        terms_b, terms_a = step_down(terms_b, sent_b, "z", 0), step_down(terms_a, sent_a, "y", 0)
        sent_b, sent_a = outgoing(terms_b), outgoing(terms_a)

    with jax.named_scope("attention_back"):
        ffb_rows = d_ffb.reshape(128, 4, 8).transpose(1, 0, 2).reshape(4, 1024)
        small = jnp.concatenate([small, ffb_rows, jnp.zeros((4, 1024), F32)], axis=0)
        keep_in, give_in, *backs = attend_back(at, toks, w_in, qkv, d_all, code_col, code_row, lse, small)

    with jax.named_scope("scatter_attn_in"):
        grad_in = (keep_in.astype(F32) + push(give_in, "core", 1).astype(F32)).astype(BF16)
        grad_in, sent_b, sent_a = lax.optimization_barrier((grad_in, sent_b, sent_a))
        got = spread(grad_in.reshape(64, 8, 896))
    with jax.named_scope("input_grad"):
        input_grad = d_one + backs[0]
        for j in (1, 3, 2):
            input_grad = input_grad + push(backs[j], "x", j).astype(F32)

    with jax.named_scope("scatter_ff"):
        for axis_b, axis_a, step in (("z", "y", 1), ("y", "z", 0), ("y", "z", 1)):
            if axis_b == "y":
                sent_b, sent_a = outgoing(terms_b), outgoing(terms_a)
                if step == 1:
                    input_grad, got, sent_b, sent_a = lax.optimization_barrier((input_grad, got, sent_b, sent_a))
            terms_b, terms_a = step_down(terms_b, sent_b, axis_b, step), step_down(terms_a, sent_a, axis_a, step)
        sum_b, sum_a = (sum(term[0].astype(F32) for term in terms) for terms in (terms_b, terms_a))
        pack = jnp.concatenate(
            [sum_a.reshape(5, 4, 8, 1024).transpose(1, 0, 2, 3).reshape(4, 40, 1024), sum_b.reshape(4, 32, 1024)], axis=1
        )
        total = pick(pack, x_at, 0)
        for k in (1, 3, 2):
            total = total + push(pick(pack, (x_at + k) % 4, 0).astype(BF16), "x", k).astype(F32)
        g_up = total[:32].reshape(4, 8, 1024).transpose(1, 0, 2).reshape(8, 4096)
        g_out, g_down = total[32:40], total[40:]

    with jax.named_scope("scatter_attn_in"):
        got = jnp.sum(got.reshape(16, 4, 8, 896).astype(F32), axis=0)
        g_in = got[:, :, :768].reshape(4, 8, 3, 256).transpose(1, 2, 0, 3).reshape(8, 3072)
        extra = jnp.sum(got[:, :, 768:780], axis=0)
        g_gains, g_biases, g_ffb = extra[:, :2], extra[:, 2:8], extra[:, 8:12].T.reshape(32)

    grads = (g_in, g_out, g_up, g_down, g_gains, g_biases, g_ffb)

    def flat(arrays):
        return (*arrays[:6], arrays[6].reshape(1, 32))

    with jax.named_scope("norm"):
        squares = spread(all_squares(flat(grads)))
        squares = jnp.sum(squares[:, :1, :1], axis=0)
        squares = squares + push(squares, "core", 1)
    with jax.named_scope("lamb"):
        steps = lamb_steps(squares, flat(shards), flat(grads), flat(firsts), flat(seconds))
        steps = (*steps[:6], steps[6].reshape(32))
    return (block_out, input_grad, *grads, *steps)


def solution(mesh):
    rows, vector, docs = P(AXES, None), P(AXES), P("dp", None)
    leaves = (rows,) * 6 + (vector,)
    return jax.shard_map(
        body,
        mesh=mesh,
        in_specs=(rows, rows, docs) + leaves * 3,
        out_specs=(rows, rows) + leaves * 2,
        check_vma=False,
    )
```

```python
import jax
import jax.numpy as jnp
import numpy as np
from jax import lax
from jax.experimental import pallas as pl
from jax.experimental.pallas import tpu as pltpu
from jax.sharding import PartitionSpec as P

HEADS = 16
WINDOW = 1024
AXES = ("dp", "group")
RADIX = {"z": 4, "y": 4, "core": 2, "x": 4}

NORM_EPS = 1e-06
CLIP_NORM = 1.0
BETA_ONE = 0.9
BETA_TWO = 0.999
STEP_COUNT = 10
ADAM_EPS = 1e-06
WEIGHT_DECAY = 0.01
MASKED_SCORE = -1e30
F32 = jnp.float32
BF16 = jnp.bfloat16


def flat_of(at):
    return ((at["z"] * 4 + at["y"]) * 2 + at["core"]) * 4 + at["x"]


def device_pairs(move):
    out = []
    for flat in range(128):
        at = {"z": flat // 32, "y": flat // 8 % 4, "core": flat // 4 % 2, "x": flat % 4}
        move(at)
        out.append((flat, flat_of(at)))
    return out


def push(value, axis, shift):
    def move(at):
        at[axis] = (at[axis] + shift) % RADIX[axis]

    return lax.ppermute(value, AXES, device_pairs(move))


def swap(value, axis, step):
    def move(at):
        at[axis] ^= (1, 3)[(at["core"] + step) % 2]

    return lax.ppermute(value, AXES, device_pairs(move))


def spread(value, axes):
    names = ("z", "y", "core", "x")
    order = [name for name in names if name not in axes] + list(axes)
    grid = np.arange(128).reshape(4, 4, 2, 4).transpose([names.index(name) for name in order])
    groups = grid.reshape(-1, value.shape[0]).tolist()
    return lax.all_to_all(value, AXES, 0, 0, axis_index_groups=groups, tiled=True)


def pick(value, index, dim):
    return lax.dynamic_index_in_dim(value, index, dim, keepdims=False)


def rolled(parts, me, dim):
    joined = jnp.concatenate(parts + parts[:3], axis=dim)
    width = parts[0].shape[dim]
    return lax.dynamic_slice_in_dim(joined, (4 - me) % 4 * width, 4 * width, dim)


def doubled(value, axis, step):
    return jnp.concatenate([value, swap(value, axis, step)], axis=0)


def outgoing(terms):
    half = terms[0].shape[0] // 2
    return sum(term[half:].astype(F32) for term in terms).astype(BF16)


def step_down(terms, sent, axis, step):
    half = terms[0].shape[0] // 2
    terms = [term[:half] for term in terms] + [swap(sent, axis, step)]
    if half == 1:
        terms = [term[0] for term in terms]
    return terms


def masks(core, owner_is_other):
    one = core * 2 + 1
    two = 3 - core * 2
    return (two, one) if owner_is_other else (one, two)


def dot_nn(a, b):
    return jnp.dot(a, b, preferred_element_type=F32)


def dot_nt(a, b):
    return lax.dot_general(a, b, (((1,), (1,)), ((), ())), preferred_element_type=F32)


def dot_tn(a, b):
    return lax.dot_general(a, b, (((0,), (0,)), ((), ())), preferred_element_type=F32)


def xor2(me, bit_one, bit_two, pair):
    value = me
    if bit_one:
        value = value ^ pair[0]
    if bit_two:
        value = value ^ pair[1]
    return value


def set_mask(mask_ref, col_ref, row_ref):
    @pl.loop(0, 8)
    def _(chunk):
        rows = pl.ds(pl.multiple_of(chunk * 128, 128), 128)
        near = jnp.abs(col_ref[rows, :] - row_ref[...]) < WINDOW // 2
        mask_ref[rows, :] = jnp.where(near, 0.0, MASKED_SCORE)


def attend_kernel(
    at_ref, own_ref, other_ref, t0, t1, t2, t3, col_ref, row_ref,
    qkv_ref, vec_ref, out_ref, lse_ref, w_ref, mask_ref, turn_ref,
):
    z_at, y_at, core, x_at = at_ref[0], at_ref[1], at_ref[2], at_ref[3]
    for side, src in ((0, own_ref), (1, other_ref)):
        pair = masks(core, side == 1)
        for block in range(16):
            y = xor2(y_at, block & 1, block >> 1 & 1, pair)
            z = xor2(z_at, block >> 2 & 1, block >> 3 & 1, pair)
            row = pl.multiple_of(((z * 4 + y) * 2 + (core ^ side)) * 32, 32)
            w_ref[pl.ds(row, 32), :] = src[block]
    vec_ref[...] = w_ref[:, 768:896].astype(F32).T[:16]
    lanes = pl.ds(pl.multiple_of(x_at * 256, 256), 256)
    bias = jnp.concatenate([vec_ref[2:3, lanes], jnp.zeros((1, 256), F32), vec_ref[3:4, lanes]], axis=1)
    for j, tok in enumerate((t0, t1, t2, t3)):
        qkv_ref[j * 256 : j * 256 + 256, :] = (dot_nn(tok[...], w_ref[:, :768]) + bias).astype(BF16)
    set_mask(mask_ref, col_ref, row_ref)
    turn_ref[...] = qkv_ref[:, 512:768].T
    outs = []
    for head in range(4):
        lanes = slice(head * 64, head * 64 + 64)
        key = qkv_ref[:, 256 + head * 64 : 320 + head * 64]
        scores = dot_nt(key, qkv_ref[:, lanes] * BF16(0.125)) + mask_ref[...]
        top = jnp.max(scores, axis=0, keepdims=True)
        raised = jnp.exp(scores - top)
        total = jnp.sum(raised, axis=0, keepdims=True)
        probs = (raised * (1.0 / total)).astype(BF16)
        outs.append(dot_nn(turn_ref[lanes, :], probs))
        lse_ref[head : head + 1, :] = jnp.log(total) + top
    out = jnp.concatenate(outs, axis=0).T.astype(BF16)
    for block in range(4):
        out_ref[(x_at + block) % 4] = out[block * 256 : block * 256 + 256]


def attend_back_kernel(
    at_ref, t0, t1, t2, t3, w_src, qkv_ref, d_ref, col_ref, row_ref, lse_ref, small_ref,
    keep_ref, give_ref, back_ref, dqkv_ref, d_rows, rows_ref, mask_ref, turn_ref, joined_ref,
    tok_ref, w_ref, sem,
):
    z_at, y_at, core, x_at = at_ref[0], at_ref[1], at_ref[2], at_ref[3]
    copies = [pltpu.make_async_copy(src, tok_ref.at[i], sem.at[i]) for i, src in enumerate((t0, t1, t2, t3))]
    copies.append(pltpu.make_async_copy(w_src, w_ref, sem.at[4]))
    for copy in copies:
        copy.start()
    set_mask(mask_ref, col_ref, row_ref)
    turn_ref[...] = qkv_ref[:, 256:512].T
    for block in range(4):
        d_rows[block * 256 : block * 256 + 256, :] = d_ref[(x_at + block) % 4]
    outs = []
    for head in range(4):
        lanes = slice(head * 64, head * 64 + 64)
        key = qkv_ref[:, 256 + head * 64 : 320 + head * 64]
        value = qkv_ref[:, 512 + head * 64 : 576 + head * 64]
        query = qkv_ref[:, lanes] * BF16(0.125)
        d_out = d_rows[:, lanes]
        probs = jnp.exp(dot_nt(key, query) + mask_ref[...] - lse_ref[head : head + 1, :])
        d_probs = dot_nt(value, d_out)
        delta = jnp.sum(probs * d_probs, axis=0, keepdims=True)
        d_scores = (probs * (d_probs - delta)).astype(BF16)
        outs.append(dot_nn(turn_ref[lanes, :], d_scores) * 0.125)
        dqkv_ref[:, 256 + head * 64 : 320 + head * 64] = dot_nn(d_scores, query).astype(BF16)
        dqkv_ref[:, 512 + head * 64 : 576 + head * 64] = dot_nn(probs.astype(BF16), d_out).astype(BF16)
    dqkv_ref[:, :256] = jnp.concatenate(outs, axis=0).T.astype(BF16)
    rows_ref[...] = jnp.zeros_like(rows_ref)
    rows_ref[:16, :] = small_ref[...]
    lanes = pl.ds(pl.multiple_of(x_at * 256, 256), 256)
    sums = jnp.sum(dqkv_ref[...].astype(F32), axis=0, keepdims=True)
    rows_ref[2:3, lanes] = sums[:, :256]
    rows_ref[3:4, lanes] = sums[:, 512:]
    joined_ref[:, :, :, 768:896] = rows_ref[...].T.astype(BF16).reshape(16, 2, 32, 128)
    for copy in copies:
        copy.wait()
    total = dot_tn(tok_ref[0], dqkv_ref[:256, :])
    for block in (1, 2, 3):
        total = total + dot_tn(tok_ref[block], dqkv_ref[block * 256 : block * 256 + 256, :])
    joined_ref[:, :, :, :768] = total.astype(BF16).reshape(16, 2, 32, 768)
    for side, dst in ((0, keep_ref), (1, give_ref)):
        pair = masks(core, side == 1)
        for block in range(16):
            y = xor2(y_at, block >> 3 & 1, block >> 2 & 1, pair)
            z = xor2(z_at, block >> 1 & 1, block & 1, pair)
            dst[block] = joined_ref[z * 4 + y, core ^ side]
    for block in range(4):
        back = dot_nt(dqkv_ref[block * 256 : block * 256 + 256, :], w_ref[:, :768])
        back_ref[(x_at + block) % 4] = back.astype(BF16)


GELU_IN = 0.7978845608028654
GELU_CUBE = 0.044715


def norm_forward(value):
    center = value - jnp.mean(value, axis=-1, keepdims=True)
    spread = lax.rsqrt(jnp.mean(center * center, axis=-1, keepdims=True) + NORM_EPS)
    return center * spread, spread


def norm_back(d_normal, normal, spread):
    return spread * (
        d_normal
        - jnp.mean(d_normal, axis=-1, keepdims=True)
        - normal * jnp.mean(d_normal * normal, axis=-1, keepdims=True)
    )


def column_sum(value):
    return jnp.sum(value, axis=0, keepdims=True)


def token_kernel(
    at_ref, a0, a1, a2, a3, e0, e1, e2, e3, ctx_ref, tok_ref, cot_ref, vec_ref, ffb_ref,
    out_ref, acts_ref, done_ref, dctx_ref, small_ref, dffb_ref,
    w5, wd, hid, act, d_act, kept, hf, n_one, r_one, d_two, d_first, d_hid, sem,
):
    z_at, y_at, core = at_ref[0], at_ref[1], at_ref[2]
    pairs = [masks(core, False), masks(core, True)]
    for parts, slot in ((pl.ds(4, 1), 0), (pl.ds(0, 4), 5)):
        for late, side, src in ((0, 0, a0), (1, 0, a1), (0, 1, a2), (1, 1, a3)):
            for block in range(8):
                y = xor2(y_at, block >> 2 & 1, late, pairs[side])
                z = xor2(z_at, block & 1, block >> 1 & 1, pairs[side])
                row = pl.multiple_of(((z * 4 + y) * 2 + (core ^ side)) * 32, 32)
                pltpu.make_async_copy(src.at[block, parts], w5.at[parts, pl.ds(row, 32), :], sem.at[slot]).start()
    for late, side, src in ((0, 0, e0), (1, 0, e1), (0, 1, e2), (1, 1, e3)):
        for block in range(8):
            z = xor2(z_at, block >> 2 & 1, late, pairs[side])
            y = xor2(y_at, block & 1, block >> 1 & 1, pairs[side])
            row = pl.multiple_of(((z * 4 + y) * 2 + (core ^ side)) * 128, 128)
            pltpu.make_async_copy(src.at[block], wd.at[pl.ds(row, 128), :], sem.at[1]).start()

    def out_z(cb):
        return pltpu.make_async_copy(act.at[cb], acts_ref.at[cb], sem.at[2])

    def out_d(cb):
        return pltpu.make_async_copy(d_act.at[cb], acts_ref.at[4 + cb], sem.at[3])

    def out_kept(part):
        return pltpu.make_async_copy(kept.at[part], acts_ref.at[8 + part], sem.at[4])

    for part in range(4):
        kept[3, :, part * 256 : part * 256 + 256] = ctx_ref[part]
    out_kept(3).start()
    pltpu.make_async_copy(w5.at[pl.ds(4, 1)], w5.at[pl.ds(4, 1)], sem.at[0]).wait()
    attended = vec_ref[4:5, :]
    for part in range(4):
        attended = attended + dot_nn(ctx_ref[part], w5[4, part * 256 : part * 256 + 256, :])
    normal, spread = norm_forward(tok_ref[...].astype(F32) + attended)
    n_one[...] = normal
    r_one[...] = spread
    hf[...] = normal * vec_ref[0:1, :] + vec_ref[5:6, :]
    kept[2] = hf[...].astype(BF16)
    out_kept(2).start()
    pltpu.make_async_copy(w5.at[pl.ds(0, 4)], w5.at[pl.ds(0, 4)], sem.at[5]).wait()

    @pl.loop(0, 4)
    def _(cb):
        cols = pl.ds(pl.multiple_of(cb * 1024, 1024), 1024)
        hid[cb] = dot_nn(kept[2], w5[cb]) + ffb_ref[:, cols]

        @pl.loop(0, 8)
        def _(chunk):
            rows = pl.ds(pl.multiple_of(chunk * 32, 32), 32)
            u = hid[cb, rows, :]
            t = jnp.tanh(GELU_IN * (u + GELU_CUBE * (u * u * u)))
            act[cb, rows, :] = (u * (0.5 * (1.0 + t))).astype(BF16)

        out_z(cb).start()

    pltpu.make_async_copy(wd, wd, sem.at[1]).wait()
    d_first[...] = hf[...] + vec_ref[6:7, :]

    @pl.loop(0, 4)
    def _(cb):
        d_first[...] += dot_nn(act[cb], wd[pl.ds(pl.multiple_of(cb * 1024, 1024), 1024), :])

    normal, spread = norm_forward(d_first[...])
    out_ref[...] = (normal * vec_ref[1:2, :] + vec_ref[7:8, :]).astype(BF16)
    cot = cot_ref[...].astype(F32)
    small_ref[...] = jnp.zeros_like(small_ref)
    small_ref[1:2, :] = column_sum(cot * normal)
    small_ref[7:8, :] = column_sum(cot)
    d_two[...] = norm_back(cot * vec_ref[1:2, :], normal, spread)
    kept[1] = d_two[...].astype(BF16)
    out_kept(1).start()
    small_ref[6:7, :] = column_sum(kept[1].astype(F32))
    d_first[...] = d_two[...]

    @pl.loop(0, 4)
    def _(cb):
        cols = pl.ds(pl.multiple_of(cb * 1024, 1024), 1024)
        d_hid[...] = dot_nt(kept[1], wd[cols, :])
        dffb_ref[:, cols] = jnp.zeros((1, 1024), F32)

        @pl.loop(0, 8)
        def _(chunk):
            rows = pl.ds(pl.multiple_of(chunk * 32, 32), 32)
            u = hid[cb, rows, :]
            square = u * u
            t = jnp.tanh(GELU_IN * (u + GELU_CUBE * (square * u)))
            slope = 0.5 * (1.0 + t) + (0.5 * GELU_IN) * u * (1.0 - t * t) * (1.0 + (3.0 * GELU_CUBE) * square)
            d_low = (d_hid[rows, :] * slope).astype(BF16)
            d_act[cb, rows, :] = d_low
            dffb_ref[:, cols] += column_sum(d_low.astype(F32))

        out_d(cb).start()
        d_first[...] += dot_nt(d_act[cb], w5[cb])

    d_h = d_first[...]
    normal = n_one[...]
    small_ref[0:1, :] = column_sum(d_h * normal)
    small_ref[5:6, :] = column_sum(d_h)
    d_one = norm_back(d_h * vec_ref[0:1, :], normal, r_one[...])
    done_ref[...] = d_one
    kept[0] = d_one.astype(BF16)
    out_kept(0).start()
    small_ref[4:5, :] = column_sum(kept[0].astype(F32))
    for part in range(4):
        dctx_ref[part] = dot_nt(kept[0], w5[4, part * 256 : part * 256 + 256, :]).astype(BF16)
    for cb in range(4):
        out_z(cb).wait()
        out_d(cb).wait()
        out_kept(cb).wait()


def wide_kernel(at_ref, d_own, d_oth, l_own, l_oth, a0_ref, a1_ref, left, turn):
    z_at, y_at, core = at_ref[0], at_ref[1], at_ref[2]
    pair = masks(core, False)
    step = pl.program_id(0)

    @pl.when((step == 0) | (step == 4))
    def _():
        for half, src in ((0, l_own), (1, l_oth)):
            turn[...] = src[0].T
            for block in range(16):
                z = xor2(z_at, block >> 3 & 1, block >> 2 & 1, pair)
                y = xor2(y_at, block >> 1 & 1, block & 1, pair)
                row = pl.multiple_of(((z * 4 + y) * 2 + core) * 32, 32)
                left[block * 32 : block * 32 + 32, half * 256 : half * 256 + 256] = turn[pl.ds(row, 32), :]

    grad = dot_nn(left[:, :256], d_own[0]) + dot_nn(left[:, 256:], d_oth[0])
    grad = grad.astype(BF16).reshape(16, 32, 1024)
    a0_ref[:, 0] = grad[:8]
    a1_ref[:, 0] = grad[8:]


def down_kernel(at_ref, z_own, z_oth, f_own, f_oth, b0_ref, b1_ref, picked):
    y_at, core = at_ref[1], at_ref[2]
    pair = masks(core, False)
    for half, src in ((0, z_own), (1, z_oth)):
        for block in range(4):
            y = xor2(y_at, block >> 1, block & 1, pair)
            lanes = pl.ds(pl.multiple_of((y * 2 + core) * 128, 128), 128)
            picked[half, :, block * 128 : block * 128 + 128] = src[0, :, lanes]
    grad = dot_tn(picked[0], f_own[0]) + dot_tn(picked[1], f_oth[0])
    grad = grad.astype(BF16).reshape(4, 128, 1024)
    b0_ref[:, 0] = grad[:2]
    b1_ref[:, 0] = grad[2:]


def act_block(index):
    return pl.BlockSpec((1, 256, 1024), lambda i, at_ref: (index(i), 0, 0))


def wide_grads(at, own, other):
    half = pl.BlockSpec((8, 1, 32, 1024), lambda i, at_ref: (0, i, 0, 0))
    return pl.pallas_call(
        wide_kernel,
        grid_spec=pltpu.PrefetchScalarGridSpec(
            num_scalar_prefetch=1,
            grid=(5,),
            in_specs=[act_block(lambda i: 4 + i)] * 2 + [act_block(lambda i: 10 + i // 4)] * 2,
            out_specs=[half, half],
            scratch_shapes=[pltpu.VMEM((512, 512), BF16), pltpu.VMEM((1024, 256), BF16)],
        ),
        out_shape=[pltpu.HBM((8, 5, 32, 1024), BF16)] * 2,
        compiler_params=pltpu.CompilerParams(vmem_limit_bytes=60 * MIB),
        cost_estimate=pl.CostEstimate(flops=3 * 10**9, bytes_accessed=12 * MIB, transcendentals=0),
        name="wide_grads",
    )(at, own, other, own, other)


def down_grads(at, own, other):
    def place(step, at_ref):
        one, two = masks(at_ref[2], False)
        gap = step ^ at_ref[0]
        both = (gap == 2).astype(jnp.int32)
        return ((gap == one).astype(jnp.int32) + both) * 2 + (gap == two).astype(jnp.int32) + both

    half = pl.BlockSpec((2, 1, 128, 1024), lambda i, at_ref: (0, place(i, at_ref), 0, 0))
    return pl.pallas_call(
        down_kernel,
        grid_spec=pltpu.PrefetchScalarGridSpec(
            num_scalar_prefetch=1,
            grid=(4,),
            in_specs=[act_block(lambda i: i)] * 2 + [act_block(lambda i: 9)] * 2,
            out_specs=[half, half],
            scratch_shapes=[pltpu.VMEM((2, 256, 512), BF16)],
        ),
        out_shape=[pltpu.HBM((2, 4, 128, 1024), BF16)] * 2,
        compiler_params=pltpu.CompilerParams(vmem_limit_bytes=60 * MIB),
        cost_estimate=pl.CostEstimate(flops=3 * 10**9, bytes_accessed=10 * MIB, transcendentals=0),
        name="down_grads",
    )(at, own, other, own, other)


SMEM = pl.BlockSpec(memory_space=pltpu.SMEM)
VMEM = pl.BlockSpec(memory_space=pltpu.VMEM)
ANY = pl.BlockSpec(memory_space=pl.ANY)
MIB = 2**20


def pack_kernel(up_ref, out_ref, down_ref, in_ref, gains_ref, bias_ref, ffb_ref, pack_ref, rows, square):
    for cb in range(4):
        rows[cb * 8 : cb * 8 + 8, :] = up_ref[:, cb * 1024 : cb * 1024 + 1024]
    rows[32:40, :] = out_ref[...]
    rows[40:72, :] = down_ref[...]
    for cb in range(3):
        rows[72 + cb * 8 : 80 + cb * 8, :] = in_ref[:, cb * 1024 : cb * 1024 + 1024]
    square[...] = jnp.zeros_like(square)
    square[0:2, :8] = gains_ref[...]
    for j in range(4):
        square[8 + j : 9 + j, :8] = ffb_ref[:, j * 8 : j * 8 + 8]
    rows[96:104, :] = jnp.zeros((8, 1024), F32)
    rows[96:104, :128] = square[...].T[:8]
    rows[96:104, 2:8] = bias_ref[...]
    pack_ref[...] = rows[...].astype(BF16)


def packed_rows(arrays):
    return pl.pallas_call(
        pack_kernel,
        in_specs=[VMEM] * 7,
        out_specs=VMEM,
        out_shape=jax.ShapeDtypeStruct((104, 1024), BF16),
        scratch_shapes=[pltpu.VMEM((104, 1024), F32), pltpu.VMEM((128, 128), F32)],
        name="pack_rows",
    )(arrays[2], arrays[1], arrays[3], arrays[0], *arrays[4:])


def finish_kernel(at_ref, p0, p1, p2, p3, in_ref, out_ref, up_ref, down_ref, gains_ref, bias_ref, ffb_ref, sq_ref, square):
    x_at = at_ref[3]
    parts = [ref[...].astype(F32) for ref in (p0, p1, p2, p3)]
    total = parts[0][:72] + parts[1][:72] + parts[2][:72] + parts[3][:72]
    for cb in range(4):
        up_ref[:, cb * 1024 : cb * 1024 + 1024] = total[cb * 8 : cb * 8 + 8]
    out_ref[...] = total[32:40]
    down_ref[...] = total[40:72]
    extra = jnp.zeros((8, 128), F32)
    squares = jnp.sum(total * total, keepdims=True)
    for j, part in enumerate(parts):
        rows = part[72:80]
        group = (x_at + j) % 4
        for block in range(3):
            cols = pl.ds(pl.multiple_of(block * 1024 + group * 256, 256), 256)
            in_ref[:, cols] = rows[:, block * 256 : block * 256 + 256]
        squares = squares + jnp.sum(rows[:, :768] * rows[:, :768], keepdims=True)
        extra = extra + rows[:, 768:896]
    square[...] = jnp.zeros_like(square)
    square[:8, :] = extra
    turned = square[...].T
    gains_ref[...] = turned[0:2, :8]
    bias_ref[...] = extra[:, 2:8]
    for j in range(4):
        ffb_ref[:, j * 8 : j * 8 + 8] = turned[8 + j : 9 + j, :8]
    squares = squares + jnp.sum(turned[:12] * turned[:12], keepdims=True)
    sq_ref[...] = jnp.broadcast_to(squares[None], sq_ref.shape)


def finished(at, parts):
    shapes = [(8, 3072), (8, 1024), (8, 4096), (32, 1024), (2, 8), (8, 6), (1, 32), (128, 8, 128)]
    return pl.pallas_call(
        finish_kernel,
        in_specs=[SMEM] + [VMEM] * 4,
        out_specs=[VMEM] * 8,
        out_shape=[jax.ShapeDtypeStruct(shape, F32) for shape in shapes],
        scratch_shapes=[pltpu.VMEM((128, 128), F32)],
        name="finish",
    )(at, *parts)


def attend(at, w_own, w_other, toks, code_col, code_row):
    return pl.pallas_call(
        attend_kernel,
        in_specs=[SMEM] + [VMEM] * 8,
        out_specs=[VMEM] * 5,
        out_shape=[
            jax.ShapeDtypeStruct((1024, 768), BF16),
            jax.ShapeDtypeStruct((16, 1024), F32),
            jax.ShapeDtypeStruct((4, 256, 256), BF16),
            jax.ShapeDtypeStruct((4, 1024), F32),
            jax.ShapeDtypeStruct((1024, 1024), BF16),
        ],
        scratch_shapes=[
            pltpu.VMEM((1024, 1024), F32),
            pltpu.VMEM((256, 1024), BF16),
        ],
        compiler_params=pltpu.CompilerParams(vmem_limit_bytes=56 * MIB),
        cost_estimate=pl.CostEstimate(flops=13 * 10**9, bytes_accessed=9 * MIB, transcendentals=4 * MIB),
        name="attend",
    )(at, w_own, w_other, *toks, code_col, code_row)


def attend_back(at, toks, w_in, qkv, d_all, code_col, code_row, lse, small):
    return pl.pallas_call(
        attend_back_kernel,
        in_specs=[SMEM] + [ANY] * 5 + [VMEM] * 6,
        out_specs=[VMEM] * 3,
        out_shape=[jax.ShapeDtypeStruct((16, 32, 896), BF16)] * 2 + [jax.ShapeDtypeStruct((4, 256, 1024), BF16)],
        scratch_shapes=[
            pltpu.VMEM((1024, 768), BF16),
            pltpu.VMEM((1024, 256), BF16),
            pltpu.VMEM((128, 1024), F32),
            pltpu.VMEM((1024, 1024), F32),
            pltpu.VMEM((256, 1024), BF16),
            pltpu.VMEM((16, 2, 32, 896), BF16),
            pltpu.VMEM((4, 256, 1024), BF16),
            pltpu.VMEM((1024, 1024), BF16),
            pltpu.SemaphoreType.DMA((5,)),
        ],
        compiler_params=pltpu.CompilerParams(vmem_limit_bytes=56 * MIB),
        cost_estimate=pl.CostEstimate(flops=22 * 10**9, bytes_accessed=14 * MIB, transcendentals=4 * MIB),
        name="attend_back",
    )(at, *toks, w_in, qkv, d_all, code_col, code_row, lse, small)


def token_layer(at, pieces_a, pieces_b, context, tokens, cotangent, vectors, ffb):
    return pl.pallas_call(
        token_kernel,
        in_specs=[SMEM] + [ANY] * 8 + [VMEM] * 5,
        out_specs=[VMEM, ANY] + [VMEM] * 4,
        out_shape=[
            jax.ShapeDtypeStruct((256, 1024), BF16),
            jax.ShapeDtypeStruct((12, 256, 1024), BF16),
            jax.ShapeDtypeStruct((256, 1024), F32),
            jax.ShapeDtypeStruct((4, 256, 256), BF16),
            jax.ShapeDtypeStruct((8, 1024), F32),
            jax.ShapeDtypeStruct((1, 4096), F32),
        ],
        scratch_shapes=[
            pltpu.VMEM((5, 1024, 1024), BF16),
            pltpu.VMEM((4096, 1024), BF16),
            pltpu.VMEM((4, 256, 1024), F32),
            pltpu.VMEM((4, 256, 1024), BF16),
            pltpu.VMEM((4, 256, 1024), BF16),
            pltpu.VMEM((4, 256, 1024), BF16),
            pltpu.VMEM((256, 1024), F32),
            pltpu.VMEM((256, 1024), F32),
            pltpu.VMEM((256, 1), F32),
            pltpu.VMEM((256, 1024), F32),
            pltpu.VMEM((256, 1024), F32),
            pltpu.VMEM((256, 1024), F32),
            pltpu.SemaphoreType.DMA((6,)),
        ],
        compiler_params=pltpu.CompilerParams(vmem_limit_bytes=60 * MIB),
        cost_estimate=pl.CostEstimate(flops=10 * 10**9, bytes_accessed=30 * MIB, transcendentals=2 * MIB),
        name="token_layer",
    )(at, *pieces_a, *pieces_b, context, tokens, cotangent, vectors, ffb)


def lamb_kernel(squares_ref, *refs):
    factor = CLIP_NORM / jnp.maximum(jnp.sqrt(squares_ref[...]), CLIP_NORM)
    for i in range(7):
        weight, grad = refs[i][...], refs[7 + i][...] * factor
        new_first = BETA_ONE * refs[14 + i][...] + (1.0 - BETA_ONE) * grad
        new_second = BETA_TWO * refs[21 + i][...] + (1.0 - BETA_TWO) * grad * grad
        direction = (
            new_first
            / (1.0 - BETA_ONE**STEP_COUNT)
            / (jnp.sqrt(new_second / (1.0 - BETA_TWO**STEP_COUNT)) + ADAM_EPS)
            + WEIGHT_DECAY * weight
        )
        weight_norm = jnp.sqrt(jnp.sum(weight * weight, keepdims=True))
        dir_norm = jnp.sqrt(jnp.sum(direction * direction, keepdims=True))
        refs[28 + i][...] = direction * (weight_norm / jnp.maximum(dir_norm, 1.0))


def lamb_steps(squares, weights, grads, firsts, seconds):
    return pl.pallas_call(
        lamb_kernel,
        in_specs=[VMEM] * 29,
        out_specs=[VMEM] * 7,
        out_shape=[jax.ShapeDtypeStruct(weight.shape, F32) for weight in weights],
        name="lamb",
    )(squares, *weights, *grads, *firsts, *seconds)


def body(tokens, cotangent, doc_lengths, *params):

    def turned(arrays):
        return (*arrays[:4], arrays[4].T, arrays[5], arrays[6].reshape(1, 32))

    shards, firsts, seconds = turned(params[:7]), turned(params[7:14]), turned(params[14:])
    dp_index = lax.axis_index("dp")
    z_at, y_at, core, x_at = dp_index // 8, dp_index // 2 % 4, dp_index % 2, lax.axis_index("group")
    at = jnp.stack([z_at, y_at, core, x_at]).astype(jnp.int32)

    with jax.named_scope("gather_x"):
        pack = packed_rows(shards)
        pack = rolled([pack[None]] + [push(pack, "x", -j)[None] for j in (1, 2, 3)], x_at, 0)
        own = lax.dynamic_slice_in_dim(pack[:, 72:96], x_at * 256, 256, axis=2)
        own = own.reshape(4, 3, 8, 256).transpose(0, 2, 1, 3).reshape(4, 8, 768)
        own = jnp.concatenate([own, pack[:, 96:, :256]], axis=2)
        part_a = pack[:, :40].reshape(4, 5, 8, 1024).transpose(1, 0, 2, 3).reshape(1, 5, 32, 1024)
        part_b = jnp.concatenate([pack[:, 40:72].reshape(1, 4, 32, 1024), own.reshape(1, 1, 32, 1024)], axis=1)

    with jax.named_scope("gather_tokens"):
        toks = [tokens, push(tokens, "x", -1), tokens, push(tokens, "x", -3)]

    with jax.named_scope("visible"):
        order = (x_at + jnp.arange(4, dtype=jnp.int32)) % 4
        positions = (order[:, None] * 256 + jnp.arange(256, dtype=jnp.int32)[None]).reshape(1024)
        ends = [doc_lengths[0, 0], doc_lengths[0, 0] + doc_lengths[0, 1]]
        ends.append(ends[1] + doc_lengths[0, 2])
        ids = sum((positions >= end).astype(jnp.int32) for end in ends)
        code = (positions + 4096 * ids).astype(F32)
        code_col, code_row = code[:, None], code[None]

    with jax.named_scope("gather_yz"):
        part_a, part_b = doubled(part_a, "z", 0), doubled(part_b, "y", 0)
        part_a, part_b = doubled(part_a, "z", 1), doubled(part_b, "y", 1)
        part_a, part_b, *toks = lax.optimization_barrier((part_a, part_b, *toks))
        toks[2] = push(toks[2], "x", -2)
        part_b, w_own = part_b[:, :4].reshape(4, 128, 1024), part_b[:, 4]
        w_own = doubled(w_own, "z", 0)
        part_a, part_b, w_own, at, code_col, code_row = lax.optimization_barrier(
            (part_a, part_b, w_own, at, code_col, code_row)
        )
        w_own = doubled(w_own, "z", 1)
        part_a, part_b = doubled(part_a, "y", 0), doubled(part_b, "z", 0)
        part_a, part_b, w_own, toks[2] = lax.optimization_barrier((part_a, part_b, w_own, toks[2]))
        w_other = push(w_own, "core", 1)
        far_a, far_b = swap(part_a, "y", 1), swap(part_b, "z", 1)
        part_a, part_b, w_other = lax.optimization_barrier((part_a, part_b, w_other))

    with jax.named_scope("attention"):
        qkv, vectors, out_all, lse, w_in = attend(at, w_own, w_other, toks, code_col, code_row)
        other_a, other_b = push(part_a, "core", 1), push(part_b, "core", 1)
        out_all, other_a, other_b = lax.optimization_barrier((out_all, other_a, other_b))
        context = lax.all_to_all(out_all, "group", 0, 0, tiled=True)
        ffb = vectors[8:12].reshape(4, 128, 8).transpose(1, 0, 2).reshape(1, 4096)

    with jax.named_scope("gather_ff"):
        far_a, far_b, context = lax.optimization_barrier((far_a, far_b, context))
        pieces_a = (part_a, far_a, other_a, push(far_a, "core", 1))
        pieces_b = (part_b, far_b, other_b, push(far_b, "core", 1))

    with jax.named_scope("tokens"):
        block_out, acts, d_one, d_context, small, d_ffb = token_layer(
            at, pieces_a, pieces_b, context, tokens, cotangent, vectors, ffb
        )

    with jax.named_scope("scatter_ff"):
        ffb_rows = d_ffb.reshape(128, 4, 8).transpose(1, 0, 2).reshape(4, 1024)
        small = jnp.concatenate([small, ffb_rows, jnp.zeros((4, 1024), F32)], axis=0)
        acts, other_acts, small = lax.optimization_barrier((acts, push(acts, "core", 1), small))
        keep_a, sent_a = wide_grads(at, acts, other_acts)
        got_a = swap(sent_a, "z", 0)
        keep_b, sent_b = down_grads(at, acts, other_acts)

    with jax.named_scope("attention_back"):
        d_all = lax.all_to_all(d_context, "group", 0, 0, tiled=True)
        d_all, sent_b = lax.optimization_barrier((d_all, sent_b))

    with jax.named_scope("scatter_ff"):
        terms_b, terms_a = [keep_b, swap(sent_b, "y", 0)], [keep_a, got_a]
        sent_b, sent_a = outgoing(terms_b), outgoing(terms_a)

    with jax.named_scope("attention_back"):
        keep_in, give_in, backs = attend_back(at, toks, w_in, qkv, d_all, code_col, code_row, lse, small)

    with jax.named_scope("scatter_attn_in"):
        give_in, sent_b, sent_a = lax.optimization_barrier((give_in, sent_b, sent_a))
        terms_in = [keep_in, push(give_in, "core", 1)]
        terms_in = step_down(terms_in, outgoing(terms_in), "y", 0)

    with jax.named_scope("input_grad"):
        backs = lax.all_to_all(backs, "group", 0, 0, tiled=True)

    with jax.named_scope("scatter_ff"):
        for axis_b, axis_a, axis_in, step in (("y", "z", "y", 1), ("z", "y", "z", 0), ("z", "y", "z", 1)):
            if axis_b == "z":
                sent_b, sent_a = outgoing(terms_b), outgoing(terms_a)
            terms_b, terms_a = step_down(terms_b, sent_b, axis_b, step), step_down(terms_a, sent_a, axis_a, step)
            terms_in = step_down(terms_in, outgoing(terms_in), axis_in, step)
        sum_b, sum_a, sum_in = (sum(term.astype(F32) for term in terms) for terms in (terms_b, terms_a, terms_in))
        sum_in = sum_in.reshape(4, 8, 896)
        pack = jnp.concatenate(
            [
                sum_a.reshape(5, 4, 8, 1024).transpose(1, 0, 2, 3).reshape(4, 40, 1024),
                sum_b.reshape(4, 32, 1024),
                jnp.concatenate([sum_in, jnp.zeros((4, 8, 128), F32)], axis=2),
            ],
            axis=1,
        )
        parts = [pick(pack, x_at, 0)]
        parts += [push(pick(pack, (x_at + 4 - j) % 4, 0).astype(BF16), "x", -j) for j in (1, 2, 3)]
        *grads, squares = finished(at, parts)

    with jax.named_scope("input_grad"):
        input_grad = d_one + jnp.sum(backs.astype(F32), axis=0)

    with jax.named_scope("norm"):
        squares = lax.all_to_all(squares, AXES, 0, 0, tiled=True)
        squares = jnp.sum(squares[:, :1, :1], axis=0)
    with jax.named_scope("lamb"):
        steps = lamb_steps(squares, shards, grads, firsts, seconds)

    def restored(arrays):
        return (*arrays[:4], arrays[4].T, arrays[5], arrays[6].reshape(32))

    return (block_out, input_grad, *restored(grads), *restored(steps))


def solution(mesh):
    rows, vector, docs = P(AXES, None), P(AXES), P("dp", None)
    leaves = (rows,) * 6 + (vector,)
    return jax.shard_map(
        body,
        mesh=mesh,
        in_specs=(rows, rows, docs) + leaves * 3,
        out_specs=(rows, rows) + leaves * 2,
        check_vma=False,
    )
```

```python
import jax
import jax.numpy as jnp
import numpy as np
from jax import lax
from jax.experimental import pallas as pl
from jax.experimental.pallas import tpu as pltpu
from jax.sharding import PartitionSpec as P

HEADS = 16
WINDOW = 1024
AXES = ("dp", "group")
RADIX = {"z": 4, "y": 4, "core": 2, "x": 4}

NORM_EPS = 1e-06
CLIP_NORM = 1.0
BETA_ONE = 0.9
BETA_TWO = 0.999
STEP_COUNT = 10
ADAM_EPS = 1e-06
WEIGHT_DECAY = 0.01
MASKED_SCORE = -1e30
F32 = jnp.float32
BF16 = jnp.bfloat16


def flat_of(at):
    return ((at["z"] * 4 + at["y"]) * 2 + at["core"]) * 4 + at["x"]


def device_pairs(move):
    out = []
    for flat in range(128):
        at = {"z": flat // 32, "y": flat // 8 % 4, "core": flat // 4 % 2, "x": flat % 4}
        move(at)
        out.append((flat, flat_of(at)))
    return out


def push(value, axis, shift):
    def move(at):
        at[axis] = (at[axis] + shift) % RADIX[axis]

    return lax.ppermute(value, AXES, device_pairs(move))


def swap(value, axis, step):
    def move(at):
        at[axis] ^= (1, 3)[(at["core"] + step) % 2]

    return lax.ppermute(value, AXES, device_pairs(move))


def spread(value, axes):
    names = ("z", "y", "core", "x")
    order = [name for name in names if name not in axes] + list(axes)
    grid = np.arange(128).reshape(4, 4, 2, 4).transpose([names.index(name) for name in order])
    groups = grid.reshape(-1, value.shape[0]).tolist()
    return lax.all_to_all(value, AXES, 0, 0, axis_index_groups=groups, tiled=True)


def pick(value, index, dim):
    return lax.dynamic_index_in_dim(value, index, dim, keepdims=False)


def rolled(parts, me, dim):
    joined = jnp.concatenate(parts + parts[:3], axis=dim)
    width = parts[0].shape[dim]
    return lax.dynamic_slice_in_dim(joined, (4 - me) % 4 * width, 4 * width, dim)


def doubled(value, axis, step):
    return jnp.concatenate([value, swap(value, axis, step)], axis=0)


def outgoing(terms):
    half = terms[0].shape[0] // 2
    return sum(term[half:].astype(F32) for term in terms).astype(BF16)


def step_down(terms, sent, axis, step):
    half = terms[0].shape[0] // 2
    terms = [term[:half] for term in terms] + [swap(sent, axis, step)]
    if half == 1:
        terms = [term[0] for term in terms]
    return terms


def masks(core, owner_is_other):
    one = core * 2 + 1
    two = 3 - core * 2
    return (two, one) if owner_is_other else (one, two)


def dot_nn(a, b):
    return jnp.dot(a, b, preferred_element_type=F32)


def dot_nt(a, b):
    return lax.dot_general(a, b, (((1,), (1,)), ((), ())), preferred_element_type=F32)


def dot_tn(a, b):
    return lax.dot_general(a, b, (((0,), (0,)), ((), ())), preferred_element_type=F32)


def xor2(me, bit_one, bit_two, pair):
    value = me
    if bit_one:
        value = value ^ pair[0]
    if bit_two:
        value = value ^ pair[1]
    return value


def unrolled(count):
    def run(part):
        for index in range(count):
            part(index)

    return run


def set_mask(mask_ref, col_ref, row_ref):
    @unrolled(8)
    def _(chunk):
        rows = slice(chunk * 128, chunk * 128 + 128)
        near = jnp.abs(col_ref[rows, :] - row_ref[...]) < WINDOW // 2
        mask_ref[rows, :] = jnp.where(near, 0.0, MASKED_SCORE)


def attend_kernel(
    at_ref, own_ref, other_ref, t0, t1, t2, t3, col_ref, row_ref,
    qkv_ref, vec_ref, out_ref, lse_ref, w_ref, mask_ref, turn_ref,
):
    z_at, y_at, core, x_at = at_ref[0], at_ref[1], at_ref[2], at_ref[3]
    for side, src in ((0, own_ref), (1, other_ref)):
        pair = masks(core, side == 1)
        for block in range(16):
            y = xor2(y_at, block & 1, block >> 1 & 1, pair)
            z = xor2(z_at, block >> 2 & 1, block >> 3 & 1, pair)
            row = pl.multiple_of(((z * 4 + y) * 2 + (core ^ side)) * 32, 32)
            w_ref[pl.ds(row, 32), :] = src[block]
    vec_ref[...] = w_ref[:, 768:896].astype(F32).T[:16]
    lanes = pl.ds(pl.multiple_of(x_at * 256, 256), 256)
    bias = jnp.concatenate([vec_ref[2:3, lanes], jnp.zeros((1, 256), F32), vec_ref[3:4, lanes]], axis=1)
    for j, tok in enumerate((t0, t1, t2, t3)):
        qkv_ref[j * 256 : j * 256 + 256, :] = (dot_nn(tok[...], w_ref[:, :768]) + bias).astype(BF16)
    set_mask(mask_ref, col_ref, row_ref)
    turn_ref[...] = qkv_ref[:, 512:768].T
    outs = []
    for head in range(4):
        lanes = slice(head * 64, head * 64 + 64)
        key = qkv_ref[:, 256 + head * 64 : 320 + head * 64]
        scores = dot_nt(key, qkv_ref[:, lanes] * BF16(0.125)) + mask_ref[...]
        top = jnp.max(scores, axis=0, keepdims=True)
        raised = jnp.exp(scores - top)
        total = jnp.sum(raised, axis=0, keepdims=True)
        probs = (raised * (1.0 / total)).astype(BF16)
        outs.append(dot_nn(turn_ref[lanes, :], probs))
        lse_ref[head : head + 1, :] = jnp.log(total) + top
    out = jnp.concatenate(outs, axis=0).T.astype(BF16)
    for block in range(4):
        out_ref[(x_at + block) % 4] = out[block * 256 : block * 256 + 256]


def attend_back_kernel(
    at_ref, t0, t1, t2, t3, w_src, qkv_ref, d_ref, col_ref, row_ref, lse_ref, small_ref,
    keep_ref, give_ref, back_ref, dqkv_ref, d_rows, rows_ref, mask_ref, turn_ref, joined_ref,
    tok_ref, w_ref, sem,
):
    z_at, y_at, core, x_at = at_ref[0], at_ref[1], at_ref[2], at_ref[3]
    copies = [pltpu.make_async_copy(src, tok_ref.at[i], sem.at[i]) for i, src in enumerate((t0, t1, t2, t3))]
    copies.append(pltpu.make_async_copy(w_src, w_ref, sem.at[4]))
    for copy in copies:
        copy.start()
    set_mask(mask_ref, col_ref, row_ref)
    turn_ref[...] = qkv_ref[:, 256:512].T
    for block in range(4):
        d_rows[block * 256 : block * 256 + 256, :] = d_ref[(x_at + block) % 4]
    outs = []
    for head in range(4):
        lanes = slice(head * 64, head * 64 + 64)
        key = qkv_ref[:, 256 + head * 64 : 320 + head * 64]
        value = qkv_ref[:, 512 + head * 64 : 576 + head * 64]
        query = qkv_ref[:, lanes] * BF16(0.125)
        d_out = d_rows[:, lanes]
        probs = jnp.exp(dot_nt(key, query) + mask_ref[...] - lse_ref[head : head + 1, :])
        d_probs = dot_nt(value, d_out)
        delta = jnp.sum(probs * d_probs, axis=0, keepdims=True)
        d_scores = (probs * (d_probs - delta)).astype(BF16)
        outs.append(dot_nn(turn_ref[lanes, :], d_scores) * 0.125)
        dqkv_ref[:, 256 + head * 64 : 320 + head * 64] = dot_nn(d_scores, query).astype(BF16)
        dqkv_ref[:, 512 + head * 64 : 576 + head * 64] = dot_nn(probs.astype(BF16), d_out).astype(BF16)
    dqkv_ref[:, :256] = jnp.concatenate(outs, axis=0).T.astype(BF16)
    rows_ref[...] = jnp.zeros_like(rows_ref)
    rows_ref[:16, :] = small_ref[...]
    lanes = pl.ds(pl.multiple_of(x_at * 256, 256), 256)
    sums = jnp.sum(dqkv_ref[...].astype(F32), axis=0, keepdims=True)
    rows_ref[2:3, lanes] = sums[:, :256]
    rows_ref[3:4, lanes] = sums[:, 512:]
    joined_ref[:, :, :, 768:896] = rows_ref[...].T.astype(BF16).reshape(16, 2, 32, 128)
    for copy in copies:
        copy.wait()
    total = dot_tn(tok_ref[0], dqkv_ref[:256, :])
    for block in (1, 2, 3):
        total = total + dot_tn(tok_ref[block], dqkv_ref[block * 256 : block * 256 + 256, :])
    joined_ref[:, :, :, :768] = total.astype(BF16).reshape(16, 2, 32, 768)
    for side, dst in ((0, keep_ref), (1, give_ref)):
        pair = masks(core, side == 1)
        for block in range(16):
            y = xor2(y_at, block >> 3 & 1, block >> 2 & 1, pair)
            z = xor2(z_at, block >> 1 & 1, block & 1, pair)
            dst[block] = joined_ref[z * 4 + y, core ^ side]
    for block in range(4):
        back = dot_nt(dqkv_ref[block * 256 : block * 256 + 256, :], w_ref[:, :768])
        back_ref[(x_at + block) % 4] = back.astype(BF16)


GELU_IN = 0.7978845608028654
GELU_CUBE = 0.044715


def norm_forward(value):
    center = value - jnp.mean(value, axis=-1, keepdims=True)
    spread = lax.rsqrt(jnp.mean(center * center, axis=-1, keepdims=True) + NORM_EPS)
    return center * spread, spread


def norm_back(d_normal, normal, spread):
    return spread * (
        d_normal
        - jnp.mean(d_normal, axis=-1, keepdims=True)
        - normal * jnp.mean(d_normal * normal, axis=-1, keepdims=True)
    )


def column_sum(value):
    return jnp.sum(value, axis=0, keepdims=True)


def token_kernel(
    at_ref, a0, a1, a2, a3, e0, e1, e2, e3, ctx_ref, tok_ref, cot_ref, vec_ref, ffb_ref,
    out_ref, acts_ref, done_ref, dctx_ref, small_ref, dffb_ref,
    w5, wd, hid, act, d_act, kept, hf, n_one, r_one, d_two, d_first, d_hid, sem,
):
    z_at, y_at, core = at_ref[0], at_ref[1], at_ref[2]
    pairs = [masks(core, False), masks(core, True)]
    for parts, slot in ((pl.ds(4, 1), 0), (pl.ds(0, 4), 5)):
        for late, side, src in ((0, 0, a0), (1, 0, a1), (0, 1, a2), (1, 1, a3)):
            for block in range(8):
                y = xor2(y_at, block >> 2 & 1, late, pairs[side])
                z = xor2(z_at, block & 1, block >> 1 & 1, pairs[side])
                row = pl.multiple_of(((z * 4 + y) * 2 + (core ^ side)) * 32, 32)
                pltpu.make_async_copy(src.at[block, parts], w5.at[parts, pl.ds(row, 32), :], sem.at[slot]).start()
    for late, side, src in ((0, 0, e0), (1, 0, e1), (0, 1, e2), (1, 1, e3)):
        for block in range(8):
            z = xor2(z_at, block >> 2 & 1, late, pairs[side])
            y = xor2(y_at, block & 1, block >> 1 & 1, pairs[side])
            row = pl.multiple_of(((z * 4 + y) * 2 + (core ^ side)) * 128, 128)
            pltpu.make_async_copy(src.at[block], wd.at[pl.ds(row, 128), :], sem.at[1]).start()

    def out_z(cb):
        return pltpu.make_async_copy(act.at[cb], acts_ref.at[cb], sem.at[2])

    def out_d(cb):
        return pltpu.make_async_copy(d_act.at[cb], acts_ref.at[4 + cb], sem.at[3])

    def out_kept(part):
        return pltpu.make_async_copy(kept.at[part], acts_ref.at[8 + part], sem.at[4])

    for part in range(4):
        kept[3, :, part * 256 : part * 256 + 256] = ctx_ref[part]
    out_kept(3).start()
    pltpu.make_async_copy(w5.at[pl.ds(4, 1)], w5.at[pl.ds(4, 1)], sem.at[0]).wait()
    attended = vec_ref[4:5, :]
    for part in range(4):
        attended = attended + dot_nn(ctx_ref[part], w5[4, part * 256 : part * 256 + 256, :])
    normal, spread = norm_forward(tok_ref[...].astype(F32) + attended)
    n_one[...] = normal
    r_one[...] = spread
    hf[...] = normal * vec_ref[0:1, :] + vec_ref[5:6, :]
    kept[2] = hf[...].astype(BF16)
    out_kept(2).start()
    pltpu.make_async_copy(w5.at[pl.ds(0, 4)], w5.at[pl.ds(0, 4)], sem.at[5]).wait()

    @unrolled(4)
    def _(cb):
        cols = slice(cb * 1024, cb * 1024 + 1024)
        hid[cb] = dot_nn(kept[2], w5[cb]) + ffb_ref[:, cols]

        @unrolled(8)
        def _(chunk):
            rows = slice(chunk * 32, chunk * 32 + 32)
            u = hid[cb, rows, :]
            t = jnp.tanh(GELU_IN * (u + GELU_CUBE * (u * u * u)))
            act[cb, rows, :] = (u * (0.5 * (1.0 + t))).astype(BF16)

        out_z(cb).start()

    pltpu.make_async_copy(wd, wd, sem.at[1]).wait()
    d_first[...] = hf[...] + vec_ref[6:7, :]

    @unrolled(4)
    def _(cb):
        d_first[...] += dot_nn(act[cb], wd[slice(cb * 1024, cb * 1024 + 1024), :])

    normal, spread = norm_forward(d_first[...])
    out_ref[...] = (normal * vec_ref[1:2, :] + vec_ref[7:8, :]).astype(BF16)
    cot = cot_ref[...].astype(F32)
    small_ref[...] = jnp.zeros_like(small_ref)
    small_ref[1:2, :] = column_sum(cot * normal)
    small_ref[7:8, :] = column_sum(cot)
    d_two[...] = norm_back(cot * vec_ref[1:2, :], normal, spread)
    kept[1] = d_two[...].astype(BF16)
    out_kept(1).start()
    small_ref[6:7, :] = column_sum(kept[1].astype(F32))
    d_first[...] = d_two[...]

    @unrolled(4)
    def _(cb):
        cols = slice(cb * 1024, cb * 1024 + 1024)
        d_hid[...] = dot_nt(kept[1], wd[cols, :])
        dffb_ref[:, cols] = jnp.zeros((1, 1024), F32)

        @unrolled(8)
        def _(chunk):
            rows = slice(chunk * 32, chunk * 32 + 32)
            u = hid[cb, rows, :]
            square = u * u
            t = jnp.tanh(GELU_IN * (u + GELU_CUBE * (square * u)))
            slope = 0.5 * (1.0 + t) + (0.5 * GELU_IN) * u * (1.0 - t * t) * (1.0 + (3.0 * GELU_CUBE) * square)
            d_low = (d_hid[rows, :] * slope).astype(BF16)
            d_act[cb, rows, :] = d_low
            dffb_ref[:, cols] += column_sum(d_low.astype(F32))

        out_d(cb).start()
        d_first[...] += dot_nt(d_act[cb], w5[cb])

    d_h = d_first[...]
    normal = n_one[...]
    small_ref[0:1, :] = column_sum(d_h * normal)
    small_ref[5:6, :] = column_sum(d_h)
    d_one = norm_back(d_h * vec_ref[0:1, :], normal, r_one[...])
    done_ref[...] = d_one
    kept[0] = d_one.astype(BF16)
    out_kept(0).start()
    small_ref[4:5, :] = column_sum(kept[0].astype(F32))
    for part in range(4):
        dctx_ref[part] = dot_nt(kept[0], w5[4, part * 256 : part * 256 + 256, :]).astype(BF16)
    for cb in range(4):
        out_z(cb).wait()
        out_d(cb).wait()
        out_kept(cb).wait()


def wide_kernel(at_ref, own_ref, oth_ref, a0_ref, a1_ref, acts, left, turn, stage, sem):
    z_at, y_at, core = at_ref[0], at_ref[1], at_ref[2]
    pair = masks(core, False)

    def load(slot, index):
        return [pltpu.make_async_copy(src.at[index], acts.at[slot, side], sem.at[slot, side]) for side, src in ((0, own_ref), (1, oth_ref))]

    order = (10, 4, 5, 6, 7, 11, 8)
    for slot, index in enumerate(order):
        for copy in load(slot, index):
            copy.start()

    def wait(slot):
        for copy in load(slot, order[slot]):
            copy.wait()

    def rows_of(slot):
        wait(slot)
        for half in range(2):
            turn[...] = acts[slot, half].T
            for block in range(16):
                z = xor2(z_at, block >> 3 & 1, block >> 2 & 1, pair)
                y = xor2(y_at, block >> 1 & 1, block & 1, pair)
                row = pl.multiple_of(((z * 4 + y) * 2 + core) * 32, 32)
                left[slot // 5, block * 32 : block * 32 + 32, half * 256 : half * 256 + 256] = turn[pl.ds(row, 32), :]

    def out(part):
        return [
            pltpu.make_async_copy(stage.at[part, pl.ds(half * 8, 8)], dst.at[:, part], sem.at[7 + part, half])
            for half, dst in ((0, a0_ref), (1, a1_ref))
        ]

    rows_of(0)
    for part in range(5):
        if part == 4:
            rows_of(5)
        wait(1 + part + part // 4)
        slot = 1 + part + part // 4
        right = acts[slot].reshape(512, 1024)
        stage[part] = dot_nn(left[part // 4], right).astype(BF16).reshape(16, 32, 1024)
        for copy in out(part):
            copy.start()
    for part in range(5):
        for copy in out(part):
            copy.wait()


def down_kernel(at_ref, own_ref, oth_ref, b0_ref, b1_ref, acts, picked, stage, sem):
    z_at, y_at, core = at_ref[0], at_ref[1], at_ref[2]
    pair = masks(core, False)

    order = (9, 0, 1, 2, 3)

    def load(slot):
        return [
            pltpu.make_async_copy(src.at[order[slot]], acts.at[slot, side], sem.at[slot, side])
            for side, src in ((0, own_ref), (1, oth_ref))
        ]

    for slot in range(5):
        for copy in load(slot):
            copy.start()

    def place(z):
        one, two = pair
        gap = z ^ z_at
        both = (gap == 2).astype(jnp.int32)
        return ((gap == one).astype(jnp.int32) + both) * 2 + (gap == two).astype(jnp.int32) + both

    def out(z):
        return [
            pltpu.make_async_copy(stage.at[z, pl.ds(half * 2, 2)], dst.at[:, place(z)], sem.at[5 + z, half])
            for half, dst in ((0, b0_ref), (1, b1_ref))
        ]

    for copy in load(0):
        copy.wait()
    for z in range(4):
        for copy in load(1 + z):
            copy.wait()
        for half in range(2):
            for block in range(4):
                y = xor2(y_at, block >> 1, block & 1, pair)
                lanes = pl.ds(pl.multiple_of((y * 2 + core) * 128, 128), 128)
                picked[z, half, :, block * 128 : block * 128 + 128] = acts[1 + z, half, :, lanes]
        grad = dot_tn(picked[z].reshape(512, 512), acts[0].reshape(512, 1024))
        stage[z] = grad.astype(BF16).reshape(4, 128, 1024)
        for copy in out(z):
            copy.start()
    for z in range(4):
        for copy in out(z):
            copy.wait()


SMEM = pl.BlockSpec(memory_space=pltpu.SMEM)
VMEM = pl.BlockSpec(memory_space=pltpu.VMEM)
ANY = pl.BlockSpec(memory_space=pl.ANY)
MIB = 2**20


def pack_kernel(up_ref, out_ref, down_ref, in_ref, gains_ref, bias_ref, ffb_ref, pack_ref, rows, square):
    for cb in range(4):
        rows[cb * 8 : cb * 8 + 8, :] = up_ref[:, cb * 1024 : cb * 1024 + 1024]
    rows[32:40, :] = out_ref[...]
    rows[40:72, :] = down_ref[...]
    for cb in range(3):
        rows[72 + cb * 8 : 80 + cb * 8, :] = in_ref[:, cb * 1024 : cb * 1024 + 1024]
    square[...] = jnp.zeros_like(square)
    square[0:2, :8] = gains_ref[...]
    for j in range(4):
        square[8 + j : 9 + j, :8] = ffb_ref[:, j * 8 : j * 8 + 8]
    rows[96:104, :] = jnp.zeros((8, 1024), F32)
    rows[96:104, :128] = square[...].T[:8]
    rows[96:104, 2:8] = bias_ref[...]
    pack_ref[...] = rows[...].astype(BF16)


def packed_rows(arrays):
    return pl.pallas_call(
        pack_kernel,
        in_specs=[VMEM] * 7,
        out_specs=VMEM,
        out_shape=jax.ShapeDtypeStruct((104, 1024), BF16),
        scratch_shapes=[pltpu.VMEM((104, 1024), F32), pltpu.VMEM((128, 128), F32)],
        name="pack_rows",
    )(arrays[2], arrays[1], arrays[3], arrays[0], *arrays[4:])


def finish_kernel(at_ref, p0, p1, p2, p3, in_ref, out_ref, up_ref, down_ref, gains_ref, bias_ref, ffb_ref, sq_ref, square):
    x_at = at_ref[3]
    parts = [ref[...].astype(F32) for ref in (p0, p1, p2, p3)]
    total = parts[0][:72] + parts[1][:72] + parts[2][:72] + parts[3][:72]
    for cb in range(4):
        up_ref[:, cb * 1024 : cb * 1024 + 1024] = total[cb * 8 : cb * 8 + 8]
    out_ref[...] = total[32:40]
    down_ref[...] = total[40:72]
    extra = jnp.zeros((8, 128), F32)
    squares = jnp.sum(total * total, keepdims=True)
    for j, part in enumerate(parts):
        rows = part[72:80]
        group = (x_at + j) % 4
        for block in range(3):
            cols = pl.ds(pl.multiple_of(block * 1024 + group * 256, 256), 256)
            in_ref[:, cols] = rows[:, block * 256 : block * 256 + 256]
        squares = squares + jnp.sum(rows[:, :768] * rows[:, :768], keepdims=True)
        extra = extra + rows[:, 768:896]
    square[...] = jnp.zeros_like(square)
    square[:8, :] = extra
    turned = square[...].T
    gains_ref[...] = turned[0:2, :8]
    bias_ref[...] = extra[:, 2:8]
    for j in range(4):
        ffb_ref[:, j * 8 : j * 8 + 8] = turned[8 + j : 9 + j, :8]
    squares = squares + jnp.sum(turned[:12] * turned[:12], keepdims=True)
    sq_ref[...] = jnp.broadcast_to(squares, sq_ref.shape)


def finished(at, parts):
    shapes = [(8, 3072), (8, 1024), (8, 4096), (32, 1024), (2, 8), (8, 6), (1, 32), (1, 128)]
    return pl.pallas_call(
        finish_kernel,
        in_specs=[SMEM] + [VMEM] * 4,
        out_specs=[VMEM] * 8,
        out_shape=[jax.ShapeDtypeStruct(shape, F32) for shape in shapes],
        scratch_shapes=[pltpu.VMEM((128, 128), F32)],
        name="finish",
    )(at, *parts)


def attend(at, w_own, w_other, toks, code_col, code_row):
    return pl.pallas_call(
        attend_kernel,
        in_specs=[SMEM] + [VMEM] * 8,
        out_specs=[VMEM] * 5,
        out_shape=[
            jax.ShapeDtypeStruct((1024, 768), BF16),
            jax.ShapeDtypeStruct((16, 1024), F32),
            jax.ShapeDtypeStruct((4, 256, 256), BF16),
            jax.ShapeDtypeStruct((4, 1024), F32),
            jax.ShapeDtypeStruct((1024, 1024), BF16),
        ],
        scratch_shapes=[
            pltpu.VMEM((1024, 1024), F32),
            pltpu.VMEM((256, 1024), BF16),
        ],
        compiler_params=pltpu.CompilerParams(vmem_limit_bytes=56 * MIB),
        cost_estimate=pl.CostEstimate(flops=13 * 10**9, bytes_accessed=9 * MIB, transcendentals=4 * MIB),
        name="attend",
    )(at, w_own, w_other, *toks, code_col, code_row)


def attend_back(at, toks, w_in, qkv, d_all, code_col, code_row, lse, small):
    return pl.pallas_call(
        attend_back_kernel,
        in_specs=[SMEM] + [ANY] * 5 + [VMEM] * 6,
        out_specs=[VMEM] * 3,
        out_shape=[jax.ShapeDtypeStruct((16, 32, 896), BF16)] * 2 + [jax.ShapeDtypeStruct((4, 256, 1024), BF16)],
        scratch_shapes=[
            pltpu.VMEM((1024, 768), BF16),
            pltpu.VMEM((1024, 256), BF16),
            pltpu.VMEM((128, 1024), F32),
            pltpu.VMEM((1024, 1024), F32),
            pltpu.VMEM((256, 1024), BF16),
            pltpu.VMEM((16, 2, 32, 896), BF16),
            pltpu.VMEM((4, 256, 1024), BF16),
            pltpu.VMEM((1024, 1024), BF16),
            pltpu.SemaphoreType.DMA((5,)),
        ],
        compiler_params=pltpu.CompilerParams(vmem_limit_bytes=56 * MIB),
        cost_estimate=pl.CostEstimate(flops=22 * 10**9, bytes_accessed=14 * MIB, transcendentals=4 * MIB),
        name="attend_back",
    )(at, *toks, w_in, qkv, d_all, code_col, code_row, lse, small)


def wide_grads(at, own, other):
    return pl.pallas_call(
        wide_kernel,
        in_specs=[SMEM, ANY, ANY],
        out_specs=[ANY, ANY],
        out_shape=[pltpu.HBM((8, 5, 32, 1024), BF16)] * 2,
        scratch_shapes=[
            pltpu.VMEM((7, 2, 256, 1024), BF16),
            pltpu.VMEM((2, 512, 512), BF16),
            pltpu.VMEM((1024, 256), BF16),
            pltpu.VMEM((5, 16, 32, 1024), BF16),
            pltpu.SemaphoreType.DMA((12, 2)),
        ],
        compiler_params=pltpu.CompilerParams(vmem_limit_bytes=56 * MIB),
        cost_estimate=pl.CostEstimate(flops=3 * 10**9, bytes_accessed=12 * MIB, transcendentals=0),
        name="wide_grads",
    )(at, own, other)


def down_grads(at, own, other):
    return pl.pallas_call(
        down_kernel,
        in_specs=[SMEM, ANY, ANY],
        out_specs=[ANY, ANY],
        out_shape=[pltpu.HBM((2, 4, 128, 1024), BF16)] * 2,
        scratch_shapes=[
            pltpu.VMEM((5, 2, 256, 1024), BF16),
            pltpu.VMEM((4, 2, 256, 512), BF16),
            pltpu.VMEM((4, 4, 128, 1024), BF16),
            pltpu.SemaphoreType.DMA((9, 2)),
        ],
        compiler_params=pltpu.CompilerParams(vmem_limit_bytes=56 * MIB),
        cost_estimate=pl.CostEstimate(flops=3 * 10**9, bytes_accessed=10 * MIB, transcendentals=0),
        name="down_grads",
    )(at, own, other)


def token_layer(at, pieces_a, pieces_b, context, tokens, cotangent, vectors, ffb):
    return pl.pallas_call(
        token_kernel,
        in_specs=[SMEM] + [ANY] * 8 + [VMEM] * 5,
        out_specs=[VMEM, ANY] + [VMEM] * 4,
        out_shape=[
            jax.ShapeDtypeStruct((256, 1024), BF16),
            jax.ShapeDtypeStruct((12, 256, 1024), BF16),
            jax.ShapeDtypeStruct((256, 1024), F32),
            jax.ShapeDtypeStruct((4, 256, 256), BF16),
            jax.ShapeDtypeStruct((8, 1024), F32),
            jax.ShapeDtypeStruct((1, 4096), F32),
        ],
        scratch_shapes=[
            pltpu.VMEM((5, 1024, 1024), BF16),
            pltpu.VMEM((4096, 1024), BF16),
            pltpu.VMEM((4, 256, 1024), F32),
            pltpu.VMEM((4, 256, 1024), BF16),
            pltpu.VMEM((4, 256, 1024), BF16),
            pltpu.VMEM((4, 256, 1024), BF16),
            pltpu.VMEM((256, 1024), F32),
            pltpu.VMEM((256, 1024), F32),
            pltpu.VMEM((256, 1), F32),
            pltpu.VMEM((256, 1024), F32),
            pltpu.VMEM((256, 1024), F32),
            pltpu.VMEM((256, 1024), F32),
            pltpu.SemaphoreType.DMA((6,)),
        ],
        compiler_params=pltpu.CompilerParams(vmem_limit_bytes=60 * MIB),
        cost_estimate=pl.CostEstimate(flops=10 * 10**9, bytes_accessed=30 * MIB, transcendentals=2 * MIB),
        name="token_layer",
    )(at, *pieces_a, *pieces_b, context, tokens, cotangent, vectors, ffb)


def lamb_kernel(squares_ref, *refs):
    factor = CLIP_NORM / jnp.maximum(jnp.sqrt(squares_ref[...]), CLIP_NORM)
    for i in range(7):
        weight, grad = refs[i][...], refs[7 + i][...] * factor
        new_first = BETA_ONE * refs[14 + i][...] + (1.0 - BETA_ONE) * grad
        new_second = BETA_TWO * refs[21 + i][...] + (1.0 - BETA_TWO) * grad * grad
        direction = (
            new_first
            / (1.0 - BETA_ONE**STEP_COUNT)
            / (jnp.sqrt(new_second / (1.0 - BETA_TWO**STEP_COUNT)) + ADAM_EPS)
            + WEIGHT_DECAY * weight
        )
        weight_norm = jnp.sqrt(jnp.sum(weight * weight, keepdims=True))
        dir_norm = jnp.sqrt(jnp.sum(direction * direction, keepdims=True))
        refs[28 + i][...] = direction * (weight_norm / jnp.maximum(dir_norm, 1.0))


def lamb_steps(squares, weights, grads, firsts, seconds):
    return pl.pallas_call(
        lamb_kernel,
        in_specs=[VMEM] * 29,
        out_specs=[VMEM] * 7,
        out_shape=[jax.ShapeDtypeStruct(weight.shape, F32) for weight in weights],
        name="lamb",
    )(squares, *weights, *grads, *firsts, *seconds)


def body(tokens, cotangent, doc_lengths, *params):

    def turned(arrays):
        return (*arrays[:4], arrays[4].T, arrays[5], arrays[6].reshape(1, 32))

    shards, firsts, seconds = turned(params[:7]), turned(params[7:14]), turned(params[14:])
    dp_index = lax.axis_index("dp")
    z_at, y_at, core, x_at = dp_index // 8, dp_index // 2 % 4, dp_index % 2, lax.axis_index("group")
    at = jnp.stack([z_at, y_at, core, x_at]).astype(jnp.int32)

    with jax.named_scope("gather_x"):
        pack = packed_rows(shards)
        pack = rolled([pack[None]] + [push(pack, "x", -j)[None] for j in (1, 2, 3)], x_at, 0)
        own = lax.dynamic_slice_in_dim(pack[:, 72:96], x_at * 256, 256, axis=2)
        own = own.reshape(4, 3, 8, 256).transpose(0, 2, 1, 3).reshape(4, 8, 768)
        own = jnp.concatenate([own, pack[:, 96:, :256]], axis=2)
        part_a = pack[:, :40].reshape(4, 5, 8, 1024).transpose(1, 0, 2, 3).reshape(1, 5, 32, 1024)
        part_b = jnp.concatenate([pack[:, 40:72].reshape(1, 4, 32, 1024), own.reshape(1, 1, 32, 1024)], axis=1)

    with jax.named_scope("gather_tokens"):
        toks = [tokens, push(tokens, "x", -1), tokens, push(tokens, "x", -3)]

    with jax.named_scope("visible"):
        order = (x_at + jnp.arange(4, dtype=jnp.int32)) % 4
        positions = (order[:, None] * 256 + jnp.arange(256, dtype=jnp.int32)[None]).reshape(1024)
        ends = [doc_lengths[0, 0], doc_lengths[0, 0] + doc_lengths[0, 1]]
        ends.append(ends[1] + doc_lengths[0, 2])
        ids = sum((positions >= end).astype(jnp.int32) for end in ends)
        code = (positions + 4096 * ids).astype(F32)
        code_col, code_row = code[:, None], code[None]

    with jax.named_scope("gather_yz"):
        part_a, part_b = doubled(part_a, "z", 0), doubled(part_b, "y", 0)
        part_a, part_b = doubled(part_a, "z", 1), doubled(part_b, "y", 1)
        part_a, part_b, *toks = lax.optimization_barrier((part_a, part_b, *toks))
        toks[2] = push(toks[2], "x", -2)
        part_b, w_own = part_b[:, :4].reshape(4, 128, 1024), part_b[:, 4]
        w_own = doubled(w_own, "z", 0)
        part_a, part_b, at, code_col, code_row = lax.optimization_barrier((part_a, part_b, at, code_col, code_row))
        w_own = doubled(w_own, "z", 1)
        part_a, part_b = doubled(part_a, "y", 0), doubled(part_b, "z", 0)
        part_a, part_b, w_own, toks[2] = lax.optimization_barrier((part_a, part_b, w_own, toks[2]))
        w_other = push(w_own, "core", 1)
        far_a, far_b = swap(part_a, "y", 1), swap(part_b, "z", 1)

    with jax.named_scope("attention"):
        qkv, vectors, out_all, lse, w_in = attend(at, w_own, w_other, toks, code_col, code_row)
        part_a, part_b, out_all = lax.optimization_barrier((part_a, part_b, out_all))
        other_a, other_b = push(part_a, "core", 1), push(part_b, "core", 1)
        context = lax.all_to_all(out_all, "group", 0, 0, tiled=True)
        ffb = vectors[8:12].reshape(4, 128, 8).transpose(1, 0, 2).reshape(1, 4096)

    with jax.named_scope("gather_ff"):
        far_a, far_b, context = lax.optimization_barrier((far_a, far_b, context))
        pieces_a = (part_a, far_a, other_a, push(far_a, "core", 1))
        pieces_b = (part_b, far_b, other_b, push(far_b, "core", 1))

    with jax.named_scope("tokens"):
        block_out, acts, d_one, d_context, small, d_ffb = token_layer(
            at, pieces_a, pieces_b, context, tokens, cotangent, vectors, ffb
        )

    with jax.named_scope("scatter_ff"):
        ffb_rows = d_ffb.reshape(128, 4, 8).transpose(1, 0, 2).reshape(4, 1024)
        small = jnp.concatenate([small, ffb_rows, jnp.zeros((4, 1024), F32)], axis=0)
        acts, other_acts, small = lax.optimization_barrier((acts, push(acts, "core", 1), small))
        keep_a, sent_a = wide_grads(at, acts, other_acts)
        got_a = swap(sent_a, "z", 0)
        keep_b, sent_b = down_grads(at, acts, other_acts)

    with jax.named_scope("attention_back"):
        d_all = lax.all_to_all(d_context, "group", 0, 0, tiled=True)
        d_all, sent_b = lax.optimization_barrier((d_all, sent_b))

    with jax.named_scope("scatter_ff"):
        terms_b, terms_a = [keep_b, swap(sent_b, "y", 0)], [keep_a, got_a]
        sent_b, sent_a = outgoing(terms_b), outgoing(terms_a)

    with jax.named_scope("attention_back"):
        keep_in, give_in, backs = attend_back(at, toks, w_in, qkv, d_all, code_col, code_row, lse, small)

    with jax.named_scope("scatter_attn_in"):
        terms_in = [keep_in, push(give_in, "core", 1)]
        terms_in = step_down(terms_in, outgoing(terms_in), "y", 0)

    with jax.named_scope("input_grad"):
        backs = lax.all_to_all(backs, "group", 0, 0, tiled=True)

    with jax.named_scope("scatter_ff"):
        for axis_b, axis_a, axis_in, step in (("y", "z", "y", 1), ("z", "y", "z", 0), ("z", "y", "z", 1)):
            if axis_b == "z":
                terms_b, terms_a, terms_in = lax.optimization_barrier((terms_b, terms_a, terms_in))
                sent_b, sent_a = outgoing(terms_b), outgoing(terms_a)
            terms_b, terms_a = step_down(terms_b, sent_b, axis_b, step), step_down(terms_a, sent_a, axis_a, step)
            terms_in = step_down(terms_in, outgoing(terms_in), axis_in, step)
        sum_b, sum_a, sum_in = (sum(term.astype(F32) for term in terms) for terms in (terms_b, terms_a, terms_in))
        sum_in = sum_in.reshape(4, 8, 896)
        pack = jnp.concatenate(
            [
                sum_a.reshape(5, 4, 8, 1024).transpose(1, 0, 2, 3).reshape(4, 40, 1024),
                sum_b.reshape(4, 32, 1024),
                jnp.concatenate([sum_in, jnp.zeros((4, 8, 128), F32)], axis=2),
            ],
            axis=1,
        )
        parts = [pick(pack, x_at, 0)]
        parts += [push(pick(pack, (x_at + 4 - j) % 4, 0).astype(BF16), "x", -j) for j in (1, 2, 3)]
        *grads, squares = finished(at, parts)

    with jax.named_scope("input_grad"):
        input_grad = d_one + jnp.sum(backs.astype(F32), axis=0)

    with jax.named_scope("norm"):
        squares = lax.all_to_all(jnp.broadcast_to(squares[None], (128, 1, 128)), AXES, 0, 0, tiled=True)
        squares = jnp.sum(squares[:, :, :1], axis=0)
    with jax.named_scope("lamb"):
        steps = lamb_steps(squares, shards, grads, firsts, seconds)

    def restored(arrays):
        return (*arrays[:4], arrays[4].T, arrays[5], arrays[6].reshape(32))

    return (block_out, input_grad, *restored(grads), *restored(steps))


def solution(mesh):
    rows, vector, docs = P(AXES, None), P(AXES), P("dp", None)
    leaves = (rows,) * 6 + (vector,)
    return jax.shard_map(
        body,
        mesh=mesh,
        in_specs=(rows, rows, docs) + leaves * 3,
        out_specs=(rows, rows) + leaves * 2,
        check_vma=False,
    )
```

```python
import jax
import jax.numpy as jnp
import numpy as np
from jax import lax
from jax.experimental import pallas as pl
from jax.experimental.pallas import tpu as pltpu
from jax.sharding import PartitionSpec as P

HEADS = 16
WINDOW = 1024
AXES = ("dp", "group")
RADIX = {"z": 4, "y": 4, "core": 2, "x": 4}

NORM_EPS = 1e-06
CLIP_NORM = 1.0
BETA_ONE = 0.9
BETA_TWO = 0.999
STEP_COUNT = 10
ADAM_EPS = 1e-06
WEIGHT_DECAY = 0.01
MASKED_SCORE = -1e30
F32 = jnp.float32
BF16 = jnp.bfloat16


def flat_of(at):
    return ((at["z"] * 4 + at["y"]) * 2 + at["core"]) * 4 + at["x"]


def device_pairs(move):
    out = []
    for flat in range(128):
        at = {"z": flat // 32, "y": flat // 8 % 4, "core": flat // 4 % 2, "x": flat % 4}
        move(at)
        out.append((flat, flat_of(at)))
    return out


def push(value, axis, shift):
    def move(at):
        at[axis] = (at[axis] + shift) % RADIX[axis]

    return lax.ppermute(value, AXES, device_pairs(move))


def swap(value, axis, step):
    def move(at):
        at[axis] ^= (1, 3)[(at["core"] + step) % 2]

    return lax.ppermute(value, AXES, device_pairs(move))


def spread(value, axes):
    names = ("z", "y", "core", "x")
    order = [name for name in names if name not in axes] + list(axes)
    grid = np.arange(128).reshape(4, 4, 2, 4).transpose([names.index(name) for name in order])
    groups = grid.reshape(-1, value.shape[0]).tolist()
    return lax.all_to_all(value, AXES, 0, 0, axis_index_groups=groups, tiled=True)


def pick(value, index, dim):
    return lax.dynamic_index_in_dim(value, index, dim, keepdims=False)


def rolled(parts, me, dim):
    joined = jnp.concatenate(parts + parts[:3], axis=dim)
    width = parts[0].shape[dim]
    return lax.dynamic_slice_in_dim(joined, (4 - me) % 4 * width, 4 * width, dim)


def doubled(value, axis, step):
    return jnp.concatenate([value, swap(value, axis, step)], axis=0)


def outgoing(terms):
    half = terms[0].shape[0] // 2
    return sum(term[half:].astype(F32) for term in terms).astype(BF16)


def step_down(terms, sent, axis, step):
    half = terms[0].shape[0] // 2
    terms = [term[:half] for term in terms] + [swap(sent, axis, step)]
    if half == 1:
        terms = [term[0] for term in terms]
    return terms


def masks(core, owner_is_other):
    one = core * 2 + 1
    two = 3 - core * 2
    return (two, one) if owner_is_other else (one, two)


def dot_nn(a, b):
    return jnp.dot(a, b, preferred_element_type=F32)


def dot_nt(a, b):
    return lax.dot_general(a, b, (((1,), (1,)), ((), ())), preferred_element_type=F32)


def dot_tn(a, b):
    return lax.dot_general(a, b, (((0,), (0,)), ((), ())), preferred_element_type=F32)


def xor2(me, bit_one, bit_two, pair):
    value = me
    if bit_one:
        value = value ^ pair[0]
    if bit_two:
        value = value ^ pair[1]
    return value


def unrolled(count):
    def run(part):
        for index in range(count):
            part(index)

    return run


def set_mask(mask_ref, col_ref, row_ref):
    @unrolled(8)
    def _(chunk):
        rows = slice(chunk * 128, chunk * 128 + 128)
        near = jnp.abs(col_ref[rows, :] - row_ref[...]) < WINDOW // 2
        mask_ref[rows, :] = jnp.where(near, 0.0, MASKED_SCORE)


def attend_kernel(
    at_ref, own_ref, other_ref, t0, t1, t2, t3, col_ref, row_ref,
    qkv_ref, vec_ref, out_ref, lse_ref, w_ref, mask_ref, turn_ref,
):
    z_at, y_at, core, x_at = at_ref[0], at_ref[1], at_ref[2], at_ref[3]
    for side, src in ((0, own_ref), (1, other_ref)):
        pair = masks(core, side == 1)
        for block in range(16):
            y = xor2(y_at, block & 1, block >> 1 & 1, pair)
            z = xor2(z_at, block >> 2 & 1, block >> 3 & 1, pair)
            row = pl.multiple_of(((z * 4 + y) * 2 + (core ^ side)) * 32, 32)
            w_ref[pl.ds(row, 32), :] = src[block]
    vec_ref[...] = w_ref[:, 768:896].astype(F32).T[:16]
    lanes = pl.ds(pl.multiple_of(x_at * 256, 256), 256)
    bias = jnp.concatenate([vec_ref[2:3, lanes], jnp.zeros((1, 256), F32), vec_ref[3:4, lanes]], axis=1)
    for j, tok in enumerate((t0, t1, t2, t3)):
        qkv_ref[j * 256 : j * 256 + 256, :] = (dot_nn(tok[...], w_ref[:, :768]) + bias).astype(BF16)
    set_mask(mask_ref, col_ref, row_ref)
    turn_ref[...] = qkv_ref[:, 512:768].T
    outs = []
    for head in range(4):
        lanes = slice(head * 64, head * 64 + 64)
        key = qkv_ref[:, 256 + head * 64 : 320 + head * 64]
        scores = dot_nt(key, qkv_ref[:, lanes] * BF16(0.125)) + mask_ref[...]
        top = jnp.max(scores, axis=0, keepdims=True)
        raised = jnp.exp(scores - top)
        total = jnp.sum(raised, axis=0, keepdims=True)
        probs = (raised * (1.0 / total)).astype(BF16)
        outs.append(dot_nn(turn_ref[lanes, :], probs))
        lse_ref[head : head + 1, :] = jnp.log(total) + top
    out = jnp.concatenate(outs, axis=0).T.astype(BF16)
    for block in range(4):
        out_ref[(x_at + block) % 4] = out[block * 256 : block * 256 + 256]


def attend_back_kernel(
    at_ref, t0, t1, t2, t3, qkv_ref, d_ref, col_ref, row_ref, lse_ref, small_ref,
    keep_ref, give_ref, dqkv_ref, d_rows, rows_ref, mask_ref, turn_ref, joined_ref, tok_ref, sem,
):
    z_at, y_at, core, x_at = at_ref[0], at_ref[1], at_ref[2], at_ref[3]
    copies = [pltpu.make_async_copy(src, tok_ref.at[i], sem.at[i]) for i, src in enumerate((t0, t1, t2, t3))]
    for copy in copies:
        copy.start()
    set_mask(mask_ref, col_ref, row_ref)
    turn_ref[...] = qkv_ref[:, 256:512].T
    for block in range(4):
        d_rows[block * 256 : block * 256 + 256, :] = d_ref[(x_at + block) % 4]
    outs = []
    for head in range(4):
        lanes = slice(head * 64, head * 64 + 64)
        key = qkv_ref[:, 256 + head * 64 : 320 + head * 64]
        value = qkv_ref[:, 512 + head * 64 : 576 + head * 64]
        query = qkv_ref[:, lanes] * BF16(0.125)
        d_out = d_rows[:, lanes]
        probs = jnp.exp(dot_nt(key, query) + mask_ref[...] - lse_ref[head : head + 1, :])
        d_probs = dot_nt(value, d_out)
        delta = jnp.sum(probs * d_probs, axis=0, keepdims=True)
        d_scores = (probs * (d_probs - delta)).astype(BF16)
        outs.append(dot_nn(turn_ref[lanes, :], d_scores) * 0.125)
        dqkv_ref[:, 256 + head * 64 : 320 + head * 64] = dot_nn(d_scores, query).astype(BF16)
        dqkv_ref[:, 512 + head * 64 : 576 + head * 64] = dot_nn(probs.astype(BF16), d_out).astype(BF16)
    dqkv_ref[:, :256] = jnp.concatenate(outs, axis=0).T.astype(BF16)
    rows_ref[...] = jnp.zeros_like(rows_ref)
    rows_ref[:16, :] = small_ref[...]
    lanes = pl.ds(pl.multiple_of(x_at * 256, 256), 256)
    sums = jnp.sum(dqkv_ref[...].astype(F32), axis=0, keepdims=True)
    rows_ref[2:3, lanes] = sums[:, :256]
    rows_ref[3:4, lanes] = sums[:, 512:]
    joined_ref[:, :, :, 768:896] = rows_ref[...].T.astype(BF16).reshape(16, 2, 32, 128)
    for copy in copies:
        copy.wait()
    total = dot_tn(tok_ref[0], dqkv_ref[:256, :])
    for block in (1, 2, 3):
        total = total + dot_tn(tok_ref[block], dqkv_ref[block * 256 : block * 256 + 256, :])
    joined_ref[:, :, :, :768] = total.astype(BF16).reshape(16, 2, 32, 768)
    for side, dst in ((0, keep_ref), (1, give_ref)):
        pair = masks(core, side == 1)
        for block in range(16):
            y = xor2(y_at, block >> 3 & 1, block >> 2 & 1, pair)
            z = xor2(z_at, block >> 1 & 1, block & 1, pair)
            dst[block] = joined_ref[z * 4 + y, core ^ side]


def back_kernel(at_ref, dqkv_ref, w_ref, back_ref):
    x_at = at_ref[3]
    for block in range(4):
        back = dot_nt(dqkv_ref[block * 256 : block * 256 + 256, :], w_ref[:, :768])
        back_ref[(x_at + block) % 4] = back.astype(BF16)


GELU_IN = 0.7978845608028654
GELU_CUBE = 0.044715


def norm_forward(value):
    center = value - jnp.mean(value, axis=-1, keepdims=True)
    spread = lax.rsqrt(jnp.mean(center * center, axis=-1, keepdims=True) + NORM_EPS)
    return center * spread, spread


def norm_back(d_normal, normal, spread):
    return spread * (
        d_normal
        - jnp.mean(d_normal, axis=-1, keepdims=True)
        - normal * jnp.mean(d_normal * normal, axis=-1, keepdims=True)
    )


def column_sum(value):
    return jnp.sum(value, axis=0, keepdims=True)


def token_kernel(
    at_ref, a0, a1, a2, a3, e0, e1, e2, e3, ctx_ref, tok_ref, cot_ref, vec_ref, ffb_ref,
    out_ref, dx_ref, lx_ref, zg_ref, zo_ref, done_ref, dctx_ref, small_ref, dffb_ref,
    w5, wd, hid, act, d_act, kept, hf, n_one, r_one, d_two, d_first, d_hid, turn, rows_out, z_out, sem,
):
    z_at, y_at, core = at_ref[0], at_ref[1], at_ref[2]
    pairs = [masks(core, False), masks(core, True)]
    for parts, slot in ((pl.ds(4, 1), 0), (pl.ds(0, 4), 5)):
        for late, side, src in ((0, 0, a0), (1, 0, a1), (0, 1, a2), (1, 1, a3)):
            for block in range(8):
                y = xor2(y_at, block >> 2 & 1, late, pairs[side])
                z = xor2(z_at, block & 1, block >> 1 & 1, pairs[side])
                row = pl.multiple_of(((z * 4 + y) * 2 + (core ^ side)) * 32, 32)
                pltpu.make_async_copy(src.at[block, parts], w5.at[parts, pl.ds(row, 32), :], sem.at[slot]).start()
    for late, side, src in ((0, 0, e0), (1, 0, e1), (0, 1, e2), (1, 1, e3)):
        for block in range(8):
            z = xor2(z_at, block >> 2 & 1, late, pairs[side])
            y = xor2(y_at, block & 1, block >> 1 & 1, pairs[side])
            row = pl.multiple_of(((z * 4 + y) * 2 + (core ^ side)) * 128, 128)
            pltpu.make_async_copy(src.at[block], wd.at[pl.ds(row, 128), :], sem.at[1]).start()

    outs = {}

    def out(name, src, dst):
        outs[name] = pltpu.make_async_copy(src, dst, sem.at[6 + len(outs)])
        outs[name].start()

    def select_rows(lanes):
        for side in range(2):
            for block in range(16):
                z = xor2(z_at, block >> 3 & 1, block >> 2 & 1, pairs[side])
                y = xor2(y_at, block >> 1 & 1, block & 1, pairs[side])
                row = pl.multiple_of(((z * 4 + y) * 2 + (core ^ side)) * 32, 32)
                to, at_lane = block % 8 * 32, lanes + block // 8 * 256
                rows_out[side, to : to + 32, at_lane : at_lane + 256] = turn[pl.ds(row, 32), :]

    for part in range(4):
        kept[3, :, part * 256 : part * 256 + 256] = ctx_ref[part]
    turn[...] = kept[3].T
    select_rows(512)
    pltpu.make_async_copy(w5.at[pl.ds(4, 1)], w5.at[pl.ds(4, 1)], sem.at[0]).wait()
    attended = vec_ref[4:5, :]
    for part in range(4):
        attended = attended + dot_nn(ctx_ref[part], w5[4, part * 256 : part * 256 + 256, :])
    normal, spread = norm_forward(tok_ref[...].astype(F32) + attended)
    n_one[...] = normal
    r_one[...] = spread
    hf[...] = normal * vec_ref[0:1, :] + vec_ref[5:6, :]
    kept[2] = hf[...].astype(BF16)
    turn[...] = kept[2].T
    select_rows(0)
    out("l_own", rows_out.at[0], lx_ref)
    out("l_give", rows_out.at[1], dx_ref.at[5])
    pltpu.make_async_copy(w5.at[pl.ds(0, 4)], w5.at[pl.ds(0, 4)], sem.at[5]).wait()

    @unrolled(4)
    def _(cb):
        cols = slice(cb * 1024, cb * 1024 + 1024)
        hid[cb] = dot_nn(kept[2], w5[cb]) + ffb_ref[:, cols]

        @unrolled(8)
        def _(chunk):
            rows = slice(chunk * 32, chunk * 32 + 32)
            u = hid[cb, rows, :]
            t = jnp.tanh(GELU_IN * (u + GELU_CUBE * (u * u * u)))
            act[cb, rows, :] = (u * (0.5 * (1.0 + t))).astype(BF16)

        for side in range(2):
            for block in range(4):
                y = xor2(y_at, block >> 1, block & 1, pairs[side])
                lanes = pl.ds(pl.multiple_of((y * 2 + (core ^ side)) * 128, 128), 128)
                to = cb % 2 * 512 + block * 128
                z_out[side, cb // 2, :, to : to + 128] = act[cb, :, lanes]

    pltpu.make_async_copy(wd, wd, sem.at[1]).wait()
    d_first[...] = hf[...] + vec_ref[6:7, :]

    @unrolled(4)
    def _(cb):
        d_first[...] += dot_nn(act[cb], wd[slice(cb * 1024, cb * 1024 + 1024), :])

    normal, spread = norm_forward(d_first[...])
    out_ref[...] = (normal * vec_ref[1:2, :] + vec_ref[7:8, :]).astype(BF16)
    cot = cot_ref[...].astype(F32)
    small_ref[...] = jnp.zeros_like(small_ref)
    small_ref[1:2, :] = column_sum(cot * normal)
    small_ref[7:8, :] = column_sum(cot)
    d_two[...] = norm_back(cot * vec_ref[1:2, :], normal, spread)
    out("z_own", z_out.at[0], zo_ref)
    out("z_give", z_out.at[1], zg_ref.at[pl.ds(0, 2)])
    kept[1] = d_two[...].astype(BF16)
    out("d_f", kept.at[1], zg_ref.at[2])
    small_ref[6:7, :] = column_sum(kept[1].astype(F32))
    d_first[...] = d_two[...]

    @unrolled(4)
    def _(cb):
        cols = slice(cb * 1024, cb * 1024 + 1024)
        d_hid[...] = dot_nt(kept[1], wd[cols, :])
        dffb_ref[:, cols] = jnp.zeros((1, 1024), F32)

        @unrolled(8)
        def _(chunk):
            rows = slice(chunk * 32, chunk * 32 + 32)
            u = hid[cb, rows, :]
            square = u * u
            t = jnp.tanh(GELU_IN * (u + GELU_CUBE * (square * u)))
            slope = 0.5 * (1.0 + t) + (0.5 * GELU_IN) * u * (1.0 - t * t) * (1.0 + (3.0 * GELU_CUBE) * square)
            d_low = (d_hid[rows, :] * slope).astype(BF16)
            d_act[cb, rows, :] = d_low
            dffb_ref[:, cols] += column_sum(d_low.astype(F32))

        out(cb, d_act.at[cb], dx_ref.at[cb])
        d_first[...] += dot_nt(d_act[cb], w5[cb])

    d_h = d_first[...]
    normal = n_one[...]
    small_ref[0:1, :] = column_sum(d_h * normal)
    small_ref[5:6, :] = column_sum(d_h)
    d_one = norm_back(d_h * vec_ref[0:1, :], normal, r_one[...])
    done_ref[...] = d_one
    kept[0] = d_one.astype(BF16)
    out("d_a", kept.at[0], dx_ref.at[4])
    small_ref[4:5, :] = column_sum(kept[0].astype(F32))
    for part in range(4):
        dctx_ref[part] = dot_nt(kept[0], w5[4, part * 256 : part * 256 + 256, :]).astype(BF16)
    for copy in outs.values():
        copy.wait()


def wide_kernel(at_ref, l_own, d_own, d_oth, a0_ref, a1_ref, acts, packed, left, stage, sem):
    loads = [
        [pltpu.make_async_copy(l_own, packed.at[0], sem.at[0, 0]), pltpu.make_async_copy(d_oth.at[5], packed.at[1], sem.at[0, 1])]
    ]
    for part in range(5):
        loads.append(
            [
                pltpu.make_async_copy(src.at[part], acts.at[part, side], sem.at[1 + part, side])
                for side, src in ((0, d_own), (1, d_oth))
            ]
        )
    for group in loads:
        for copy in group:
            copy.start()

    def out(part):
        return [
            pltpu.make_async_copy(stage.at[part, pl.ds(half * 8, 8)], dst.at[:, part], sem.at[6 + part, half])
            for half, dst in ((0, a0_ref), (1, a1_ref))
        ]

    for copy in loads[0]:
        copy.wait()
    for kind in range(2):
        for rows in range(2):
            for side in range(2):
                lanes = kind * 512 + rows * 256
                left[kind, rows * 256 : rows * 256 + 256, side * 256 : side * 256 + 256] = packed[side, :, lanes : lanes + 256]
    for part in range(5):
        for copy in loads[1 + part]:
            copy.wait()
        grad = dot_nn(left[part // 4], acts[part].reshape(512, 1024))
        stage[part] = grad.astype(BF16).reshape(16, 32, 1024)
        for copy in out(part):
            copy.start()
    for part in range(5):
        for copy in out(part):
            copy.wait()


def down_kernel(at_ref, z_own, f_own, z_oth, b0_ref, b1_ref, zs, fs, stage, sem):
    z_at, core = at_ref[0], at_ref[2]
    one, two = masks(core, False)
    loads = [
        [pltpu.make_async_copy(src.at[2], fs.at[side], sem.at[0, side]) for side, src in ((0, f_own), (1, z_oth))]
    ]
    for half in range(2):
        loads.append(
            [
                pltpu.make_async_copy(src.at[half], zs.at[half, side], sem.at[1 + half, side])
                for side, src in ((0, z_own), (1, z_oth))
            ]
        )
    for group in loads:
        for copy in group:
            copy.start()

    def place(z):
        gap = z ^ z_at
        both = (gap == 2).astype(jnp.int32)
        return ((gap == one).astype(jnp.int32) + both) * 2 + (gap == two).astype(jnp.int32) + both

    def out(z):
        return [
            pltpu.make_async_copy(stage.at[z, pl.ds(half * 2, 2)], dst.at[:, place(z)], sem.at[3 + z, half])
            for half, dst in ((0, b0_ref), (1, b1_ref))
        ]

    for copy in loads[0]:
        copy.wait()
    for z in range(4):
        if z % 2 == 0:
            for copy in loads[1 + z // 2]:
                copy.wait()
        picked = zs[z // 2, :, :, z % 2 * 512 : z % 2 * 512 + 512].reshape(512, 512)
        stage[z] = dot_tn(picked, fs[...].reshape(512, 1024)).astype(BF16).reshape(4, 128, 1024)
        for copy in out(z):
            copy.start()
    for z in range(4):
        for copy in out(z):
            copy.wait()


SMEM = pl.BlockSpec(memory_space=pltpu.SMEM)
VMEM = pl.BlockSpec(memory_space=pltpu.VMEM)
ANY = pl.BlockSpec(memory_space=pl.ANY)
MIB = 2**20


def pack_kernel(up_ref, out_ref, down_ref, in_ref, gains_ref, bias_ref, ffb_ref, pack_ref, rows, square):
    for cb in range(4):
        rows[cb * 8 : cb * 8 + 8, :] = up_ref[:, cb * 1024 : cb * 1024 + 1024]
    rows[32:40, :] = out_ref[...]
    rows[40:72, :] = down_ref[...]
    for cb in range(3):
        rows[72 + cb * 8 : 80 + cb * 8, :] = in_ref[:, cb * 1024 : cb * 1024 + 1024]
    square[...] = jnp.zeros_like(square)
    square[0:2, :8] = gains_ref[...]
    for j in range(4):
        square[8 + j : 9 + j, :8] = ffb_ref[:, j * 8 : j * 8 + 8]
    rows[96:104, :] = jnp.zeros((8, 1024), F32)
    rows[96:104, :128] = square[...].T[:8]
    rows[96:104, 2:8] = bias_ref[...]
    pack_ref[...] = rows[...].astype(BF16)


def packed_rows(arrays):
    return pl.pallas_call(
        pack_kernel,
        in_specs=[VMEM] * 7,
        out_specs=VMEM,
        out_shape=jax.ShapeDtypeStruct((104, 1024), BF16),
        scratch_shapes=[pltpu.VMEM((104, 1024), F32), pltpu.VMEM((128, 128), F32)],
        name="pack_rows",
    )(arrays[2], arrays[1], arrays[3], arrays[0], *arrays[4:])


def finish_kernel(at_ref, p0, p1, p2, p3, in_ref, out_ref, up_ref, down_ref, gains_ref, bias_ref, ffb_ref, sq_ref, square):
    x_at = at_ref[3]
    parts = [ref[...].astype(F32) for ref in (p0, p1, p2, p3)]
    total = parts[0][:72] + parts[1][:72] + parts[2][:72] + parts[3][:72]
    for cb in range(4):
        up_ref[:, cb * 1024 : cb * 1024 + 1024] = total[cb * 8 : cb * 8 + 8]
    out_ref[...] = total[32:40]
    down_ref[...] = total[40:72]
    extra = jnp.zeros((8, 128), F32)
    squares = jnp.sum(total * total, keepdims=True)
    for j, part in enumerate(parts):
        rows = part[72:80]
        group = (x_at + j) % 4
        for block in range(3):
            cols = pl.ds(pl.multiple_of(block * 1024 + group * 256, 256), 256)
            in_ref[:, cols] = rows[:, block * 256 : block * 256 + 256]
        squares = squares + jnp.sum(rows[:, :768] * rows[:, :768], keepdims=True)
        extra = extra + rows[:, 768:896]
    square[...] = jnp.zeros_like(square)
    square[:8, :] = extra
    turned = square[...].T
    gains_ref[...] = turned[0:2, :8]
    bias_ref[...] = extra[:, 2:8]
    for j in range(4):
        ffb_ref[:, j * 8 : j * 8 + 8] = turned[8 + j : 9 + j, :8]
    squares = squares + jnp.sum(turned[:12] * turned[:12], keepdims=True)
    sq_ref[...] = jnp.broadcast_to(squares, sq_ref.shape)


def finished(at, parts):
    shapes = [(8, 3072), (8, 1024), (8, 4096), (32, 1024), (2, 8), (8, 6), (1, 32), (1, 128)]
    return pl.pallas_call(
        finish_kernel,
        in_specs=[SMEM] + [VMEM] * 4,
        out_specs=[VMEM] * 8,
        out_shape=[jax.ShapeDtypeStruct(shape, F32) for shape in shapes],
        scratch_shapes=[pltpu.VMEM((128, 128), F32)],
        name="finish",
    )(at, *parts)


def attend(at, w_own, w_other, toks, code_col, code_row):
    return pl.pallas_call(
        attend_kernel,
        in_specs=[SMEM] + [VMEM] * 8,
        out_specs=[VMEM] * 5,
        out_shape=[
            jax.ShapeDtypeStruct((1024, 768), BF16),
            jax.ShapeDtypeStruct((16, 1024), F32),
            jax.ShapeDtypeStruct((4, 256, 256), BF16),
            jax.ShapeDtypeStruct((4, 1024), F32),
            jax.ShapeDtypeStruct((1024, 1024), BF16),
        ],
        scratch_shapes=[
            pltpu.VMEM((1024, 1024), F32),
            pltpu.VMEM((256, 1024), BF16),
        ],
        compiler_params=pltpu.CompilerParams(vmem_limit_bytes=56 * MIB),
        cost_estimate=pl.CostEstimate(flops=13 * 10**9, bytes_accessed=9 * MIB, transcendentals=4 * MIB),
        name="attend",
    )(at, w_own, w_other, *toks, code_col, code_row)


def input_back(at, d_qkv, w_in):
    return pl.pallas_call(
        back_kernel,
        in_specs=[SMEM, VMEM, VMEM],
        out_specs=VMEM,
        out_shape=jax.ShapeDtypeStruct((4, 256, 1024), BF16),
        compiler_params=pltpu.CompilerParams(vmem_limit_bytes=24 * MIB),
        cost_estimate=pl.CostEstimate(flops=2 * 10**9, bytes_accessed=6 * MIB, transcendentals=0),
        name="input_back",
    )(at, d_qkv, w_in)


def attend_back(at, toks, qkv, d_all, code_col, code_row, lse, small):
    return pl.pallas_call(
        attend_back_kernel,
        in_specs=[SMEM] + [ANY] * 4 + [VMEM] * 6,
        out_specs=[VMEM] * 3,
        out_shape=[jax.ShapeDtypeStruct((16, 32, 896), BF16)] * 2 + [jax.ShapeDtypeStruct((1024, 768), BF16)],
        scratch_shapes=[
            pltpu.VMEM((1024, 256), BF16),
            pltpu.VMEM((128, 1024), F32),
            pltpu.VMEM((1024, 1024), F32),
            pltpu.VMEM((256, 1024), BF16),
            pltpu.VMEM((16, 2, 32, 896), BF16),
            pltpu.VMEM((4, 256, 1024), BF16),
            pltpu.SemaphoreType.DMA((4,)),
        ],
        compiler_params=pltpu.CompilerParams(vmem_limit_bytes=56 * MIB),
        cost_estimate=pl.CostEstimate(flops=22 * 10**9, bytes_accessed=14 * MIB, transcendentals=4 * MIB),
        name="attend_back",
    )(at, *toks, qkv, d_all, code_col, code_row, lse, small)


def wide_grads(at, l_own, d_own, d_oth):
    return pl.pallas_call(
        wide_kernel,
        in_specs=[SMEM, ANY, ANY, ANY],
        out_specs=[ANY, ANY],
        out_shape=[pltpu.HBM((8, 5, 32, 1024), BF16)] * 2,
        scratch_shapes=[
            pltpu.VMEM((5, 2, 256, 1024), BF16),
            pltpu.VMEM((2, 256, 1024), BF16),
            pltpu.VMEM((2, 512, 512), BF16),
            pltpu.VMEM((5, 16, 32, 1024), BF16),
            pltpu.SemaphoreType.DMA((11, 2)),
        ],
        compiler_params=pltpu.CompilerParams(vmem_limit_bytes=56 * MIB),
        cost_estimate=pl.CostEstimate(flops=3 * 10**9, bytes_accessed=12 * MIB, transcendentals=0),
        name="wide_grads",
    )(at, l_own, d_own, d_oth)


def down_grads(at, z_own, f_own, z_oth):
    return pl.pallas_call(
        down_kernel,
        in_specs=[SMEM, ANY, ANY, ANY],
        out_specs=[ANY, ANY],
        out_shape=[pltpu.HBM((2, 4, 128, 1024), BF16)] * 2,
        scratch_shapes=[
            pltpu.VMEM((2, 2, 256, 1024), BF16),
            pltpu.VMEM((2, 256, 1024), BF16),
            pltpu.VMEM((4, 4, 128, 1024), BF16),
            pltpu.SemaphoreType.DMA((7, 2)),
        ],
        compiler_params=pltpu.CompilerParams(vmem_limit_bytes=56 * MIB),
        cost_estimate=pl.CostEstimate(flops=3 * 10**9, bytes_accessed=10 * MIB, transcendentals=0),
        name="down_grads",
    )(at, z_own, f_own, z_oth)


def token_layer(at, pieces_a, pieces_b, context, tokens, cotangent, vectors, ffb):
    return pl.pallas_call(
        token_kernel,
        in_specs=[SMEM] + [ANY] * 8 + [VMEM] * 5,
        out_specs=[VMEM] + [ANY] * 4 + [VMEM] * 4,
        out_shape=[
            jax.ShapeDtypeStruct((256, 1024), BF16),
            pltpu.HBM((6, 256, 1024), BF16),
            pltpu.HBM((256, 1024), BF16),
            pltpu.HBM((3, 256, 1024), BF16),
            pltpu.HBM((2, 256, 1024), BF16),
            jax.ShapeDtypeStruct((256, 1024), F32),
            jax.ShapeDtypeStruct((4, 256, 256), BF16),
            jax.ShapeDtypeStruct((8, 1024), F32),
            jax.ShapeDtypeStruct((1, 4096), F32),
        ],
        scratch_shapes=[
            pltpu.VMEM((5, 1024, 1024), BF16),
            pltpu.VMEM((4096, 1024), BF16),
            pltpu.VMEM((4, 256, 1024), F32),
            pltpu.VMEM((4, 256, 1024), BF16),
            pltpu.VMEM((4, 256, 1024), BF16),
            pltpu.VMEM((4, 256, 1024), BF16),
            pltpu.VMEM((256, 1024), F32),
            pltpu.VMEM((256, 1024), F32),
            pltpu.VMEM((256, 1), F32),
            pltpu.VMEM((256, 1024), F32),
            pltpu.VMEM((256, 1024), F32),
            pltpu.VMEM((256, 1024), F32),
            pltpu.VMEM((1024, 256), BF16),
            pltpu.VMEM((2, 256, 1024), BF16),
            pltpu.VMEM((2, 2, 256, 1024), BF16),
            pltpu.SemaphoreType.DMA((16,)),
        ],
        compiler_params=pltpu.CompilerParams(vmem_limit_bytes=60 * MIB),
        cost_estimate=pl.CostEstimate(flops=10 * 10**9, bytes_accessed=30 * MIB, transcendentals=2 * MIB),
        name="token_layer",
    )(at, *pieces_a, *pieces_b, context, tokens, cotangent, vectors, ffb)


def lamb_kernel(squares_ref, *refs):
    factor = CLIP_NORM / jnp.maximum(jnp.sqrt(jnp.sum(squares_ref[...], axis=0)[:, :1]), CLIP_NORM)
    for i in range(7):
        weight, grad = refs[i][...], refs[7 + i][...] * factor
        new_first = BETA_ONE * refs[14 + i][...] + (1.0 - BETA_ONE) * grad
        new_second = BETA_TWO * refs[21 + i][...] + (1.0 - BETA_TWO) * grad * grad
        direction = (
            new_first
            / (1.0 - BETA_ONE**STEP_COUNT)
            / (jnp.sqrt(new_second / (1.0 - BETA_TWO**STEP_COUNT)) + ADAM_EPS)
            + WEIGHT_DECAY * weight
        )
        weight_norm = jnp.sqrt(jnp.sum(weight * weight, keepdims=True))
        dir_norm = jnp.sqrt(jnp.sum(direction * direction, keepdims=True))
        refs[28 + i][...] = direction * (weight_norm / jnp.maximum(dir_norm, 1.0))


def lamb_steps(squares, weights, grads, firsts, seconds):
    return pl.pallas_call(
        lamb_kernel,
        in_specs=[VMEM] * 29,
        out_specs=[VMEM] * 7,
        out_shape=[jax.ShapeDtypeStruct(weight.shape, F32) for weight in weights],
        name="lamb",
    )(squares, *weights, *grads, *firsts, *seconds)


def body(tokens, cotangent, doc_lengths, *params):

    def turned(arrays):
        return (*arrays[:4], arrays[4].T, arrays[5], arrays[6].reshape(1, 32))

    shards, firsts, seconds = turned(params[:7]), turned(params[7:14]), turned(params[14:])
    dp_index = lax.axis_index("dp")
    z_at, y_at, core, x_at = dp_index // 8, dp_index // 2 % 4, dp_index % 2, lax.axis_index("group")
    at = jnp.stack([z_at, y_at, core, x_at]).astype(jnp.int32)

    with jax.named_scope("gather_x"):
        pack = packed_rows(shards)
        pack = rolled([pack[None]] + [push(pack, "x", -j)[None] for j in (1, 2, 3)], x_at, 0)
        own = lax.dynamic_slice_in_dim(pack[:, 72:96], x_at * 256, 256, axis=2)
        own = own.reshape(4, 3, 8, 256).transpose(0, 2, 1, 3).reshape(4, 8, 768)
        own = jnp.concatenate([own, pack[:, 96:, :256]], axis=2)
        part_a = pack[:, :40].reshape(4, 5, 8, 1024).transpose(1, 0, 2, 3).reshape(1, 5, 32, 1024)
        part_b = jnp.concatenate([pack[:, 40:72].reshape(1, 4, 32, 1024), own.reshape(1, 1, 32, 1024)], axis=1)

    with jax.named_scope("gather_tokens"):
        toks = [tokens, push(tokens, "x", -1), tokens, push(tokens, "x", -3)]

    with jax.named_scope("visible"):
        order = (x_at + jnp.arange(4, dtype=jnp.int32)) % 4
        positions = (order[:, None] * 256 + jnp.arange(256, dtype=jnp.int32)[None]).reshape(1024)
        ends = [doc_lengths[0, 0], doc_lengths[0, 0] + doc_lengths[0, 1]]
        ends.append(ends[1] + doc_lengths[0, 2])
        ids = sum((positions >= end).astype(jnp.int32) for end in ends)
        code = (positions + 4096 * ids).astype(F32)
        code_col, code_row = code[:, None], code[None]

    with jax.named_scope("gather_yz"):
        part_a, part_b = doubled(part_a, "z", 0), doubled(part_b, "y", 0)
        part_a, part_b = doubled(part_a, "z", 1), doubled(part_b, "y", 1)
        part_a, part_b, *toks = lax.optimization_barrier((part_a, part_b, *toks))
        toks[2] = push(toks[2], "x", -2)
        part_b, w_own = part_b[:, :4].reshape(4, 128, 1024), part_b[:, 4]
        w_own = doubled(w_own, "z", 0)
        part_a, part_b, at, code_col, code_row = lax.optimization_barrier((part_a, part_b, at, code_col, code_row))
        w_own = doubled(w_own, "z", 1)
        part_a, part_b = doubled(part_a, "y", 0), doubled(part_b, "z", 0)
        w_own, toks[2] = lax.optimization_barrier((w_own, toks[2]))
        w_other = push(w_own, "core", 1)
        far_a, far_b = swap(part_a, "y", 1), swap(part_b, "z", 1)

    with jax.named_scope("attention"):
        qkv, vectors, out_all, lse, w_in = attend(at, w_own, w_other, toks, code_col, code_row)
        other_b = push(part_b, "core", 1)
        part_a, other_b, out_all = lax.optimization_barrier((part_a, other_b, out_all))
        other_a = push(part_a, "core", 1)
        context = lax.all_to_all(out_all, "group", 0, 0, tiled=True)
        ffb = vectors[8:12].reshape(4, 128, 8).transpose(1, 0, 2).reshape(1, 4096)

    with jax.named_scope("gather_ff"):
        far_a, far_b, context = lax.optimization_barrier((far_a, far_b, context))
        pieces_a = (part_a, far_a, other_a, push(far_a, "core", 1))
        pieces_b = (part_b, far_b, other_b, push(far_b, "core", 1))

    with jax.named_scope("tokens"):
        block_out, dx, lx, zg, zo, d_one, d_context, small, d_ffb = token_layer(
            at, pieces_a, pieces_b, context, tokens, cotangent, vectors, ffb
        )

    with jax.named_scope("scatter_ff"):
        dx_other, zg_other = push(dx, "core", 1), push(zg, "core", 1)
        keep_a, sent_a = wide_grads(at, lx, dx, dx_other)
        sent_a, zg_other, small, d_ffb = lax.optimization_barrier((sent_a, zg_other, small, d_ffb))
        got_a = swap(sent_a, "z", 0)
        keep_b, sent_b = down_grads(at, zo, zg, zg_other)
        ffb_rows = d_ffb.reshape(128, 4, 8).transpose(1, 0, 2).reshape(4, 1024)
        small = jnp.concatenate([small, ffb_rows, jnp.zeros((4, 1024), F32)], axis=0)

    with jax.named_scope("attention_back"):
        d_all = lax.all_to_all(d_context, "group", 0, 0, tiled=True)
        d_all, sent_b = lax.optimization_barrier((d_all, sent_b))

    with jax.named_scope("scatter_ff"):
        terms_b, terms_a = [keep_b, swap(sent_b, "y", 0)], [keep_a, got_a]
        sent_b, sent_a = outgoing(terms_b), outgoing(terms_a)

    with jax.named_scope("attention_back"):
        keep_in, give_in, d_qkv = attend_back(at, toks, qkv, d_all, code_col, code_row, lse, small)

    with jax.named_scope("scatter_attn_in"):
        terms_in = [keep_in, push(give_in, "core", 1)]
        terms_in = step_down(terms_in, outgoing(terms_in), "y", 0)
        backs, terms_in[-1] = lax.optimization_barrier((input_back(at, d_qkv, w_in), terms_in[-1]))

    with jax.named_scope("input_grad"):
        backs = lax.all_to_all(backs, "group", 0, 0, tiled=True)

    with jax.named_scope("scatter_ff"):
        for axis_b, axis_a, axis_in, step in (("y", "z", "y", 1), ("z", "y", "z", 0), ("z", "y", "z", 1)):
            if axis_b == "z":
                terms_b, terms_a, terms_in = lax.optimization_barrier((terms_b, terms_a, terms_in))
                sent_b, sent_a = outgoing(terms_b), outgoing(terms_a)
            terms_b, terms_a = step_down(terms_b, sent_b, axis_b, step), step_down(terms_a, sent_a, axis_a, step)
            terms_in = step_down(terms_in, outgoing(terms_in), axis_in, step)
        sum_b, sum_a, sum_in = (sum(term.astype(F32) for term in terms) for terms in (terms_b, terms_a, terms_in))
        sum_in = sum_in.reshape(4, 8, 896)
        pack = jnp.concatenate(
            [
                sum_a.reshape(5, 4, 8, 1024).transpose(1, 0, 2, 3).reshape(4, 40, 1024),
                sum_b.reshape(4, 32, 1024),
                jnp.concatenate([sum_in, jnp.zeros((4, 8, 128), F32)], axis=2),
            ],
            axis=1,
        )
        parts = [pick(pack, x_at, 0)]
        parts += [push(pick(pack, (x_at + 4 - j) % 4, 0).astype(BF16), "x", -j) for j in (1, 2, 3)]
        *grads, squares = finished(at, parts)

    with jax.named_scope("input_grad"):
        input_grad = d_one + jnp.sum(backs.astype(F32), axis=0)

    with jax.named_scope("norm"):
        squares = lax.all_to_all(jnp.broadcast_to(squares[None], (128, 1, 128)), AXES, 0, 0, tiled=True)
    with jax.named_scope("lamb"):
        steps = lamb_steps(squares, shards, grads, firsts, seconds)

    def restored(arrays):
        return (*arrays[:4], arrays[4].T, arrays[5], arrays[6].reshape(32))

    return (block_out, input_grad, *restored(grads), *restored(steps))


def solution(mesh):
    rows, vector, docs = P(AXES, None), P(AXES), P("dp", None)
    leaves = (rows,) * 6 + (vector,)
    return jax.shard_map(
        body,
        mesh=mesh,
        in_specs=(rows, rows, docs) + leaves * 3,
        out_specs=(rows, rows) + leaves * 2,
        check_vma=False,
    )
```

```python
import jax
import jax.numpy as jnp
import numpy as np
from jax import lax
from jax.experimental import pallas as pl
from jax.experimental.pallas import tpu as pltpu
from jax.sharding import PartitionSpec as P

HEADS = 16
WINDOW = 1024
AXES = ("dp", "group")
RADIX = {"z": 4, "y": 4, "core": 2, "x": 4}

NORM_EPS = 1e-06
CLIP_NORM = 1.0
BETA_ONE = 0.9
BETA_TWO = 0.999
STEP_COUNT = 10
ADAM_EPS = 1e-06
WEIGHT_DECAY = 0.01
MASKED_SCORE = -1e30
F32 = jnp.float32
BF16 = jnp.bfloat16


def flat_of(at):
    return ((at["z"] * 4 + at["y"]) * 2 + at["core"]) * 4 + at["x"]


def device_pairs(move):
    out = []
    for flat in range(128):
        at = {"z": flat // 32, "y": flat // 8 % 4, "core": flat // 4 % 2, "x": flat % 4}
        move(at)
        out.append((flat, flat_of(at)))
    return out


def push(value, axis, shift):
    def move(at):
        at[axis] = (at[axis] + shift) % RADIX[axis]

    return lax.ppermute(value, AXES, device_pairs(move))


def swap(value, axis, step):
    def move(at):
        at[axis] ^= (1, 3)[(at["core"] + step) % 2]

    return lax.ppermute(value, AXES, device_pairs(move))


def spread(value, axes):
    names = ("z", "y", "core", "x")
    order = [name for name in names if name not in axes] + list(axes)
    grid = np.arange(128).reshape(4, 4, 2, 4).transpose([names.index(name) for name in order])
    groups = grid.reshape(-1, value.shape[0]).tolist()
    return lax.all_to_all(value, AXES, 0, 0, axis_index_groups=groups, tiled=True)


def pick(value, index, dim):
    return lax.dynamic_index_in_dim(value, index, dim, keepdims=False)


def rolled(parts, me, dim):
    joined = jnp.concatenate(parts + parts[:3], axis=dim)
    width = parts[0].shape[dim]
    return lax.dynamic_slice_in_dim(joined, (4 - me) % 4 * width, 4 * width, dim)


def doubled(value, axis, step):
    return jnp.concatenate([value, swap(value, axis, step)], axis=0)


def outgoing(terms):
    half = terms[0].shape[0] // 2
    return sum(term[half:].astype(F32) for term in terms).astype(BF16)


def step_down(terms, sent, axis, step):
    half = terms[0].shape[0] // 2
    terms = [term[:half] for term in terms] + [swap(sent, axis, step)]
    if half == 1:
        terms = [term[0] for term in terms]
    return terms


def masks(core, owner_is_other):
    one = core * 2 + 1
    two = 3 - core * 2
    return (two, one) if owner_is_other else (one, two)


def dot_nn(a, b):
    return jnp.dot(a, b, preferred_element_type=F32)


def dot_nt(a, b):
    return lax.dot_general(a, b, (((1,), (1,)), ((), ())), preferred_element_type=F32)


def dot_tn(a, b):
    return lax.dot_general(a, b, (((0,), (0,)), ((), ())), preferred_element_type=F32)


def xor2(me, bit_one, bit_two, pair):
    value = me
    if bit_one:
        value = value ^ pair[0]
    if bit_two:
        value = value ^ pair[1]
    return value


def unrolled(count):
    def run(part):
        for index in range(count):
            part(index)

    return run


def set_mask(mask_ref, col_ref, row_ref):
    @unrolled(8)
    def _(chunk):
        rows = slice(chunk * 128, chunk * 128 + 128)
        near = jnp.abs(col_ref[rows, :] - row_ref[...]) < WINDOW // 2
        mask_ref[rows, :] = jnp.where(near, 0.0, MASKED_SCORE)


def attend_kernel(
    at_ref, own_ref, other_ref, t0, t1, t2, t3, col_ref, row_ref,
    qkv_ref, vec_ref, out_ref, lse_ref, w_ref, mask_ref, turn_ref,
):
    z_at, y_at, core, x_at = at_ref[0], at_ref[1], at_ref[2], at_ref[3]
    for side, src in ((0, own_ref), (1, other_ref)):
        pair = masks(core, side == 1)
        for block in range(16):
            y = xor2(y_at, block & 1, block >> 1 & 1, pair)
            z = xor2(z_at, block >> 2 & 1, block >> 3 & 1, pair)
            row = pl.multiple_of(((z * 4 + y) * 2 + (core ^ side)) * 32, 32)
            w_ref[pl.ds(row, 32), :] = src[block]
    vec_ref[...] = w_ref[:, 768:896].astype(F32).T[:16]
    lanes = pl.ds(pl.multiple_of(x_at * 256, 256), 256)
    bias = jnp.concatenate([vec_ref[2:3, lanes], jnp.zeros((1, 256), F32), vec_ref[3:4, lanes]], axis=1)
    for j, tok in enumerate((t0, t1, t2, t3)):
        qkv_ref[j * 256 : j * 256 + 256, :] = (dot_nn(tok[...], w_ref[:, :768]) + bias).astype(BF16)
    set_mask(mask_ref, col_ref, row_ref)
    turn_ref[...] = qkv_ref[:, 512:768].T
    outs = []
    for head in range(4):
        lanes = slice(head * 64, head * 64 + 64)
        key = qkv_ref[:, 256 + head * 64 : 320 + head * 64]
        scores = dot_nt(key, qkv_ref[:, lanes] * BF16(0.125)) + mask_ref[...]
        top = jnp.max(scores, axis=0, keepdims=True)
        raised = jnp.exp(scores - top)
        total = jnp.sum(raised, axis=0, keepdims=True)
        probs = (raised * (1.0 / total)).astype(BF16)
        outs.append(dot_nn(turn_ref[lanes, :], probs))
        lse_ref[head : head + 1, :] = jnp.log(total) + top
    out = jnp.concatenate(outs, axis=0).T.astype(BF16)
    for block in range(4):
        out_ref[(x_at + block) % 4] = out[block * 256 : block * 256 + 256]


def attend_back_kernel(
    at_ref, t0, t1, t2, t3, qkv_ref, d_ref, col_ref, row_ref, lse_ref, small_ref,
    keep_ref, give_ref, dqkv_ref, d_rows, rows_ref, mask_ref, turn_ref, joined_ref, tok_ref, sem,
):
    z_at, y_at, core, x_at = at_ref[0], at_ref[1], at_ref[2], at_ref[3]
    copies = [pltpu.make_async_copy(src, tok_ref.at[i], sem.at[i]) for i, src in enumerate((t0, t1, t2, t3))]
    for copy in copies:
        copy.start()
    set_mask(mask_ref, col_ref, row_ref)
    turn_ref[...] = qkv_ref[:, 256:512].T
    for block in range(4):
        d_rows[block * 256 : block * 256 + 256, :] = d_ref[(x_at + block) % 4]
    outs = []
    for head in range(4):
        lanes = slice(head * 64, head * 64 + 64)
        key = qkv_ref[:, 256 + head * 64 : 320 + head * 64]
        value = qkv_ref[:, 512 + head * 64 : 576 + head * 64]
        query = qkv_ref[:, lanes] * BF16(0.125)
        d_out = d_rows[:, lanes]
        probs = jnp.exp(dot_nt(key, query) + mask_ref[...] - lse_ref[head : head + 1, :])
        d_probs = dot_nt(value, d_out)
        delta = jnp.sum(probs * d_probs, axis=0, keepdims=True)
        d_scores = (probs * (d_probs - delta)).astype(BF16)
        outs.append(dot_nn(turn_ref[lanes, :], d_scores) * 0.125)
        dqkv_ref[:, 256 + head * 64 : 320 + head * 64] = dot_nn(d_scores, query).astype(BF16)
        dqkv_ref[:, 512 + head * 64 : 576 + head * 64] = dot_nn(probs.astype(BF16), d_out).astype(BF16)
    dqkv_ref[:, :256] = jnp.concatenate(outs, axis=0).T.astype(BF16)
    rows_ref[...] = jnp.zeros_like(rows_ref)
    rows_ref[:16, :] = small_ref[...]
    lanes = pl.ds(pl.multiple_of(x_at * 256, 256), 256)
    sums = jnp.sum(dqkv_ref[...].astype(F32), axis=0, keepdims=True)
    rows_ref[2:3, lanes] = sums[:, :256]
    rows_ref[3:4, lanes] = sums[:, 512:]
    joined_ref[:, :, :, 768:896] = rows_ref[...].T.astype(BF16).reshape(16, 2, 32, 128)
    for copy in copies:
        copy.wait()
    total = dot_tn(tok_ref[0], dqkv_ref[:256, :])
    for block in (1, 2, 3):
        total = total + dot_tn(tok_ref[block], dqkv_ref[block * 256 : block * 256 + 256, :])
    joined_ref[:, :, :, :768] = total.astype(BF16).reshape(16, 2, 32, 768)
    for side, dst in ((0, keep_ref), (1, give_ref)):
        pair = masks(core, side == 1)
        for block in range(16):
            y = xor2(y_at, block >> 3 & 1, block >> 2 & 1, pair)
            z = xor2(z_at, block >> 1 & 1, block & 1, pair)
            dst[block] = joined_ref[z * 4 + y, core ^ side]


def back_kernel(at_ref, dqkv_ref, w_ref, back_ref):
    x_at = at_ref[3]
    for block in range(4):
        back = dot_nt(dqkv_ref[block * 256 : block * 256 + 256, :], w_ref[:, :768])
        back_ref[(x_at + block) % 4] = back.astype(BF16)


GELU_IN = 0.7978845608028654
GELU_CUBE = 0.044715


def norm_forward(value):
    center = value - jnp.mean(value, axis=-1, keepdims=True)
    spread = lax.rsqrt(jnp.mean(center * center, axis=-1, keepdims=True) + NORM_EPS)
    return center * spread, spread


def norm_back(d_normal, normal, spread):
    return spread * (
        d_normal
        - jnp.mean(d_normal, axis=-1, keepdims=True)
        - normal * jnp.mean(d_normal * normal, axis=-1, keepdims=True)
    )


def column_sum(value):
    return jnp.sum(value, axis=0, keepdims=True)


def token_kernel(
    at_ref, a0, a1, a2, a3, e0, e1, e2, e3, ctx_ref, tok_ref, cot_ref, vec_ref, ffb_ref,
    out_ref, dx_ref, lx_ref, zg_ref, zo_ref, done_ref, dctx_ref, small_ref, dffb_ref,
    w5, wd, hid, act, d_act, kept, hf, n_one, r_one, d_two, d_first, d_hid, turn, rows_out, z_out, sem,
):
    z_at, y_at, core = at_ref[0], at_ref[1], at_ref[2]
    pairs = [masks(core, False), masks(core, True)]
    for parts, slot in ((pl.ds(4, 1), 0), (pl.ds(0, 2), 5), (pl.ds(2, 2), 2)):
        for late, side, src in ((0, 0, a0), (1, 0, a1), (0, 1, a2), (1, 1, a3)):
            for block in range(8):
                y = xor2(y_at, block >> 2 & 1, late, pairs[side])
                z = xor2(z_at, block & 1, block >> 1 & 1, pairs[side])
                row = pl.multiple_of(((z * 4 + y) * 2 + (core ^ side)) * 32, 32)
                pltpu.make_async_copy(src.at[block, parts], w5.at[parts, pl.ds(row, 32), :], sem.at[slot]).start()
    for late, side, src in ((0, 0, e0), (1, 0, e1), (0, 1, e2), (1, 1, e3)):
        for block in range(8):
            z = xor2(z_at, block >> 2 & 1, late, pairs[side])
            y = xor2(y_at, block & 1, block >> 1 & 1, pairs[side])
            row = pl.multiple_of(((z * 4 + y) * 2 + (core ^ side)) * 128, 128)
            pltpu.make_async_copy(src.at[block], wd.at[pl.ds(row, 128), :], sem.at[1]).start()

    outs = {}

    def out(name, src, dst):
        outs[name] = pltpu.make_async_copy(src, dst, sem.at[6 + len(outs)])
        outs[name].start()

    def select_rows(lanes):
        for side in range(2):
            for block in range(16):
                z = xor2(z_at, block >> 3 & 1, block >> 2 & 1, pairs[side])
                y = xor2(y_at, block >> 1 & 1, block & 1, pairs[side])
                row = pl.multiple_of(((z * 4 + y) * 2 + (core ^ side)) * 32, 32)
                to, at_lane = block % 8 * 32, lanes + block // 8 * 256
                rows_out[side, to : to + 32, at_lane : at_lane + 256] = turn[pl.ds(row, 32), :]

    for part in range(4):
        kept[3, :, part * 256 : part * 256 + 256] = ctx_ref[part]
    turn[...] = kept[3].T
    select_rows(512)
    pltpu.make_async_copy(w5.at[pl.ds(4, 1)], w5.at[pl.ds(4, 1)], sem.at[0]).wait()
    attended = vec_ref[4:5, :]
    for part in range(4):
        attended = attended + dot_nn(ctx_ref[part], w5[4, part * 256 : part * 256 + 256, :])
    normal, spread = norm_forward(tok_ref[...].astype(F32) + attended)
    n_one[...] = normal
    r_one[...] = spread
    hf[...] = normal * vec_ref[0:1, :] + vec_ref[5:6, :]
    kept[2] = hf[...].astype(BF16)
    turn[...] = kept[2].T
    select_rows(0)
    out("l_own", rows_out.at[0], lx_ref)
    out("l_give", rows_out.at[1], dx_ref.at[5])

    @unrolled(4)
    def _(cb):
        cols = slice(cb * 1024, cb * 1024 + 1024)
        if cb % 2 == 0:
            half = w5.at[pl.ds(cb, 2)]
            pltpu.make_async_copy(half, half, sem.at[(5, 2)[cb // 2]]).wait()
        hid[cb] = dot_nn(kept[2], w5[cb]) + ffb_ref[:, cols]

        @unrolled(8)
        def _(chunk):
            rows = slice(chunk * 32, chunk * 32 + 32)
            u = hid[cb, rows, :]
            t = jnp.tanh(GELU_IN * (u + GELU_CUBE * (u * u * u)))
            act[cb, rows, :] = (u * (0.5 * (1.0 + t))).astype(BF16)

        for side in range(2):
            for block in range(4):
                y = xor2(y_at, block >> 1, block & 1, pairs[side])
                lanes = pl.ds(pl.multiple_of((y * 2 + (core ^ side)) * 128, 128), 128)
                to = cb % 2 * 512 + block * 128
                z_out[side, cb // 2, :, to : to + 128] = act[cb, :, lanes]

    pltpu.make_async_copy(wd, wd, sem.at[1]).wait()
    d_first[...] = hf[...] + vec_ref[6:7, :]

    @unrolled(4)
    def _(cb):
        d_first[...] += dot_nn(act[cb], wd[slice(cb * 1024, cb * 1024 + 1024), :])

    normal, spread = norm_forward(d_first[...])
    out_ref[...] = (normal * vec_ref[1:2, :] + vec_ref[7:8, :]).astype(BF16)
    cot = cot_ref[...].astype(F32)
    small_ref[...] = jnp.zeros_like(small_ref)
    small_ref[1:2, :] = column_sum(cot * normal)
    small_ref[7:8, :] = column_sum(cot)
    d_two[...] = norm_back(cot * vec_ref[1:2, :], normal, spread)
    out("z_own", z_out.at[0], zo_ref)
    out("z_give", z_out.at[1], zg_ref.at[pl.ds(0, 2)])
    kept[1] = d_two[...].astype(BF16)
    out("d_f", kept.at[1], zg_ref.at[2])
    small_ref[6:7, :] = column_sum(kept[1].astype(F32))
    d_first[...] = d_two[...]

    @unrolled(4)
    def _(cb):
        cols = slice(cb * 1024, cb * 1024 + 1024)
        d_hid[...] = dot_nt(kept[1], wd[cols, :])
        dffb_ref[:, cols] = jnp.zeros((1, 1024), F32)

        @unrolled(8)
        def _(chunk):
            rows = slice(chunk * 32, chunk * 32 + 32)
            u = hid[cb, rows, :]
            square = u * u
            t = jnp.tanh(GELU_IN * (u + GELU_CUBE * (square * u)))
            slope = 0.5 * (1.0 + t) + (0.5 * GELU_IN) * u * (1.0 - t * t) * (1.0 + (3.0 * GELU_CUBE) * square)
            d_low = (d_hid[rows, :] * slope).astype(BF16)
            d_act[cb, rows, :] = d_low
            dffb_ref[:, cols] += column_sum(d_low.astype(F32))

        out(cb, d_act.at[cb], dx_ref.at[cb])
        d_first[...] += dot_nt(d_act[cb], w5[cb])

    d_h = d_first[...]
    normal = n_one[...]
    small_ref[0:1, :] = column_sum(d_h * normal)
    small_ref[5:6, :] = column_sum(d_h)
    d_one = norm_back(d_h * vec_ref[0:1, :], normal, r_one[...])
    done_ref[...] = d_one
    kept[0] = d_one.astype(BF16)
    out("d_a", kept.at[0], dx_ref.at[4])
    small_ref[4:5, :] = column_sum(kept[0].astype(F32))
    for part in range(4):
        dctx_ref[part] = dot_nt(kept[0], w5[4, part * 256 : part * 256 + 256, :]).astype(BF16)
    for copy in outs.values():
        copy.wait()


def wide_kernel(at_ref, l_own, d_own, d_oth, a0_ref, a1_ref, acts, packed, left, stage, sem):
    loads = [
        [pltpu.make_async_copy(l_own, packed.at[0], sem.at[0, 0]), pltpu.make_async_copy(d_oth.at[5], packed.at[1], sem.at[0, 1])]
    ]
    for part in range(5):
        loads.append(
            [
                pltpu.make_async_copy(src.at[part], acts.at[part, side], sem.at[1 + part, side])
                for side, src in ((0, d_own), (1, d_oth))
            ]
        )
    for group in loads:
        for copy in group:
            copy.start()

    def out(part):
        return [
            pltpu.make_async_copy(stage.at[part, pl.ds(half * 8, 8)], dst.at[:, part], sem.at[6 + part, half])
            for half, dst in ((0, a0_ref), (1, a1_ref))
        ]

    for copy in loads[0]:
        copy.wait()
    for kind in range(2):
        for rows in range(2):
            for side in range(2):
                lanes = kind * 512 + rows * 256
                left[kind, rows * 256 : rows * 256 + 256, side * 256 : side * 256 + 256] = packed[side, :, lanes : lanes + 256]
    for part in range(5):
        for copy in loads[1 + part]:
            copy.wait()
        grad = dot_nn(left[part // 4], acts[part].reshape(512, 1024))
        stage[part] = grad.astype(BF16).reshape(16, 32, 1024)
        for copy in out(part):
            copy.start()
    for part in range(5):
        for copy in out(part):
            copy.wait()


def down_kernel(at_ref, z_own, f_own, z_oth, b0_ref, b1_ref, zs, fs, stage, sem):
    z_at, core = at_ref[0], at_ref[2]
    one, two = masks(core, False)
    loads = [
        [pltpu.make_async_copy(src.at[2], fs.at[side], sem.at[0, side]) for side, src in ((0, f_own), (1, z_oth))]
    ]
    for half in range(2):
        loads.append(
            [
                pltpu.make_async_copy(src.at[half], zs.at[half, side], sem.at[1 + half, side])
                for side, src in ((0, z_own), (1, z_oth))
            ]
        )
    for group in loads:
        for copy in group:
            copy.start()

    def place(z):
        gap = z ^ z_at
        both = (gap == 2).astype(jnp.int32)
        return ((gap == one).astype(jnp.int32) + both) * 2 + (gap == two).astype(jnp.int32) + both

    def out(z):
        return [
            pltpu.make_async_copy(stage.at[z, pl.ds(half * 2, 2)], dst.at[:, place(z)], sem.at[3 + z, half])
            for half, dst in ((0, b0_ref), (1, b1_ref))
        ]

    for copy in loads[0]:
        copy.wait()
    for z in range(4):
        if z % 2 == 0:
            for copy in loads[1 + z // 2]:
                copy.wait()
        picked = zs[z // 2, :, :, z % 2 * 512 : z % 2 * 512 + 512].reshape(512, 512)
        stage[z] = dot_tn(picked, fs[...].reshape(512, 1024)).astype(BF16).reshape(4, 128, 1024)
        for copy in out(z):
            copy.start()
    for z in range(4):
        for copy in out(z):
            copy.wait()


SMEM = pl.BlockSpec(memory_space=pltpu.SMEM)
VMEM = pl.BlockSpec(memory_space=pltpu.VMEM)
ANY = pl.BlockSpec(memory_space=pl.ANY)
MIB = 2**20


def pack_kernel(up_ref, out_ref, down_ref, in_ref, gains_ref, bias_ref, ffb_ref, pack_ref, rows, square):
    for cb in range(4):
        rows[cb * 8 : cb * 8 + 8, :] = up_ref[:, cb * 1024 : cb * 1024 + 1024]
    rows[32:40, :] = out_ref[...]
    rows[40:72, :] = down_ref[...]
    for cb in range(3):
        rows[72 + cb * 8 : 80 + cb * 8, :] = in_ref[:, cb * 1024 : cb * 1024 + 1024]
    square[...] = jnp.zeros_like(square)
    square[0:2, :8] = gains_ref[...]
    for j in range(4):
        square[8 + j : 9 + j, :8] = ffb_ref[:, j * 8 : j * 8 + 8]
    rows[96:104, :] = jnp.zeros((8, 1024), F32)
    rows[96:104, :128] = square[...].T[:8]
    rows[96:104, 2:8] = bias_ref[...]
    pack_ref[...] = rows[...].astype(BF16)


def packed_rows(arrays):
    return pl.pallas_call(
        pack_kernel,
        in_specs=[VMEM] * 7,
        out_specs=VMEM,
        out_shape=jax.ShapeDtypeStruct((104, 1024), BF16),
        scratch_shapes=[pltpu.VMEM((104, 1024), F32), pltpu.VMEM((128, 128), F32)],
        name="pack_rows",
    )(arrays[2], arrays[1], arrays[3], arrays[0], *arrays[4:])


def finish_kernel(at_ref, p0, p1, p2, p3, in_ref, out_ref, up_ref, down_ref, gains_ref, bias_ref, ffb_ref, sq_ref, square):
    x_at = at_ref[3]
    parts = [ref[...].astype(F32) for ref in (p0, p1, p2, p3)]
    total = parts[0][:72] + parts[1][:72] + parts[2][:72] + parts[3][:72]
    for cb in range(4):
        up_ref[:, cb * 1024 : cb * 1024 + 1024] = total[cb * 8 : cb * 8 + 8]
    out_ref[...] = total[32:40]
    down_ref[...] = total[40:72]
    extra = jnp.zeros((8, 128), F32)
    squares = jnp.sum(total * total, keepdims=True)
    for j, part in enumerate(parts):
        rows = part[72:80]
        group = (x_at + j) % 4
        for block in range(3):
            cols = pl.ds(pl.multiple_of(block * 1024 + group * 256, 256), 256)
            in_ref[:, cols] = rows[:, block * 256 : block * 256 + 256]
        squares = squares + jnp.sum(rows[:, :768] * rows[:, :768], keepdims=True)
        extra = extra + rows[:, 768:896]
    square[...] = jnp.zeros_like(square)
    square[:8, :] = extra
    turned = square[...].T
    gains_ref[...] = turned[0:2, :8]
    bias_ref[...] = extra[:, 2:8]
    for j in range(4):
        ffb_ref[:, j * 8 : j * 8 + 8] = turned[8 + j : 9 + j, :8]
    squares = squares + jnp.sum(turned[:12] * turned[:12], keepdims=True)
    sq_ref[...] = jnp.broadcast_to(squares[None], sq_ref.shape)


def finished(at, parts):
    shapes = [(8, 3072), (8, 1024), (8, 4096), (32, 1024), (2, 8), (8, 6), (1, 32), (128, 1, 128)]
    return pl.pallas_call(
        finish_kernel,
        in_specs=[SMEM] + [VMEM] * 4,
        out_specs=[VMEM] * 8,
        out_shape=[jax.ShapeDtypeStruct(shape, F32) for shape in shapes],
        scratch_shapes=[pltpu.VMEM((128, 128), F32)],
        name="finish",
    )(at, *parts)


def attend(at, w_own, w_other, toks, code_col, code_row):
    return pl.pallas_call(
        attend_kernel,
        in_specs=[SMEM] + [VMEM] * 8,
        out_specs=[VMEM] * 5,
        out_shape=[
            jax.ShapeDtypeStruct((1024, 768), BF16),
            jax.ShapeDtypeStruct((16, 1024), F32),
            jax.ShapeDtypeStruct((4, 256, 256), BF16),
            jax.ShapeDtypeStruct((4, 1024), F32),
            jax.ShapeDtypeStruct((1024, 1024), BF16),
        ],
        scratch_shapes=[
            pltpu.VMEM((1024, 1024), F32),
            pltpu.VMEM((256, 1024), BF16),
        ],
        compiler_params=pltpu.CompilerParams(vmem_limit_bytes=56 * MIB),
        cost_estimate=pl.CostEstimate(flops=13 * 10**9, bytes_accessed=9 * MIB, transcendentals=4 * MIB),
        name="attend",
    )(at, w_own, w_other, *toks, code_col, code_row)


def input_back(at, d_qkv, w_in):
    return pl.pallas_call(
        back_kernel,
        in_specs=[SMEM, VMEM, VMEM],
        out_specs=VMEM,
        out_shape=jax.ShapeDtypeStruct((4, 256, 1024), BF16),
        compiler_params=pltpu.CompilerParams(vmem_limit_bytes=24 * MIB),
        cost_estimate=pl.CostEstimate(flops=2 * 10**9, bytes_accessed=6 * MIB, transcendentals=0),
        name="input_back",
    )(at, d_qkv, w_in)


def attend_back(at, toks, qkv, d_all, code_col, code_row, lse, small):
    return pl.pallas_call(
        attend_back_kernel,
        in_specs=[SMEM] + [ANY] * 4 + [VMEM] * 6,
        out_specs=[VMEM] * 3,
        out_shape=[jax.ShapeDtypeStruct((16, 32, 896), BF16)] * 2 + [jax.ShapeDtypeStruct((1024, 768), BF16)],
        scratch_shapes=[
            pltpu.VMEM((1024, 256), BF16),
            pltpu.VMEM((128, 1024), F32),
            pltpu.VMEM((1024, 1024), F32),
            pltpu.VMEM((256, 1024), BF16),
            pltpu.VMEM((16, 2, 32, 896), BF16),
            pltpu.VMEM((4, 256, 1024), BF16),
            pltpu.SemaphoreType.DMA((4,)),
        ],
        compiler_params=pltpu.CompilerParams(vmem_limit_bytes=56 * MIB),
        cost_estimate=pl.CostEstimate(flops=22 * 10**9, bytes_accessed=14 * MIB, transcendentals=4 * MIB),
        name="attend_back",
    )(at, *toks, qkv, d_all, code_col, code_row, lse, small)


def wide_grads(at, l_own, d_own, d_oth):
    return pl.pallas_call(
        wide_kernel,
        in_specs=[SMEM, ANY, ANY, ANY],
        out_specs=[ANY, ANY],
        out_shape=[pltpu.HBM((8, 5, 32, 1024), BF16)] * 2,
        scratch_shapes=[
            pltpu.VMEM((5, 2, 256, 1024), BF16),
            pltpu.VMEM((2, 256, 1024), BF16),
            pltpu.VMEM((2, 512, 512), BF16),
            pltpu.VMEM((5, 16, 32, 1024), BF16),
            pltpu.SemaphoreType.DMA((11, 2)),
        ],
        compiler_params=pltpu.CompilerParams(vmem_limit_bytes=56 * MIB),
        cost_estimate=pl.CostEstimate(flops=3 * 10**9, bytes_accessed=12 * MIB, transcendentals=0),
        name="wide_grads",
    )(at, l_own, d_own, d_oth)


def down_grads(at, z_own, f_own, z_oth):
    return pl.pallas_call(
        down_kernel,
        in_specs=[SMEM, ANY, ANY, ANY],
        out_specs=[ANY, ANY],
        out_shape=[pltpu.HBM((2, 4, 128, 1024), BF16)] * 2,
        scratch_shapes=[
            pltpu.VMEM((2, 2, 256, 1024), BF16),
            pltpu.VMEM((2, 256, 1024), BF16),
            pltpu.VMEM((4, 4, 128, 1024), BF16),
            pltpu.SemaphoreType.DMA((7, 2)),
        ],
        compiler_params=pltpu.CompilerParams(vmem_limit_bytes=56 * MIB),
        cost_estimate=pl.CostEstimate(flops=3 * 10**9, bytes_accessed=10 * MIB, transcendentals=0),
        name="down_grads",
    )(at, z_own, f_own, z_oth)


def token_layer(at, pieces_a, pieces_b, context, tokens, cotangent, vectors, ffb):
    return pl.pallas_call(
        token_kernel,
        in_specs=[SMEM] + [ANY] * 8 + [VMEM] * 5,
        out_specs=[VMEM] + [ANY] * 4 + [VMEM] * 4,
        out_shape=[
            jax.ShapeDtypeStruct((256, 1024), BF16),
            pltpu.HBM((6, 256, 1024), BF16),
            pltpu.HBM((256, 1024), BF16),
            pltpu.HBM((3, 256, 1024), BF16),
            pltpu.HBM((2, 256, 1024), BF16),
            jax.ShapeDtypeStruct((256, 1024), F32),
            jax.ShapeDtypeStruct((4, 256, 256), BF16),
            jax.ShapeDtypeStruct((8, 1024), F32),
            jax.ShapeDtypeStruct((1, 4096), F32),
        ],
        scratch_shapes=[
            pltpu.VMEM((5, 1024, 1024), BF16),
            pltpu.VMEM((4096, 1024), BF16),
            pltpu.VMEM((4, 256, 1024), F32),
            pltpu.VMEM((4, 256, 1024), BF16),
            pltpu.VMEM((4, 256, 1024), BF16),
            pltpu.VMEM((4, 256, 1024), BF16),
            pltpu.VMEM((256, 1024), F32),
            pltpu.VMEM((256, 1024), F32),
            pltpu.VMEM((256, 1), F32),
            pltpu.VMEM((256, 1024), F32),
            pltpu.VMEM((256, 1024), F32),
            pltpu.VMEM((256, 1024), F32),
            pltpu.VMEM((1024, 256), BF16),
            pltpu.VMEM((2, 256, 1024), BF16),
            pltpu.VMEM((2, 2, 256, 1024), BF16),
            pltpu.SemaphoreType.DMA((16,)),
        ],
        compiler_params=pltpu.CompilerParams(vmem_limit_bytes=60 * MIB),
        cost_estimate=pl.CostEstimate(flops=10 * 10**9, bytes_accessed=30 * MIB, transcendentals=2 * MIB),
        name="token_layer",
    )(at, *pieces_a, *pieces_b, context, tokens, cotangent, vectors, ffb)


def lamb_kernel(squares_ref, *refs):
    factor = CLIP_NORM / jnp.maximum(jnp.sqrt(jnp.sum(squares_ref[...], axis=0)[:, :1]), CLIP_NORM)
    for i in range(7):
        weight, grad = refs[i][...], refs[7 + i][...] * factor
        new_first = BETA_ONE * refs[14 + i][...] + (1.0 - BETA_ONE) * grad
        new_second = BETA_TWO * refs[21 + i][...] + (1.0 - BETA_TWO) * grad * grad
        direction = (
            new_first
            / (1.0 - BETA_ONE**STEP_COUNT)
            / (jnp.sqrt(new_second / (1.0 - BETA_TWO**STEP_COUNT)) + ADAM_EPS)
            + WEIGHT_DECAY * weight
        )
        weight_norm = jnp.sqrt(jnp.sum(weight * weight, keepdims=True))
        dir_norm = jnp.sqrt(jnp.sum(direction * direction, keepdims=True))
        refs[28 + i][...] = direction * (weight_norm / jnp.maximum(dir_norm, 1.0))


def lamb_steps(squares, weights, grads, firsts, seconds):
    return pl.pallas_call(
        lamb_kernel,
        in_specs=[VMEM] * 29,
        out_specs=[VMEM] * 7,
        out_shape=[jax.ShapeDtypeStruct(weight.shape, F32) for weight in weights],
        name="lamb",
    )(squares, *weights, *grads, *firsts, *seconds)


def body(tokens, cotangent, doc_lengths, *params):

    def turned(arrays):
        return (*arrays[:4], arrays[4].T, arrays[5], arrays[6].reshape(1, 32))

    shards, firsts, seconds = turned(params[:7]), turned(params[7:14]), turned(params[14:])
    dp_index = lax.axis_index("dp")
    z_at, y_at, core, x_at = dp_index // 8, dp_index // 2 % 4, dp_index % 2, lax.axis_index("group")
    at = jnp.stack([z_at, y_at, core, x_at]).astype(jnp.int32)

    with jax.named_scope("gather_x"):
        pack = packed_rows(shards)
        pack = rolled([pack[None]] + [push(pack, "x", -j)[None] for j in (1, 2, 3)], x_at, 0)
        own = lax.dynamic_slice_in_dim(pack[:, 72:96], x_at * 256, 256, axis=2)
        own = own.reshape(4, 3, 8, 256).transpose(0, 2, 1, 3).reshape(4, 8, 768)
        own = jnp.concatenate([own, pack[:, 96:, :256]], axis=2)
        part_a = pack[:, :40].reshape(4, 5, 8, 1024).transpose(1, 0, 2, 3).reshape(1, 5, 32, 1024)
        part_b = jnp.concatenate([pack[:, 40:72].reshape(1, 4, 32, 1024), own.reshape(1, 1, 32, 1024)], axis=1)

    with jax.named_scope("gather_tokens"):
        toks = [tokens, push(tokens, "x", -1), tokens, push(tokens, "x", -3)]

    with jax.named_scope("visible"):
        order = (x_at + jnp.arange(4, dtype=jnp.int32)) % 4
        positions = (order[:, None] * 256 + jnp.arange(256, dtype=jnp.int32)[None]).reshape(1024)
        ends = [doc_lengths[0, 0], doc_lengths[0, 0] + doc_lengths[0, 1]]
        ends.append(ends[1] + doc_lengths[0, 2])
        ids = sum((positions >= end).astype(jnp.int32) for end in ends)
        code = (positions + 4096 * ids).astype(F32)
        code_col, code_row = code[:, None], code[None]

    with jax.named_scope("gather_yz"):
        part_a, part_b = doubled(part_a, "z", 0), doubled(part_b, "y", 0)
        part_a, part_b = doubled(part_a, "z", 1), doubled(part_b, "y", 1)
        part_a, part_b, *toks = lax.optimization_barrier((part_a, part_b, *toks))
        toks[2] = push(toks[2], "x", -2)
        part_b, w_own = part_b[:, :4].reshape(4, 128, 1024), part_b[:, 4]
        w_own = doubled(w_own, "z", 0)
        part_a, part_b, at, code_col, code_row = lax.optimization_barrier((part_a, part_b, at, code_col, code_row))
        w_own = doubled(w_own, "z", 1)
        part_a, part_b = doubled(part_a, "y", 0), doubled(part_b, "z", 0)
        w_own, toks[2] = lax.optimization_barrier((w_own, toks[2]))
        w_other = push(w_own, "core", 1)
        far_a, far_b = swap(part_a, "y", 1), swap(part_b, "z", 1)

    with jax.named_scope("attention"):
        qkv, vectors, out_all, lse, w_in = attend(at, w_own, w_other, toks, code_col, code_row)
        other_b = push(part_b, "core", 1)
        part_a, other_b, out_all = lax.optimization_barrier((part_a, other_b, out_all))
        other_a = push(part_a, "core", 1)
        context = lax.all_to_all(out_all, "group", 0, 0, tiled=True)
        ffb = vectors[8:12].reshape(4, 128, 8).transpose(1, 0, 2).reshape(1, 4096)

    with jax.named_scope("gather_ff"):
        far_a, far_b, context = lax.optimization_barrier((far_a, far_b, context))
        pieces_a = (part_a, far_a, other_a, push(far_a, "core", 1))
        pieces_b = (part_b, far_b, other_b, push(far_b, "core", 1))

    with jax.named_scope("tokens"):
        block_out, dx, lx, zg, zo, d_one, d_context, small, d_ffb = token_layer(
            at, pieces_a, pieces_b, context, tokens, cotangent, vectors, ffb
        )

    with jax.named_scope("scatter_ff"):
        dx_other, zg_other = push(dx, "core", 1), push(zg, "core", 1)
        keep_a, sent_a = wide_grads(at, lx, dx, dx_other)
        sent_a, zg_other, small, d_ffb = lax.optimization_barrier((sent_a, zg_other, small, d_ffb))
        got_a = swap(sent_a, "z", 0)
        keep_b, sent_b = down_grads(at, zo, zg, zg_other)
        ffb_rows = d_ffb.reshape(128, 4, 8).transpose(1, 0, 2).reshape(4, 1024)
        small = jnp.concatenate([small, ffb_rows, jnp.zeros((4, 1024), F32)], axis=0)

    with jax.named_scope("attention_back"):
        d_all = lax.all_to_all(d_context, "group", 0, 0, tiled=True)
        d_all, sent_b = lax.optimization_barrier((d_all, sent_b))

    with jax.named_scope("scatter_ff"):
        terms_b, terms_a = [keep_b, swap(sent_b, "y", 0)], [keep_a, got_a]
        sent_b, sent_a = outgoing(terms_b), outgoing(terms_a)

    with jax.named_scope("attention_back"):
        keep_in, give_in, d_qkv = attend_back(at, toks, qkv, d_all, code_col, code_row, lse, small)

    with jax.named_scope("scatter_attn_in"):
        terms_in = [keep_in, push(give_in, "core", 1)]
        terms_in = step_down(terms_in, outgoing(terms_in), "y", 0)
        backs, terms_in[-1] = lax.optimization_barrier((input_back(at, d_qkv, w_in), terms_in[-1]))

    with jax.named_scope("input_grad"):
        backs = lax.all_to_all(backs, "group", 0, 0, tiled=True)

    with jax.named_scope("scatter_ff"):
        for axis_b, axis_a, axis_in, step in (("y", "z", "y", 1), ("z", "y", "z", 0), ("z", "y", "z", 1)):
            if axis_b == "z":
                terms_b, terms_a, terms_in = lax.optimization_barrier((terms_b, terms_a, terms_in))
                sent_b, sent_a = outgoing(terms_b), outgoing(terms_a)
            terms_b, terms_a = step_down(terms_b, sent_b, axis_b, step), step_down(terms_a, sent_a, axis_a, step)
            terms_in = step_down(terms_in, outgoing(terms_in), axis_in, step)
        sum_b, sum_a, sum_in = (sum(term.astype(F32) for term in terms) for terms in (terms_b, terms_a, terms_in))
        sum_in = sum_in.reshape(4, 8, 896)
        pack = jnp.concatenate(
            [
                sum_a.reshape(5, 4, 8, 1024).transpose(1, 0, 2, 3).reshape(4, 40, 1024),
                sum_b.reshape(4, 32, 1024),
                jnp.concatenate([sum_in, jnp.zeros((4, 8, 128), F32)], axis=2),
            ],
            axis=1,
        )
        parts = [pick(pack, x_at, 0)]
        parts += [push(pick(pack, (x_at + 4 - j) % 4, 0).astype(BF16), "x", -j) for j in (1, 2, 3)]
        *grads, squares = finished(at, parts)

    with jax.named_scope("input_grad"):
        input_grad = d_one + jnp.sum(backs.astype(F32), axis=0)

    with jax.named_scope("norm"):
        squares = lax.all_to_all(squares, AXES, 0, 0, tiled=True)
    with jax.named_scope("lamb"):
        steps = lamb_steps(squares, shards, grads, firsts, seconds)

    def restored(arrays):
        return (*arrays[:4], arrays[4].T, arrays[5], arrays[6].reshape(32))

    return (block_out, input_grad, *restored(grads), *restored(steps))


def solution(mesh):
    rows, vector, docs = P(AXES, None), P(AXES), P("dp", None)
    leaves = (rows,) * 6 + (vector,)
    return jax.shard_map(
        body,
        mesh=mesh,
        in_specs=(rows, rows, docs) + leaves * 3,
        out_specs=(rows, rows) + leaves * 2,
        check_vma=False,
    )
```

```python
import jax
import jax.numpy as jnp
import numpy as np
from jax import lax
from jax.experimental import pallas as pl
from jax.experimental.pallas import tpu as pltpu
from jax.sharding import PartitionSpec as P

HEADS = 16
WINDOW = 1024
AXES = ("dp", "group")
RADIX = {"z": 4, "y": 4, "core": 2, "x": 4}

NORM_EPS = 1e-06
CLIP_NORM = 1.0
BETA_ONE = 0.9
BETA_TWO = 0.999
STEP_COUNT = 10
ADAM_EPS = 1e-06
WEIGHT_DECAY = 0.01
MASKED_SCORE = -1e30
F32 = jnp.float32
BF16 = jnp.bfloat16


def flat_of(at):
    return ((at["z"] * 4 + at["y"]) * 2 + at["core"]) * 4 + at["x"]


def device_pairs(move):
    out = []
    for flat in range(128):
        at = {"z": flat // 32, "y": flat // 8 % 4, "core": flat // 4 % 2, "x": flat % 4}
        move(at)
        out.append((flat, flat_of(at)))
    return out


def push(value, axis, shift):
    def move(at):
        at[axis] = (at[axis] + shift) % RADIX[axis]

    return lax.ppermute(value, AXES, device_pairs(move))


def swap(value, axis, step):
    def move(at):
        at[axis] ^= (1, 3)[(at["core"] + step) % 2]

    return lax.ppermute(value, AXES, device_pairs(move))


def spread(value, axes):
    names = ("z", "y", "core", "x")
    order = [name for name in names if name not in axes] + list(axes)
    grid = np.arange(128).reshape(4, 4, 2, 4).transpose([names.index(name) for name in order])
    groups = grid.reshape(-1, value.shape[0]).tolist()
    return lax.all_to_all(value, AXES, 0, 0, axis_index_groups=groups, tiled=True)


def pick(value, index, dim):
    return lax.dynamic_index_in_dim(value, index, dim, keepdims=False)


def rolled(parts, me, dim):
    joined = jnp.concatenate(parts + parts[:3], axis=dim)
    width = parts[0].shape[dim]
    return lax.dynamic_slice_in_dim(joined, (4 - me) % 4 * width, 4 * width, dim)


def doubled(value, axis, step):
    return jnp.concatenate([value, swap(value, axis, step)], axis=0)


def outgoing(terms):
    half = terms[0].shape[0] // 2
    return sum(term[half:].astype(F32) for term in terms).astype(BF16)


def step_down(terms, sent, axis, step):
    half = terms[0].shape[0] // 2
    terms = [term[:half] for term in terms] + [swap(sent, axis, step)]
    if half == 1:
        terms = [term[0] for term in terms]
    return terms


def masks(core, owner_is_other):
    one = core * 2 + 1
    two = 3 - core * 2
    return (two, one) if owner_is_other else (one, two)


def dot_nn(a, b):
    return jnp.dot(a, b, preferred_element_type=F32)


def dot_nt(a, b):
    return lax.dot_general(a, b, (((1,), (1,)), ((), ())), preferred_element_type=F32)


def dot_tn(a, b):
    return lax.dot_general(a, b, (((0,), (0,)), ((), ())), preferred_element_type=F32)


def xor2(me, bit_one, bit_two, pair):
    value = me
    if bit_one:
        value = value ^ pair[0]
    if bit_two:
        value = value ^ pair[1]
    return value


def unrolled(count):
    def run(part):
        for index in range(count):
            part(index)

    return run


def set_mask(mask_ref, col_ref, row_ref):
    @unrolled(8)
    def _(chunk):
        rows = slice(chunk * 128, chunk * 128 + 128)
        near = jnp.abs(col_ref[rows, :] - row_ref[...]) < WINDOW // 2
        mask_ref[rows, :] = jnp.where(near, 0.0, MASKED_SCORE)


def attend_kernel(
    at_ref, own_ref, other_ref, t0, t1, t2, t3, col_ref, row_ref,
    qkv_ref, vec_ref, out_ref, lse_ref, w_ref, mask_ref, turn_ref,
):
    z_at, y_at, core, x_at = at_ref[0], at_ref[1], at_ref[2], at_ref[3]
    for side, src in ((0, own_ref), (1, other_ref)):
        pair = masks(core, side == 1)
        for block in range(16):
            y = xor2(y_at, block & 1, block >> 1 & 1, pair)
            z = xor2(z_at, block >> 2 & 1, block >> 3 & 1, pair)
            row = pl.multiple_of(((z * 4 + y) * 2 + (core ^ side)) * 32, 32)
            w_ref[pl.ds(row, 32), :] = src[block]
    vec_ref[...] = w_ref[:, 768:896].astype(F32).T[:16]
    lanes = pl.ds(pl.multiple_of(x_at * 256, 256), 256)
    bias = jnp.concatenate([vec_ref[2:3, lanes], jnp.zeros((1, 256), F32), vec_ref[3:4, lanes]], axis=1)
    for j, tok in enumerate((t0, t1, t2, t3)):
        qkv_ref[j * 256 : j * 256 + 256, :] = (dot_nn(tok[...], w_ref[:, :768]) + bias).astype(BF16)
    set_mask(mask_ref, col_ref, row_ref)
    turn_ref[...] = qkv_ref[:, 512:768].T
    outs = []
    for head in range(4):
        lanes = slice(head * 64, head * 64 + 64)
        key = qkv_ref[:, 256 + head * 64 : 320 + head * 64]
        scores = dot_nt(key, qkv_ref[:, lanes] * BF16(0.125)) + mask_ref[...]
        top = jnp.max(scores, axis=0, keepdims=True)
        raised = jnp.exp(scores - top)
        total = jnp.sum(raised, axis=0, keepdims=True)
        probs = (raised * (1.0 / total)).astype(BF16)
        outs.append(dot_nn(turn_ref[lanes, :], probs))
        lse_ref[head : head + 1, :] = jnp.log(total) + top
    out = jnp.concatenate(outs, axis=0).T.astype(BF16)
    for block in range(4):
        out_ref[(x_at + block) % 4] = out[block * 256 : block * 256 + 256]


def attend_back_kernel(
    at_ref, t0, t1, t2, t3, qkv_ref, d_ref, col_ref, row_ref, lse_ref, small_ref,
    keep_ref, give_ref, dqkv_ref, d_rows, rows_ref, mask_ref, turn_ref, joined_ref, tok_ref, sem,
):
    z_at, y_at, core, x_at = at_ref[0], at_ref[1], at_ref[2], at_ref[3]
    copies = [pltpu.make_async_copy(src, tok_ref.at[i], sem.at[i]) for i, src in enumerate((t0, t1, t2, t3))]
    for copy in copies:
        copy.start()
    set_mask(mask_ref, col_ref, row_ref)
    turn_ref[...] = qkv_ref[:, 256:512].T
    for block in range(4):
        d_rows[block * 256 : block * 256 + 256, :] = d_ref[(x_at + block) % 4]
    outs = []
    for head in range(4):
        lanes = slice(head * 64, head * 64 + 64)
        key = qkv_ref[:, 256 + head * 64 : 320 + head * 64]
        value = qkv_ref[:, 512 + head * 64 : 576 + head * 64]
        query = qkv_ref[:, lanes] * BF16(0.125)
        d_out = d_rows[:, lanes]
        probs = jnp.exp(dot_nt(key, query) + mask_ref[...] - lse_ref[head : head + 1, :])
        d_probs = dot_nt(value, d_out)
        delta = jnp.sum(probs * d_probs, axis=0, keepdims=True)
        d_scores = (probs * (d_probs - delta)).astype(BF16)
        outs.append(dot_nn(turn_ref[lanes, :], d_scores) * 0.125)
        dqkv_ref[:, 256 + head * 64 : 320 + head * 64] = dot_nn(d_scores, query).astype(BF16)
        dqkv_ref[:, 512 + head * 64 : 576 + head * 64] = dot_nn(probs.astype(BF16), d_out).astype(BF16)
    dqkv_ref[:, :256] = jnp.concatenate(outs, axis=0).T.astype(BF16)
    rows_ref[...] = jnp.zeros_like(rows_ref)
    rows_ref[:16, :] = small_ref[...]
    lanes = pl.ds(pl.multiple_of(x_at * 256, 256), 256)
    sums = jnp.sum(dqkv_ref[...].astype(F32), axis=0, keepdims=True)
    rows_ref[2:3, lanes] = sums[:, :256]
    rows_ref[3:4, lanes] = sums[:, 512:]
    joined_ref[:, :, :, 768:896] = rows_ref[...].T.astype(BF16).reshape(16, 2, 32, 128)
    for copy in copies:
        copy.wait()
    total = dot_tn(tok_ref[0], dqkv_ref[:256, :])
    for block in (1, 2, 3):
        total = total + dot_tn(tok_ref[block], dqkv_ref[block * 256 : block * 256 + 256, :])
    joined_ref[:, :, :, :768] = total.astype(BF16).reshape(16, 2, 32, 768)
    for side, dst in ((0, keep_ref), (1, give_ref)):
        pair = masks(core, side == 1)
        for block in range(16):
            y = xor2(y_at, block >> 3 & 1, block >> 2 & 1, pair)
            z = xor2(z_at, block >> 1 & 1, block & 1, pair)
            dst[block] = joined_ref[z * 4 + y, core ^ side]


def back_kernel(at_ref, dqkv_ref, w_ref, back_ref):
    x_at = at_ref[3]
    for block in range(4):
        back = dot_nt(dqkv_ref[block * 256 : block * 256 + 256, :], w_ref[:, :768])
        back_ref[(x_at + block) % 4] = back.astype(BF16)


GELU_IN = 0.7978845608028654
GELU_CUBE = 0.044715


def norm_forward(value):
    center = value - jnp.mean(value, axis=-1, keepdims=True)
    spread = lax.rsqrt(jnp.mean(center * center, axis=-1, keepdims=True) + NORM_EPS)
    return center * spread, spread


def norm_back(d_normal, normal, spread):
    return spread * (
        d_normal
        - jnp.mean(d_normal, axis=-1, keepdims=True)
        - normal * jnp.mean(d_normal * normal, axis=-1, keepdims=True)
    )


def column_sum(value):
    return jnp.sum(value, axis=0, keepdims=True)


def token_kernel(
    at_ref, a0, a1, a2, a3, e0, e1, e2, e3, ctx_ref, tok_ref, cot_ref, vec_ref, ffb_ref,
    out_ref, dx_ref, lx_ref, zg_ref, zo_ref, done_ref, dctx_ref, small_ref, dffb_ref,
    w5, wd, hid, act, d_act, kept, hf, n_one, r_one, d_two, d_first, d_hid, turn, rows_out, z_out, sem,
):
    z_at, y_at, core = at_ref[0], at_ref[1], at_ref[2]
    pairs = [masks(core, False), masks(core, True)]
    for parts, slot in ((pl.ds(4, 1), 0), *((pl.ds(cb, 1), 2 + cb) for cb in range(4))):
        for late, side, src in ((0, 0, a0), (1, 0, a1), (0, 1, a2), (1, 1, a3)):
            for block in range(8):
                y = xor2(y_at, block >> 2 & 1, late, pairs[side])
                z = xor2(z_at, block & 1, block >> 1 & 1, pairs[side])
                row = pl.multiple_of(((z * 4 + y) * 2 + (core ^ side)) * 32, 32)
                pltpu.make_async_copy(src.at[block, parts], w5.at[parts, pl.ds(row, 32), :], sem.at[slot]).start()
    for late, side, src in ((0, 0, e0), (1, 0, e1), (0, 1, e2), (1, 1, e3)):
        for block in range(8):
            z = xor2(z_at, block >> 2 & 1, late, pairs[side])
            y = xor2(y_at, block & 1, block >> 1 & 1, pairs[side])
            row = pl.multiple_of(((z * 4 + y) * 2 + (core ^ side)) * 128, 128)
            pltpu.make_async_copy(src.at[block], wd.at[pl.ds(row, 128), :], sem.at[1]).start()

    outs = {}

    def out(name, src, dst):
        outs[name] = pltpu.make_async_copy(src, dst, sem.at[6 + len(outs)])
        outs[name].start()

    def select_rows(lanes):
        for side in range(2):
            for block in range(16):
                z = xor2(z_at, block >> 3 & 1, block >> 2 & 1, pairs[side])
                y = xor2(y_at, block >> 1 & 1, block & 1, pairs[side])
                row = pl.multiple_of(((z * 4 + y) * 2 + (core ^ side)) * 32, 32)
                to, at_lane = block % 8 * 32, lanes + block // 8 * 256
                rows_out[side, to : to + 32, at_lane : at_lane + 256] = turn[pl.ds(row, 32), :]

    for part in range(4):
        kept[3, :, part * 256 : part * 256 + 256] = ctx_ref[part]
    turn[...] = kept[3].T
    select_rows(512)
    pltpu.make_async_copy(w5.at[pl.ds(4, 1)], w5.at[pl.ds(4, 1)], sem.at[0]).wait()
    attended = vec_ref[4:5, :]
    for part in range(4):
        attended = attended + dot_nn(ctx_ref[part], w5[4, part * 256 : part * 256 + 256, :])
    normal, spread = norm_forward(tok_ref[...].astype(F32) + attended)
    n_one[...] = normal
    r_one[...] = spread
    hf[...] = normal * vec_ref[0:1, :] + vec_ref[5:6, :]
    kept[2] = hf[...].astype(BF16)
    turn[...] = kept[2].T
    select_rows(0)
    out("l_own", rows_out.at[0], lx_ref)
    out("l_give", rows_out.at[1], dx_ref.at[5])

    @unrolled(4)
    def _(cb):
        cols = slice(cb * 1024, cb * 1024 + 1024)
        part = w5.at[pl.ds(cb, 1)]
        pltpu.make_async_copy(part, part, sem.at[2 + cb]).wait()
        hid[cb] = dot_nn(kept[2], w5[cb]) + ffb_ref[:, cols]

        @unrolled(8)
        def _(chunk):
            rows = slice(chunk * 32, chunk * 32 + 32)
            u = hid[cb, rows, :]
            t = jnp.tanh(GELU_IN * (u + GELU_CUBE * (u * u * u)))
            act[cb, rows, :] = (u * (0.5 * (1.0 + t))).astype(BF16)

        for side in range(2):
            for block in range(4):
                y = xor2(y_at, block >> 1, block & 1, pairs[side])
                lanes = pl.ds(pl.multiple_of((y * 2 + (core ^ side)) * 128, 128), 128)
                to = cb % 2 * 512 + block * 128
                z_out[side, cb // 2, :, to : to + 128] = act[cb, :, lanes]

    pltpu.make_async_copy(wd, wd, sem.at[1]).wait()
    d_first[...] = hf[...] + vec_ref[6:7, :]

    @unrolled(4)
    def _(cb):
        d_first[...] += dot_nn(act[cb], wd[slice(cb * 1024, cb * 1024 + 1024), :])

    normal, spread = norm_forward(d_first[...])
    out_ref[...] = (normal * vec_ref[1:2, :] + vec_ref[7:8, :]).astype(BF16)
    cot = cot_ref[...].astype(F32)
    small_ref[...] = jnp.zeros_like(small_ref)
    small_ref[1:2, :] = column_sum(cot * normal)
    small_ref[7:8, :] = column_sum(cot)
    d_two[...] = norm_back(cot * vec_ref[1:2, :], normal, spread)
    out("z_own", z_out.at[0], zo_ref)
    out("z_give", z_out.at[1], zg_ref.at[pl.ds(0, 2)])
    kept[1] = d_two[...].astype(BF16)
    out("d_f", kept.at[1], zg_ref.at[2])
    small_ref[6:7, :] = column_sum(kept[1].astype(F32))
    d_first[...] = d_two[...]

    @unrolled(4)
    def _(cb):
        cols = slice(cb * 1024, cb * 1024 + 1024)
        d_hid[...] = dot_nt(kept[1], wd[cols, :])
        dffb_ref[:, cols] = jnp.zeros((1, 1024), F32)

        @unrolled(8)
        def _(chunk):
            rows = slice(chunk * 32, chunk * 32 + 32)
            u = hid[cb, rows, :]
            square = u * u
            t = jnp.tanh(GELU_IN * (u + GELU_CUBE * (square * u)))
            slope = 0.5 * (1.0 + t) + (0.5 * GELU_IN) * u * (1.0 - t * t) * (1.0 + (3.0 * GELU_CUBE) * square)
            d_low = (d_hid[rows, :] * slope).astype(BF16)
            d_act[cb, rows, :] = d_low
            dffb_ref[:, cols] += column_sum(d_low.astype(F32))

        out(cb, d_act.at[cb], dx_ref.at[cb])
        d_first[...] += dot_nt(d_act[cb], w5[cb])

    d_h = d_first[...]
    normal = n_one[...]
    small_ref[0:1, :] = column_sum(d_h * normal)
    small_ref[5:6, :] = column_sum(d_h)
    d_one = norm_back(d_h * vec_ref[0:1, :], normal, r_one[...])
    done_ref[...] = d_one
    kept[0] = d_one.astype(BF16)
    out("d_a", kept.at[0], dx_ref.at[4])
    small_ref[4:5, :] = column_sum(kept[0].astype(F32))
    for part in range(4):
        dctx_ref[part] = dot_nt(kept[0], w5[4, part * 256 : part * 256 + 256, :]).astype(BF16)
    for copy in outs.values():
        copy.wait()


def wide_kernel(at_ref, l_own, d_own, d_oth, a0_ref, a1_ref, acts, packed, left, stage, sem):
    loads = [
        [pltpu.make_async_copy(l_own, packed.at[0], sem.at[0, 0]), pltpu.make_async_copy(d_oth.at[5], packed.at[1], sem.at[0, 1])]
    ]
    for part in range(5):
        loads.append(
            [
                pltpu.make_async_copy(src.at[part], acts.at[part, side], sem.at[1 + part, side])
                for side, src in ((0, d_own), (1, d_oth))
            ]
        )
    for group in loads:
        for copy in group:
            copy.start()

    def out(part):
        return [
            pltpu.make_async_copy(stage.at[part, pl.ds(half * 8, 8)], dst.at[:, part], sem.at[6 + part, half])
            for half, dst in ((0, a0_ref), (1, a1_ref))
        ]

    for copy in loads[0]:
        copy.wait()
    for kind in range(2):
        for rows in range(2):
            for side in range(2):
                lanes = kind * 512 + rows * 256
                left[kind, rows * 256 : rows * 256 + 256, side * 256 : side * 256 + 256] = packed[side, :, lanes : lanes + 256]
    for part in range(5):
        for copy in loads[1 + part]:
            copy.wait()
        grad = dot_nn(left[part // 4], acts[part].reshape(512, 1024))
        stage[part] = grad.astype(BF16).reshape(16, 32, 1024)
        for copy in out(part):
            copy.start()
    for part in range(5):
        for copy in out(part):
            copy.wait()


def down_kernel(at_ref, z_own, f_own, z_oth, b0_ref, b1_ref, zs, fs, stage, sem):
    z_at, core = at_ref[0], at_ref[2]
    one, two = masks(core, False)
    loads = [
        [pltpu.make_async_copy(src.at[2], fs.at[side], sem.at[0, side]) for side, src in ((0, f_own), (1, z_oth))]
    ]
    for half in range(2):
        loads.append(
            [
                pltpu.make_async_copy(src.at[half], zs.at[half, side], sem.at[1 + half, side])
                for side, src in ((0, z_own), (1, z_oth))
            ]
        )
    for group in loads:
        for copy in group:
            copy.start()

    def place(z):
        gap = z ^ z_at
        both = (gap == 2).astype(jnp.int32)
        return ((gap == one).astype(jnp.int32) + both) * 2 + (gap == two).astype(jnp.int32) + both

    def out(z):
        return [
            pltpu.make_async_copy(stage.at[z, pl.ds(half * 2, 2)], dst.at[:, place(z)], sem.at[3 + z, half])
            for half, dst in ((0, b0_ref), (1, b1_ref))
        ]

    for copy in loads[0]:
        copy.wait()
    for z in range(4):
        if z % 2 == 0:
            for copy in loads[1 + z // 2]:
                copy.wait()
        picked = zs[z // 2, :, :, z % 2 * 512 : z % 2 * 512 + 512].reshape(512, 512)
        stage[z] = dot_tn(picked, fs[...].reshape(512, 1024)).astype(BF16).reshape(4, 128, 1024)
        for copy in out(z):
            copy.start()
    for z in range(4):
        for copy in out(z):
            copy.wait()


SMEM = pl.BlockSpec(memory_space=pltpu.SMEM)
VMEM = pl.BlockSpec(memory_space=pltpu.VMEM)
ANY = pl.BlockSpec(memory_space=pl.ANY)
MIB = 2**20


def pack_kernel(up_ref, out_ref, down_ref, in_ref, gains_ref, bias_ref, ffb_ref, pack_ref, rows, square):
    for cb in range(4):
        rows[cb * 8 : cb * 8 + 8, :] = up_ref[:, cb * 1024 : cb * 1024 + 1024]
    rows[32:40, :] = out_ref[...]
    rows[40:72, :] = down_ref[...]
    for cb in range(3):
        rows[72 + cb * 8 : 80 + cb * 8, :] = in_ref[:, cb * 1024 : cb * 1024 + 1024]
    square[...] = jnp.zeros_like(square)
    square[0:2, :8] = gains_ref[...]
    for j in range(4):
        square[8 + j : 9 + j, :8] = ffb_ref[:, j * 8 : j * 8 + 8]
    rows[96:104, :] = jnp.zeros((8, 1024), F32)
    rows[96:104, :128] = square[...].T[:8]
    rows[96:104, 2:8] = bias_ref[...]
    pack_ref[...] = rows[...].astype(BF16)


def packed_rows(arrays):
    return pl.pallas_call(
        pack_kernel,
        in_specs=[VMEM] * 7,
        out_specs=VMEM,
        out_shape=jax.ShapeDtypeStruct((104, 1024), BF16),
        scratch_shapes=[pltpu.VMEM((104, 1024), F32), pltpu.VMEM((128, 128), F32)],
        name="pack_rows",
    )(arrays[2], arrays[1], arrays[3], arrays[0], *arrays[4:])


def finish_kernel(at_ref, p0, p1, p2, p3, in_ref, out_ref, up_ref, down_ref, gains_ref, bias_ref, ffb_ref, sq_ref, square):
    x_at = at_ref[3]
    parts = [ref[...].astype(F32) for ref in (p0, p1, p2, p3)]
    total = parts[0][:72] + parts[1][:72] + parts[2][:72] + parts[3][:72]
    for cb in range(4):
        up_ref[:, cb * 1024 : cb * 1024 + 1024] = total[cb * 8 : cb * 8 + 8]
    out_ref[...] = total[32:40]
    down_ref[...] = total[40:72]
    extra = jnp.zeros((8, 128), F32)
    squares = jnp.sum(total * total, keepdims=True)
    for j, part in enumerate(parts):
        rows = part[72:80]
        group = (x_at + j) % 4
        for block in range(3):
            cols = pl.ds(pl.multiple_of(block * 1024 + group * 256, 256), 256)
            in_ref[:, cols] = rows[:, block * 256 : block * 256 + 256]
        squares = squares + jnp.sum(rows[:, :768] * rows[:, :768], keepdims=True)
        extra = extra + rows[:, 768:896]
    square[...] = jnp.zeros_like(square)
    square[:8, :] = extra
    turned = square[...].T
    gains_ref[...] = turned[0:2, :8]
    bias_ref[...] = extra[:, 2:8]
    for j in range(4):
        ffb_ref[:, j * 8 : j * 8 + 8] = turned[8 + j : 9 + j, :8]
    squares = squares + jnp.sum(turned[:12] * turned[:12], keepdims=True)
    sq_ref[...] = jnp.broadcast_to(squares[None], sq_ref.shape)


def finished(at, parts):
    shapes = [(8, 3072), (8, 1024), (8, 4096), (32, 1024), (2, 8), (8, 6), (1, 32), (128, 1, 128)]
    return pl.pallas_call(
        finish_kernel,
        in_specs=[SMEM] + [VMEM] * 4,
        out_specs=[VMEM] * 8,
        out_shape=[jax.ShapeDtypeStruct(shape, F32) for shape in shapes],
        scratch_shapes=[pltpu.VMEM((128, 128), F32)],
        name="finish",
    )(at, *parts)


def attend(at, w_own, w_other, toks, code_col, code_row):
    return pl.pallas_call(
        attend_kernel,
        in_specs=[SMEM] + [VMEM] * 8,
        out_specs=[VMEM] * 5,
        out_shape=[
            jax.ShapeDtypeStruct((1024, 768), BF16),
            jax.ShapeDtypeStruct((16, 1024), F32),
            jax.ShapeDtypeStruct((4, 256, 256), BF16),
            jax.ShapeDtypeStruct((4, 1024), F32),
            jax.ShapeDtypeStruct((1024, 1024), BF16),
        ],
        scratch_shapes=[
            pltpu.VMEM((1024, 1024), F32),
            pltpu.VMEM((256, 1024), BF16),
        ],
        compiler_params=pltpu.CompilerParams(vmem_limit_bytes=56 * MIB),
        cost_estimate=pl.CostEstimate(flops=13 * 10**9, bytes_accessed=9 * MIB, transcendentals=4 * MIB),
        name="attend",
    )(at, w_own, w_other, *toks, code_col, code_row)


def input_back(at, d_qkv, w_in):
    return pl.pallas_call(
        back_kernel,
        in_specs=[SMEM, VMEM, VMEM],
        out_specs=VMEM,
        out_shape=jax.ShapeDtypeStruct((4, 256, 1024), BF16),
        compiler_params=pltpu.CompilerParams(vmem_limit_bytes=24 * MIB),
        cost_estimate=pl.CostEstimate(flops=2 * 10**9, bytes_accessed=6 * MIB, transcendentals=0),
        name="input_back",
    )(at, d_qkv, w_in)


def attend_back(at, toks, qkv, d_all, code_col, code_row, lse, small):
    return pl.pallas_call(
        attend_back_kernel,
        in_specs=[SMEM] + [ANY] * 4 + [VMEM] * 6,
        out_specs=[VMEM] * 3,
        out_shape=[jax.ShapeDtypeStruct((16, 32, 896), BF16)] * 2 + [jax.ShapeDtypeStruct((1024, 768), BF16)],
        scratch_shapes=[
            pltpu.VMEM((1024, 256), BF16),
            pltpu.VMEM((128, 1024), F32),
            pltpu.VMEM((1024, 1024), F32),
            pltpu.VMEM((256, 1024), BF16),
            pltpu.VMEM((16, 2, 32, 896), BF16),
            pltpu.VMEM((4, 256, 1024), BF16),
            pltpu.SemaphoreType.DMA((4,)),
        ],
        compiler_params=pltpu.CompilerParams(vmem_limit_bytes=56 * MIB),
        cost_estimate=pl.CostEstimate(flops=22 * 10**9, bytes_accessed=14 * MIB, transcendentals=4 * MIB),
        name="attend_back",
    )(at, *toks, qkv, d_all, code_col, code_row, lse, small)


def wide_grads(at, l_own, d_own, d_oth):
    return pl.pallas_call(
        wide_kernel,
        in_specs=[SMEM, ANY, ANY, ANY],
        out_specs=[ANY, ANY],
        out_shape=[pltpu.HBM((8, 5, 32, 1024), BF16)] * 2,
        scratch_shapes=[
            pltpu.VMEM((5, 2, 256, 1024), BF16),
            pltpu.VMEM((2, 256, 1024), BF16),
            pltpu.VMEM((2, 512, 512), BF16),
            pltpu.VMEM((5, 16, 32, 1024), BF16),
            pltpu.SemaphoreType.DMA((11, 2)),
        ],
        compiler_params=pltpu.CompilerParams(vmem_limit_bytes=56 * MIB),
        cost_estimate=pl.CostEstimate(flops=3 * 10**9, bytes_accessed=12 * MIB, transcendentals=0),
        name="wide_grads",
    )(at, l_own, d_own, d_oth)


def down_grads(at, z_own, f_own, z_oth):
    return pl.pallas_call(
        down_kernel,
        in_specs=[SMEM, ANY, ANY, ANY],
        out_specs=[ANY, ANY],
        out_shape=[pltpu.HBM((2, 4, 128, 1024), BF16)] * 2,
        scratch_shapes=[
            pltpu.VMEM((2, 2, 256, 1024), BF16),
            pltpu.VMEM((2, 256, 1024), BF16),
            pltpu.VMEM((4, 4, 128, 1024), BF16),
            pltpu.SemaphoreType.DMA((7, 2)),
        ],
        compiler_params=pltpu.CompilerParams(vmem_limit_bytes=56 * MIB),
        cost_estimate=pl.CostEstimate(flops=3 * 10**9, bytes_accessed=10 * MIB, transcendentals=0),
        name="down_grads",
    )(at, z_own, f_own, z_oth)


def token_layer(at, pieces_a, pieces_b, context, tokens, cotangent, vectors, ffb):
    return pl.pallas_call(
        token_kernel,
        in_specs=[SMEM] + [ANY] * 8 + [VMEM] * 5,
        out_specs=[VMEM] + [ANY] * 4 + [VMEM] * 4,
        out_shape=[
            jax.ShapeDtypeStruct((256, 1024), BF16),
            pltpu.HBM((6, 256, 1024), BF16),
            pltpu.HBM((256, 1024), BF16),
            pltpu.HBM((3, 256, 1024), BF16),
            pltpu.HBM((2, 256, 1024), BF16),
            jax.ShapeDtypeStruct((256, 1024), F32),
            jax.ShapeDtypeStruct((4, 256, 256), BF16),
            jax.ShapeDtypeStruct((8, 1024), F32),
            jax.ShapeDtypeStruct((1, 4096), F32),
        ],
        scratch_shapes=[
            pltpu.VMEM((5, 1024, 1024), BF16),
            pltpu.VMEM((4096, 1024), BF16),
            pltpu.VMEM((4, 256, 1024), F32),
            pltpu.VMEM((4, 256, 1024), BF16),
            pltpu.VMEM((4, 256, 1024), BF16),
            pltpu.VMEM((4, 256, 1024), BF16),
            pltpu.VMEM((256, 1024), F32),
            pltpu.VMEM((256, 1024), F32),
            pltpu.VMEM((256, 1), F32),
            pltpu.VMEM((256, 1024), F32),
            pltpu.VMEM((256, 1024), F32),
            pltpu.VMEM((256, 1024), F32),
            pltpu.VMEM((1024, 256), BF16),
            pltpu.VMEM((2, 256, 1024), BF16),
            pltpu.VMEM((2, 2, 256, 1024), BF16),
            pltpu.SemaphoreType.DMA((16,)),
        ],
        compiler_params=pltpu.CompilerParams(vmem_limit_bytes=60 * MIB),
        cost_estimate=pl.CostEstimate(flops=10 * 10**9, bytes_accessed=30 * MIB, transcendentals=2 * MIB),
        name="token_layer",
    )(at, *pieces_a, *pieces_b, context, tokens, cotangent, vectors, ffb)


def lamb_kernel(squares_ref, *refs):
    factor = CLIP_NORM / jnp.maximum(jnp.sqrt(jnp.sum(squares_ref[...], axis=0)[:, :1]), CLIP_NORM)
    for i in range(7):
        weight, grad = refs[i][...], refs[7 + i][...] * factor
        new_first = BETA_ONE * refs[14 + i][...] + (1.0 - BETA_ONE) * grad
        new_second = BETA_TWO * refs[21 + i][...] + (1.0 - BETA_TWO) * grad * grad
        direction = (
            new_first
            / (1.0 - BETA_ONE**STEP_COUNT)
            / (jnp.sqrt(new_second / (1.0 - BETA_TWO**STEP_COUNT)) + ADAM_EPS)
            + WEIGHT_DECAY * weight
        )
        weight_norm = jnp.sqrt(jnp.sum(weight * weight, keepdims=True))
        dir_norm = jnp.sqrt(jnp.sum(direction * direction, keepdims=True))
        refs[28 + i][...] = direction * (weight_norm / jnp.maximum(dir_norm, 1.0))


def lamb_steps(squares, weights, grads, firsts, seconds):
    return pl.pallas_call(
        lamb_kernel,
        in_specs=[VMEM] * 29,
        out_specs=[VMEM] * 7,
        out_shape=[jax.ShapeDtypeStruct(weight.shape, F32) for weight in weights],
        name="lamb",
    )(squares, *weights, *grads, *firsts, *seconds)


def body(tokens, cotangent, doc_lengths, *params):

    def turned(arrays):
        return (*arrays[:4], arrays[4].T, arrays[5], arrays[6].reshape(1, 32))

    shards, firsts, seconds = turned(params[:7]), turned(params[7:14]), turned(params[14:])
    dp_index = lax.axis_index("dp")
    z_at, y_at, core, x_at = dp_index // 8, dp_index // 2 % 4, dp_index % 2, lax.axis_index("group")
    at = jnp.stack([z_at, y_at, core, x_at]).astype(jnp.int32)

    with jax.named_scope("gather_x"):
        pack = packed_rows(shards)
        pack = rolled([pack[None]] + [push(pack, "x", -j)[None] for j in (1, 2, 3)], x_at, 0)
        own = lax.dynamic_slice_in_dim(pack[:, 72:96], x_at * 256, 256, axis=2)
        own = own.reshape(4, 3, 8, 256).transpose(0, 2, 1, 3).reshape(4, 8, 768)
        own = jnp.concatenate([own, pack[:, 96:, :256]], axis=2)
        part_a = pack[:, :40].reshape(4, 5, 8, 1024).transpose(1, 0, 2, 3).reshape(1, 5, 32, 1024)
        part_b = jnp.concatenate([pack[:, 40:72].reshape(1, 4, 32, 1024), own.reshape(1, 1, 32, 1024)], axis=1)

    with jax.named_scope("gather_tokens"):
        toks = [tokens, push(tokens, "x", -1), tokens, push(tokens, "x", -3)]

    with jax.named_scope("visible"):
        order = (x_at + jnp.arange(4, dtype=jnp.int32)) % 4
        positions = (order[:, None] * 256 + jnp.arange(256, dtype=jnp.int32)[None]).reshape(1024)
        ends = [doc_lengths[0, 0], doc_lengths[0, 0] + doc_lengths[0, 1]]
        ends.append(ends[1] + doc_lengths[0, 2])
        ids = sum((positions >= end).astype(jnp.int32) for end in ends)
        code = (positions + 4096 * ids).astype(F32)
        code_col, code_row = code[:, None], code[None]

    with jax.named_scope("gather_yz"):
        part_a, part_b = doubled(part_a, "z", 0), doubled(part_b, "y", 0)
        part_a, part_b = doubled(part_a, "z", 1), doubled(part_b, "y", 1)
        part_a, part_b, *toks = lax.optimization_barrier((part_a, part_b, *toks))
        toks[2] = push(toks[2], "x", -2)
        part_b, w_own = part_b[:, :4].reshape(4, 128, 1024), part_b[:, 4]
        w_own = doubled(w_own, "z", 0)
        part_a, part_b, at, code_col, code_row = lax.optimization_barrier((part_a, part_b, at, code_col, code_row))
        w_own = doubled(w_own, "z", 1)
        part_a, part_b = doubled(part_a, "y", 0), doubled(part_b, "z", 0)
        w_own, toks[2] = lax.optimization_barrier((w_own, toks[2]))
        w_other = push(w_own, "core", 1)
        far_a, far_b = swap(part_a, "y", 1), swap(part_b, "z", 1)

    with jax.named_scope("attention"):
        qkv, vectors, out_all, lse, w_in = attend(at, w_own, w_other, toks, code_col, code_row)
        other_b = push(part_b, "core", 1)
        part_a, other_b, out_all = lax.optimization_barrier((part_a, other_b, out_all))
        other_a = push(part_a, "core", 1)
        context = lax.all_to_all(out_all, "group", 0, 0, tiled=True)
        ffb = vectors[8:12].reshape(4, 128, 8).transpose(1, 0, 2).reshape(1, 4096)

    with jax.named_scope("gather_ff"):
        far_a, far_b, context = lax.optimization_barrier((far_a, far_b, context))
        pieces_a = (part_a, far_a, other_a, push(far_a, "core", 1))
        pieces_b = (part_b, far_b, other_b, push(far_b, "core", 1))

    with jax.named_scope("tokens"):
        block_out, dx, lx, zg, zo, d_one, d_context, small, d_ffb = token_layer(
            at, pieces_a, pieces_b, context, tokens, cotangent, vectors, ffb
        )

    with jax.named_scope("scatter_ff"):
        dx_other, zg_other = push(dx, "core", 1), push(zg, "core", 1)
        keep_a, sent_a = wide_grads(at, lx, dx, dx_other)
        sent_a, zg_other, small, d_ffb = lax.optimization_barrier((sent_a, zg_other, small, d_ffb))
        got_a = swap(sent_a, "z", 0)
        keep_b, sent_b = down_grads(at, zo, zg, zg_other)
        ffb_rows = d_ffb.reshape(128, 4, 8).transpose(1, 0, 2).reshape(4, 1024)
        small = jnp.concatenate([small, ffb_rows, jnp.zeros((4, 1024), F32)], axis=0)

    with jax.named_scope("attention_back"):
        d_all = lax.all_to_all(d_context, "group", 0, 0, tiled=True)
        d_all, sent_b = lax.optimization_barrier((d_all, sent_b))

    with jax.named_scope("scatter_ff"):
        terms_b, terms_a = [keep_b, swap(sent_b, "y", 0)], [keep_a, got_a]
        sent_b, sent_a = outgoing(terms_b), outgoing(terms_a)

    with jax.named_scope("attention_back"):
        keep_in, give_in, d_qkv = attend_back(at, toks, qkv, d_all, code_col, code_row, lse, small)

    with jax.named_scope("scatter_attn_in"):
        terms_in = [keep_in, push(give_in, "core", 1)]
        terms_in = step_down(terms_in, outgoing(terms_in), "y", 0)
        backs, terms_in[-1] = lax.optimization_barrier((input_back(at, d_qkv, w_in), terms_in[-1]))

    with jax.named_scope("input_grad"):
        backs = lax.all_to_all(backs, "group", 0, 0, tiled=True)

    with jax.named_scope("scatter_ff"):
        for axis_b, axis_a, axis_in, step in (("y", "z", "y", 1), ("z", "y", "z", 0), ("z", "y", "z", 1)):
            if axis_b == "z":
                terms_b, terms_a, terms_in = lax.optimization_barrier((terms_b, terms_a, terms_in))
                sent_b, sent_a = outgoing(terms_b), outgoing(terms_a)
            terms_b, terms_a = step_down(terms_b, sent_b, axis_b, step), step_down(terms_a, sent_a, axis_a, step)
            terms_in = step_down(terms_in, outgoing(terms_in), axis_in, step)
        sum_b, sum_a, sum_in = (sum(term.astype(F32) for term in terms) for terms in (terms_b, terms_a, terms_in))
        sum_in = sum_in.reshape(4, 8, 896)
        pack = jnp.concatenate(
            [
                sum_a.reshape(5, 4, 8, 1024).transpose(1, 0, 2, 3).reshape(4, 40, 1024),
                sum_b.reshape(4, 32, 1024),
                jnp.concatenate([sum_in, jnp.zeros((4, 8, 128), F32)], axis=2),
            ],
            axis=1,
        )
        parts = [pick(pack, x_at, 0)]
        parts += [push(pick(pack, (x_at + 4 - j) % 4, 0).astype(BF16), "x", -j) for j in (1, 2, 3)]
        *grads, squares = finished(at, parts)

    with jax.named_scope("input_grad"):
        input_grad = d_one + jnp.sum(backs.astype(F32), axis=0)

    with jax.named_scope("norm"):
        squares = lax.all_to_all(squares, AXES, 0, 0, tiled=True)
    with jax.named_scope("lamb"):
        steps = lamb_steps(squares, shards, grads, firsts, seconds)

    def restored(arrays):
        return (*arrays[:4], arrays[4].T, arrays[5], arrays[6].reshape(32))

    return (block_out, input_grad, *restored(grads), *restored(steps))


def solution(mesh):
    rows, vector, docs = P(AXES, None), P(AXES), P("dp", None)
    leaves = (rows,) * 6 + (vector,)
    return jax.shard_map(
        body,
        mesh=mesh,
        in_specs=(rows, rows, docs) + leaves * 3,
        out_specs=(rows, rows) + leaves * 2,
        check_vma=False,
    )
```
